32 devices in a mesh: dp: 2 (over core), seq: 16 (over z, y, x).
Axes of the slice: x: 2, y: 2, z: 4, core: 2. Of those that a mesh axis runs over, the one named last changes fastest.
Arguments:
- tokens: bfloat16 [2, 2, 8192, 768], P(None, 'dp', 'seq'), may hold values from -6 to 6
- in_weight: bfloat16 [768, 3352], P('dp'), may hold values from -0.21875 to 0.21875
- out_weight: bfloat16 [1536, 768], P('dp'), may hold values from -0.15625 to 0.15625
- conv_weight: float32 [4, 1792], replicated, may hold values from -3 to 3
- conv_bias: float32 [1792], replicated, may hold values from -0.5 to 0.5
- norm_gain: float32 [768], replicated, may hold values from 0.5 to 1.5
- out_gain: float32 [1536], replicated, may hold values from 0.5 to 1.5
- skip_gain: float32 [24], replicated, may hold values from 0.5 to 1.5
- rate_code: int32 [24], replicated, may hold values from 0 to 31
- step_code: int32 [24], replicated, may hold values from 0 to 31
- cotangent: bfloat16 [2, 2, 8192, 768], P(None, 'dp', 'seq'), may hold values from -6 to 6
Outputs:
- mixed: bfloat16 [2, 2, 8192, 768], P(None, 'dp', 'seq')
- grad_tokens: bfloat16 [2, 2, 8192, 768], P(None, 'dp', 'seq')
- grad_in_weight: float32 [768, 3352], P('dp')
- grad_out_weight: float32 [1536, 768], P('dp')
- grad_conv_weight: float32 [4, 1792], replicated
- grad_conv_bias: float32 [1792], replicated
- grad_norm_gain: float32 [768], replicated
- grad_out_gain: float32 [1536], replicated
- grad_skip_gain: float32 [24], replicated
- grad_log_rate: float32 [24], replicated
- grad_step_bias: float32 [24], replicated
The draws below stay inside these ranges and needn't reach their ends.
All inputs are finite; a program needn't handle non-finite values.
Results may differ from the reference program's by a relative error of at most 0.0072.
Values may be sent and summed in bfloat16 or wider, within the bound.
A program may use at most 320 MiB of HBM per device.

```python
import jax
import jax.numpy as jnp
from jax import lax

D = 768
DIN = 1536
HEADS = 24
HEAD_DIM = 64
STATE = 128
CONV = 4
BLOCK = 256
MICRO = 2
XBC = 1792
PROJ = 3352
LENGTH = 8192
SEQS = 2


def plant(entries, rng, low, top_value):
    index_at = [jax.random.randint(jax.random.fold_in(rng, axis), (), 0, length) for axis, length in enumerate(entries.shape)]
    longest = entries.shape.index(max(entries.shape))
    beside = index_at[:longest] + [(index_at[longest] + 1) % entries.shape[longest]] + index_at[longest + 1:]
    return entries.at[tuple(index_at)].set(low).at[tuple(beside)].set(top_value)


def block_levels(stream_key, shape, cuts, smallest, top_value):
    loudness, own = 1.0, jax.random.fold_in(stream_key, 6)
    for axis_at, shards_of in cuts:
        steps = jnp.exp(jax.random.uniform(jax.random.fold_in(own, axis_at), (shards_of,), jnp.float32, smallest / len(cuts), top_value / len(cuts)))
        loudness = loudness * jnp.repeat(steps, shape[axis_at] // shards_of).reshape([-1 if axis == axis_at else 1 for axis in range(len(shape))])
    return loudness


def centred(stream_key, extent, deviation, bound, cuts=(), kind=jnp.bfloat16):
    values = jax.random.normal(stream_key, extent, jnp.float32) * deviation
    if len(cuts) > 0:
        values = block_levels(stream_key, extent, cuts, -0.22, 0.18) * values
    return jnp.clip(values, min=-bound, max=bound).astype(kind)


def setup_inputs(seed: int = 0) -> dict:
    key_of = jax.random.split(jax.random.key(seed), 12)
    return {
        "tokens": centred(key_of[0], (MICRO, SEQS, LENGTH, D), 1.0, 6.0, ((1, 2), (2, 16))),
        "in_weight": centred(key_of[1], (D, PROJ), D ** -0.5, 0.21875, ((0, 2),)),
        "out_weight": centred(key_of[2], (DIN, D), DIN ** -0.5, 0.15625, ((0, 2),)),
        "conv_weight": centred(key_of[3], (CONV, XBC), 0.5, 3.0, (), jnp.float32),
        "conv_bias": jnp.clip(jax.random.uniform(key_of[4], (XBC,), jnp.float32, -0.5, 0.5), -0.5, 0.5),
        "norm_gain": jnp.clip(1.0 + 0.1 * jax.random.normal(key_of[5], (D,), jnp.float32), 0.5, 1.5),
        "out_gain": jnp.clip(1.0 + 0.1 * jax.random.normal(key_of[6], (DIN,), jnp.float32), 0.5, 1.5),
        "skip_gain": jnp.clip(jax.random.uniform(key_of[7], (HEADS,), jnp.float32, 0.5, 1.5), 0.5, 1.5),
        "rate_code": plant(jax.random.randint(key_of[8], (HEADS,), 0, 32), jax.random.fold_in(key_of[8], 1), 0, 31).astype(jnp.int32),
        "step_code": plant(jax.random.randint(key_of[9], (HEADS,), 0, 32), jax.random.fold_in(key_of[9], 1), 0, 31).astype(jnp.int32),
        "cotangent": centred(key_of[10], (MICRO, SEQS, LENGTH, D), 1.0, 6.0, ((1, 2), (2, 16))),
    }


EPS = 1e-05
HIGH = lax.Precision.HIGHEST

@jax.custom_vjp
def low(v):
    return lax.optimization_barrier(v.astype(jnp.bfloat16)).astype(jnp.float32)

@jax.custom_vjp
def low_back(v):
    return v

def low_keep(v):
    return (low(v), None)

def low_pass(kept, grad):
    return (grad,)

def back_keep(v):
    return (v, None)

def back_low(kept, grad):
    return (low(grad),)
low.defvjp(low_keep, low_pass)
low_back.defvjp(back_keep, back_low)

def rms_scale(values):
    return lax.rsqrt(lax.optimization_barrier(jnp.mean(values * values, axis=-1, keepdims=True)) + EPS)

def layer(params, source):
    in_weight, out_weight, conv_weight, conv_bias, norm_gain, out_gain, skip_gain, log_rate, step_bias = params
    count = source.shape[0]
    decay_rate = -jnp.exp(log_rate)
    normed = low(source * rms_scale(source) * norm_gain)
    projected = low_back(jnp.dot(normed, in_weight, precision=HIGH))
    gate_in = projected[:, :DIN]
    conv_in = projected[:, DIN:DIN + XBC]
    step_raw = projected[:, DIN + XBC:]
    padded = jnp.concatenate([jnp.zeros((CONV - 1, XBC), jnp.float32), conv_in], axis=0)
    conv_out = conv_bias + sum((conv_weight[k] * padded[k:k + count] for k in range(CONV)))
    mixed_in = jax.nn.silu(conv_out)
    x_heads = mixed_in[:, :DIN].reshape(count, HEADS, HEAD_DIM)
    b_proj = mixed_in[:, DIN:DIN + STATE]
    c_proj = mixed_in[:, DIN + STATE:]
    step_size = jax.nn.softplus(step_raw + step_bias)
    causal = jnp.tril(jnp.ones((BLOCK, BLOCK), dtype=bool))

    def block_step(state, pieces):
        x_blk, b_blk, c_blk, step_blk = pieces
        log_decay = jnp.cumsum(step_blk * decay_rate, axis=0)
        heads_decay = log_decay.T
        gaps = heads_decay[:, :, None] - heads_decay[:, None, :]
        lower_mat = jnp.where(causal, jnp.exp(jnp.where(causal, gaps, 0.0)), 0.0)
        gram = jnp.dot(c_blk, b_blk.T, precision=HIGH)
        mixing = gram[None] * lower_mat * step_blk.T[:, None, :]
        y_inner = jnp.einsum('hts,shp->thp', mixing, x_blk, precision=HIGH)
        y_state = jnp.exp(log_decay)[:, :, None] * jnp.einsum('hpn,tn->thp', state, c_blk, precision=HIGH)
        total = log_decay[-1]
        weighted = (jnp.exp(total[None] - log_decay) * step_blk)[:, :, None] * x_blk
        new_state = jnp.exp(total)[:, None, None] * state + jnp.einsum('shp,sn->hpn', weighted, b_blk, precision=HIGH)
        return (new_state, y_inner + y_state)
    blocks = count // BLOCK
    pieces = (x_heads.reshape(blocks, BLOCK, HEADS, HEAD_DIM), b_proj.reshape(blocks, BLOCK, STATE), c_proj.reshape(blocks, BLOCK, STATE), step_size.reshape(blocks, BLOCK, HEADS))
    start = jnp.zeros((HEADS, HEAD_DIM, STATE), jnp.float32)
    unused, y_blocks = lax.scan(jax.checkpoint(block_step), start, pieces)
    y_heads = y_blocks.reshape(count, HEADS, HEAD_DIM) + skip_gain[:, None] * x_heads
    gated = y_heads.reshape(count, DIN) * jax.nn.silu(gate_in)
    branch = low(gated * rms_scale(gated) * out_gain)
    return jnp.dot(branch, out_weight, precision=HIGH)

def reference(tokens, in_weight, out_weight, conv_weight, conv_bias, norm_gain, out_gain, skip_gain, rate_code, step_code, cotangent):
    log_rate = -4.0 + 0.25 * rate_code.astype(jnp.float32)
    step_bias = -9.0 + 0.25 * step_code.astype(jnp.float32)
    params = (in_weight.astype(jnp.float32), out_weight.astype(jnp.float32), conv_weight.astype(jnp.float32), conv_bias.astype(jnp.float32), norm_gain.astype(jnp.float32), out_gain.astype(jnp.float32), skip_gain.astype(jnp.float32), log_rate, step_bias)
    sources = tokens.reshape(-1, LENGTH, D)
    upstreams = cotangent.reshape(-1, LENGTH, D)

    def one_sequence(totals, pair):
        source = pair[0].astype(jnp.float32)
        upstream = pair[1].astype(jnp.float32)
        result, pull = jax.vjp(layer, params, source)
        grad_params, grad_source = pull(upstream)
        mixed = (source + result).astype(jnp.bfloat16)
        grad_tok = (upstream + grad_source).astype(jnp.bfloat16)
        totals = jax.tree.map(lambda left, right: left + right, totals, grad_params)
        return (totals, (mixed, grad_tok))
    zeros = jax.tree.map(jnp.zeros_like, params)
    totals, outputs = lax.scan(one_sequence, zeros, (sources, upstreams))
    mixed = outputs[0].reshape(tokens.shape)
    grad_tokens = outputs[1].reshape(tokens.shape)
    return (mixed, grad_tokens, totals[0], totals[1], totals[2], totals[3], totals[4], totals[5], totals[6], totals[7], totals[8])
```

```python
import functools

import jax
import jax.numpy as jnp
from jax import lax
from jax.experimental import pallas as pl
from jax.experimental.pallas import tpu as pltpu
from jax.sharding import PartitionSpec as P

D = 768
DIN = 1536
HEADS = 24
HEAD_DIM = 64
STATE = 128
CONV = 4
XBC = 1792
PROJ = 3352
EPS = 1e-05
LOG2E = 1.4426950408889634
CHUNK = 128
TILE = 256
HALO = 16
UNIT = 16
KIND = jnp.bfloat16
F32 = jnp.float32
BF16 = jnp.bfloat16
VMEM_LIMIT = 62 * 1024 * 1024


def mm(a, b):
    return lax.dot_general(a, b, (((1,), (0,)), ((), ())), preferred_element_type=F32)


def mm_nt(a, b):
    return lax.dot_general(a, b, (((1,), (1,)), ((), ())), preferred_element_type=F32)


def mm_tn(a, b):
    return lax.dot_general(a, b, (((0,), (0,)), ((), ())), preferred_element_type=F32)


def split2(v):
    hi = v.astype(BF16)
    return hi, (v - hi.astype(F32)).astype(BF16)


def split3(v):
    hi = v.astype(BF16)
    rest = v - hi.astype(F32)
    mid = rest.astype(BF16)
    return hi, mid, (rest - mid.astype(F32)).astype(BF16)


def iota(shape, dim):
    return lax.broadcasted_iota(jnp.int32, shape, dim)


def spread_matrix(start, width):
    head = iota((2 * STATE, width), 0) & (STATE - 1)
    column = (iota((2 * STATE, width), 1) + start) >> 6
    return jnp.where(head == column, 1.0, 0.0).astype(BF16)


def gather_matrix():
    return jnp.where((iota((DIN, STATE), 0) >> 6) == iota((DIN, STATE), 1), 1.0, 0.0).astype(BF16)


def spread(v, matrix):
    return mm(jnp.concatenate(split2(v), axis=1), matrix)


def head_sums(v, matrix, parts=3):
    pieces = split3(v) if parts == 3 else split2(v)
    total = mm(pieces[0], matrix)
    for piece in pieces[1:]:
        total = total + mm(piece, matrix)
    return total


def fine_nt(a, b):
    ah, al = split2(a)
    bh, bl = split2(b)
    return mm_nt(jnp.concatenate([ah, ah, al], axis=1), jnp.concatenate([bh, bl, bh], axis=1))


def halves(v):
    return jnp.concatenate(split2(v), axis=0)


def triangle(upper):
    row, column = iota((CHUNK, CHUNK), 0), iota((CHUNK, CHUNK), 1)
    keep = column >= row if upper else column <= row
    return jnp.where(keep, 1.0, 0.0).astype(BF16)


def tri_sum(tri, v):
    return mm(jnp.concatenate([tri] * 3, axis=1), jnp.concatenate(split3(v), axis=0))


def head_params(hp_ref):
    hp = hp_ref[...]
    decay = -jnp.exp(-4.0 + 0.25 * hp[0:1])
    bias = -9.0 + 0.25 * hp[1:2]
    return decay, bias, hp


def sigmoid(v):
    return 1.0 / (1.0 + jnp.exp(-v))


def norm_rows(tok, gain):
    src = tok.astype(F32)
    scale = lax.rsqrt(jnp.mean(src * src, axis=-1, keepdims=True) + EPS)
    return src, scale, (src * scale * gain).astype(BF16)


def pair_masks():
    low = iota((CHUNK, STATE), 1) < HEAD_DIM
    return low, jnp.logical_not(low)


def doubled(v):
    low, high = pair_masks()
    wide = v.astype(F32)
    return jnp.concatenate([jnp.where(low, wide, 0.0).astype(BF16), jnp.where(high, wide, 0.0).astype(BF16)], axis=0)


def k1_body(tok_ref, halo_ref, w_ref, ws_ref, cw_ref, cb_ref, ng_ref, hp_ref,
            gate_ref, cin_ref, cout_ref, bc_ref, ypart_ref, info_ref, sl_ref, sdev_ref, tot_ref,
            an, u, ub, dt2, tw2):
    T = tok_ref.shape[1]
    NC = T // CHUNK
    decay, bias, hp = head_params(hp_ref)
    decay2 = decay * LOG2E
    gain = ng_ref[...]
    first = lax.axis_index("seq") == 0
    an[0:HALO] = jnp.where(first, 0.0, norm_rows(halo_ref[0], gain)[2].astype(F32)).astype(BF16)
    an[HALO:] = norm_rows(tok_ref[0], gain)[2]
    arg = mm_nt(an[HALO:], ws_ref[...]) + bias
    dt = jnp.maximum(arg, 0.0) + jnp.log1p(jnp.exp(-jnp.abs(arg)))
    info_ref[0, 0] = arg
    info_ref[0, 1] = dt
    dt2[...] = jnp.concatenate(split2(dt), axis=1)
    tri = triangle(False)
    total = jnp.zeros((1, STATE), F32)
    for c in range(NC):
        rows = slice(c * CHUNK, (c + 1) * CHUNK)
        lc = tri_sum(tri, dt[rows] * decay2)
        info_ref[0, 2, rows] = lc
        total = total + lc[CHUNK - 1:CHUNK]
        tw2[rows] = jnp.concatenate(split2(jnp.exp2(lc[CHUNK - 1:CHUNK] - lc)), axis=1)

    tot_ref[pl.ds(pl.program_id(0), 1)] = total

    @pl.loop(0, DIN // TILE)
    def _(j):
        cols = pl.ds(pl.multiple_of(j * TILE, TILE), TILE)
        gate_ref[0, :, cols] = mm_nt(an[HALO:], w_ref[cols, :])

    def conv_tile(j, cols):
        wcols = pl.ds(pl.multiple_of(DIN + j * TILE, TILE), TILE)
        cin_ref[0, :, cols] = mm_nt(an[...], w_ref[wcols, :])
        out = cb_ref[:, cols]
        for k in range(CONV):
            out = out + cw_ref[k:k + 1, cols] * cin_ref[0, HALO - CONV + 1 + k:HALO - CONV + 1 + k + T, cols]
        cout_ref[0, :, cols] = out
        return out * sigmoid(out)

    @pl.loop(0, DIN // TILE)
    def _(j):
        cols = pl.ds(pl.multiple_of(j * TILE, TILE), TILE)
        x = conv_tile(j, cols)
        matrix = spread_matrix(j * TILE, TILE)
        ux = x * mm(dt2[...], matrix)
        u[:, cols] = ux.astype(BF16)
        hi, lo = split2(ux * mm(tw2[...], matrix))
        for c in range(NC):
            rows = slice(c * CHUNK, (c + 1) * CHUNK)
            ub[c, 0:CHUNK, cols] = hi[rows]
            ub[c, CHUNK:, cols] = lo[rows]
        skip_tile = spread(jnp.broadcast_to(hp[2:3], (8, STATE)), matrix)[0:1]
        ypart_ref[0, :, cols] = x * skip_tile

    bc_ref[0] = conv_tile(DIN // TILE, pl.ds(DIN, TILE))

    causal = iota((CHUNK, CHUNK), 0) >= iota((CHUNK, CHUNK), 1)
    sdev_ref[0] = jnp.zeros((STATE, DIN), F32)

    @pl.loop(0, NC)
    def _(c):
        rows = pl.ds(pl.multiple_of(c * CHUNK, CHUNK), CHUNK)
        b = bc_ref[0, rows, 0:STATE]
        gram = jnp.where(causal, fine_nt(bc_ref[0, rows, STATE:2 * STATE], b), 0.0)
        b16 = b.astype(BF16)
        lc = info_ref[0, 2, rows]
        lct = lc.T
        sl_ref[0, c] = sdev_ref[0]
        total = jnp.exp2(jnp.broadcast_to(lc[CHUNK - 1:CHUNK], (8, STATE)))
        keep = spread(total, spread_matrix(0, DIN))[0:1]
        sdev_ref[0] = keep * sdev_ref[0] + mm_tn(jnp.concatenate([b16, b16], axis=0), ub[c])
        for p in range(HEADS // 2):
            cols = slice(p * STATE, (p + 1) * STATE)
            mixes = []
            for h in (2 * p, 2 * p + 1):
                gap = lc[:, h:h + 1] - lct[h:h + 1, :]
                mixes.append((gram * jnp.exp2(jnp.minimum(gap, 0.0))).astype(BF16))
            ypart_ref[0, rows, cols] = ypart_ref[0, rows, cols] + mm(jnp.concatenate(mixes, axis=1), doubled(u[rows, cols]))

    sl_ref[0, NC] = sdev_ref[0]


def whole(shape):
    rank = len(shape)
    return pl.BlockSpec(shape, lambda m: (0,) * rank)


def per_micro(shape, buffers=None):
    rank = len(shape)
    mode = None if buffers is None else pl.Buffered(buffers)
    return pl.BlockSpec((1,) + shape, lambda m: (m,) + (0,) * rank, pipeline_mode=mode)


def call(body, grid, ins, outs, scratch, name):
    return pl.pallas_call(
        body,
        grid=grid,
        in_specs=[s for s, _ in ins],
        out_specs=[s for s, _ in outs],
        out_shape=[o for _, o in outs],
        scratch_shapes=scratch,
        compiler_params=pltpu.CompilerParams(vmem_limit_bytes=VMEM_LIMIT, dimension_semantics=("arbitrary",) * len(grid)),
        name=name,
    )(*[a for _, a in ins])


def k1(tok, halo, w, ws, cw, cb, ng, hp):
    M, T, _ = tok.shape
    NC = T // CHUNK
    S = lambda shape, dt: (per_micro(shape), jax.ShapeDtypeStruct((M,) + shape, dt))
    return call(
        k1_body, (M,),
        [(per_micro((T, D)), tok), (per_micro((HALO, D)), halo), (whole(w.shape), w), (whole(ws.shape), ws),
         (whole(cw.shape), cw), (whole(cb.shape), cb), (whole(ng.shape), ng), (whole(hp.shape), hp)],
        [S((T, DIN), F32), S((HALO + T, XBC), F32), S((T, XBC), F32), S((T, 2 * STATE), F32), S((T, DIN), F32),
         S((3, T, STATE), F32), S((NC + 1, STATE, DIN), F32), S((STATE, DIN), F32),
         (whole((M, STATE)), jax.ShapeDtypeStruct((M, STATE), F32))],
        [pltpu.VMEM((HALO + T, D), BF16), pltpu.VMEM((T, DIN), BF16), pltpu.VMEM((NC, 2 * CHUNK, DIN), BF16),
         pltpu.VMEM((T, 2 * STATE), BF16), pltpu.VMEM((T, 2 * STATE), BF16)],
        "forward_local",
    )


def chunk_totals(info_ref, NC):
    return [info_ref[0, 2, (c + 1) * CHUNK - 1:(c + 1) * CHUNK] for c in range(NC)]


def product_sum(left, right, cols):
    total = mm(left[0], right[0, :, cols])
    for m in range(1, left.shape[0]):
        total = total + mm(left[m], right[m, :, cols])
    return total


def put_tile(gtile_ref, d, tile, part):
    count = part.shape[0] // UNIT
    gtile_ref[d, pl.ds(tile * count, count)] = part.reshape(count, UNIT, STATE)


def clear_tiles(gtile_ref, rows, tiles):
    low, high = tiles * (rows // UNIT), gtile_ref.shape[1]
    if high > low:
        gtile_ref[:, low:] = jnp.zeros((gtile_ref.shape[0], high - low, UNIT, STATE), BF16)


def weight_tiles(gtile_ref, rows, left, right, count):
    @pl.loop(0, count)
    def _(j):
        part = product_sum(left, right, pl.ds(pl.multiple_of(j * STATE, STATE), STATE)).astype(BF16)
        for d in range(gtile_ref.shape[0]):
            put_tile(gtile_ref, d, j, part[d * rows:(d + 1) * rows])


def k2_body(tok_ref, cot_ref, ng_ref, og_ref, wo_ref, hp_ref, gate_ref, ypart_ref, bc_ref, info_ref, sl_ref, start_ref,
            mixed_ref, dgate_ref, dy_ref, r_ref, gl_ref, gdev_ref, ogr_ref, gtile_ref,
            y, dbr, branch, branch_t, norm_t, oscale, cot_all):
    m = pl.program_id(0)
    T = tok_ref.shape[1]
    NC = T // CHUNK
    matrix = spread_matrix(0, DIN)
    gather = gather_matrix()
    src, _, normed = norm_rows(tok_ref[0], ng_ref[...])
    norm_t[m] = normed.T
    cot_all[m] = cot_ref[0]

    @pl.when(m == 0)
    def _():
        ogr_ref[...] = jnp.zeros_like(ogr_ref)

    totals = chunk_totals(info_ref, NC)
    before = jnp.zeros((1, STATE), F32)
    for c in range(NC):
        rows = slice(c * CHUNK, (c + 1) * CHUNK)
        keep = spread(jnp.exp2(jnp.broadcast_to(before, (8, STATE))), matrix)[0:1]
        before = before + totals[c]
        state = halves(sl_ref[0, c].astype(F32) + keep * start_ref[0].astype(F32))
        c16 = bc_ref[0, rows, STATE:2 * STATE].astype(BF16)
        lift = spread(jnp.exp2(info_ref[0, 2, rows]), matrix)
        yc = ypart_ref[0, rows] + lift * mm(jnp.concatenate([c16, c16], axis=1), state)
        y[rows] = yc
        g = gate_ref[0, rows]
        gated = yc * (g * sigmoid(g))
        scale = lax.rsqrt(jnp.mean(gated * gated, axis=-1, keepdims=True) + EPS)
        oscale[rows] = jnp.broadcast_to(scale, (CHUNK, STATE))
        branch[rows] = (gated * scale * og_ref[...]).astype(BF16)
    branch_t[m] = branch[...].T
    cot = cot_ref[0]
    for j in range(D // TILE):
        cols = slice(j * TILE, (j + 1) * TILE)
        mixed_ref[0, :, cols] = (tok_ref[0, :, cols].astype(F32) + mm(branch[...], wo_ref[:, cols])).astype(BF16)

    @pl.loop(0, DIN // TILE)
    def _(j):
        cols = pl.ds(pl.multiple_of(j * TILE, TILE), TILE)
        dbr[:, cols] = mm_nt(cot, wo_ref[cols, :])

    gdev_ref[0] = jnp.zeros((STATE, DIN), F32)

    @pl.loop(0, NC)
    def _(i):
        c = NC - 1 - i
        rows = pl.ds(pl.multiple_of(c * CHUNK, CHUNK), CHUNK)
        g = gate_ref[0, rows]
        yc = y[rows]
        db = dbr[rows]
        scale = oscale[rows][:, 0:1]
        sig = sigmoid(g)
        act = g * sig
        gated = yc * act
        unit = gated * scale
        ogr_ref[...] += jnp.sum(db * unit, axis=0, keepdims=True)
        e = db * og_ref[...]
        mean = jnp.mean(e * unit, axis=-1, keepdims=True)
        dgated = scale * (e - unit * mean)
        dgate_ref[m, rows] = (dgated * yc * (sig * (1.0 + g * (1.0 - sig)))).astype(BF16)
        dy = (dgated * act).astype(BF16)
        dy_ref[0, rows] = dy
        dyf = dy.astype(F32)
        r_ref[0, rows] = head_sums(dyf * yc, gather)
        lc = info_ref[0, 2, rows]
        lifted = halves(dyf * spread(jnp.exp2(lc), matrix))
        c16 = bc_ref[0, rows, STATE:2 * STATE].astype(BF16)
        gl_ref[0, c] = gdev_ref[0]
        total = jnp.exp2(jnp.broadcast_to(lc[CHUNK - 1:CHUNK], (8, STATE)))
        keep = spread(total, matrix)[0:1]
        gdev_ref[0] = keep * gdev_ref[0] + mm_tn(jnp.concatenate([c16, c16], axis=0), lifted)

    @pl.when(m == pl.num_programs(0) - 1)
    def _():
        dp = gtile_ref.shape[0]
        rows = D // dp
        weight_tiles(gtile_ref, rows, norm_t, dgate_ref, DIN // STATE)
        clear_tiles(gtile_ref, rows, 24)

        @pl.loop(0, D // STATE)
        def _(j):
            part = product_sum(branch_t, cot_all, pl.ds(pl.multiple_of(j * STATE, STATE), STATE)).astype(BF16)
            for d in range(dp):
                for half in range(2):
                    low = (2 * d + half) * rows
                    put_tile(gtile_ref, d, 12 + half * 6 + j, part[low:low + rows])


def k2(tok, cot, ng, og, wo, hp, gate, ypart, bc, info, sl, start, dp, units):
    M, T, _ = tok.shape
    NC = T // CHUNK
    S = lambda shape, dt: (per_micro(shape), jax.ShapeDtypeStruct((M,) + shape, dt))
    W = lambda shape, dt: (whole(shape), jax.ShapeDtypeStruct(shape, dt))
    one = lambda a, n=1: (per_micro(a.shape[1:], n), a)
    all_ = lambda a: (whole(a.shape), a)
    return call(
        k2_body, (M,),
        [one(tok), one(cot), all_(ng), all_(og), all_(wo), all_(hp), one(gate), one(ypart, 1), one(bc), one(info), one(sl), one(start, 1)],
        [S((T, D), BF16), W((M, T, DIN), BF16), S((T, DIN), BF16), S((T, STATE), F32), S((NC, STATE, DIN), F32),
         S((STATE, DIN), F32), W((1, DIN), F32), W((dp, units, UNIT, STATE), BF16)],
        [pltpu.VMEM((T, DIN), F32), pltpu.VMEM((T, DIN), F32), pltpu.VMEM((T, DIN), BF16), pltpu.VMEM((M, DIN, T), BF16),
         pltpu.VMEM((M, D, T), BF16), pltpu.VMEM((T, STATE), F32), pltpu.VMEM((M, T, D), BF16)],
        "gate_and_out",
    )


def k3_body(hp_ref, cw_ref, cin_ref, cout_ref, bc_ref, info_ref, sl_ref, start_ref, dy_ref, r_ref, gl_ref, later_ref,
            dcin_ref, tail_ref, head_ref, dstep_ref, gcw_ref, gcb_ref, gskip_ref, ghead_ref,
            dconv, w, xdu, ub, dyl, dgt, dt_x, tail_x, bg):
    m = pl.program_id(0)
    T = cout_ref.shape[1]
    NC = T // CHUNK
    decay, _, hp = head_params(hp_ref)
    matrix = spread_matrix(0, DIN)
    gather = gather_matrix()
    skip = spread(jnp.broadcast_to(hp[2:3], (8, STATE)), matrix)[0:1]

    @pl.when(m == 0)
    def _():
        gcw_ref[...] = jnp.zeros_like(gcw_ref)
        gcb_ref[...] = jnp.zeros_like(gcb_ref)
        gskip_ref[...] = jnp.zeros_like(gskip_ref)
        ghead_ref[...] = jnp.zeros_like(ghead_ref)

    dconv[T:] = jnp.zeros((HALO, XBC), F32)
    tri_up = triangle(True)
    keeps_st = iota((CHUNK, CHUNK), 0) <= iota((CHUNK, CHUNK), 1)
    totals = chunk_totals(info_ref, NC)
    afters, befores = [jnp.zeros((1, STATE), F32)], [jnp.zeros((1, STATE), F32)]
    for c in range(NC):
        befores.append(befores[-1] + totals[c])
        afters.append(afters[-1] + totals[NC - 1 - c])
    afters = afters[::-1]

    for c in range(NC):
        rows = slice(c * CHUNK, (c + 1) * CHUNK)
        b = bc_ref[0, rows, 0:STATE]
        cc = bc_ref[0, rows, STATE:2 * STATE]
        gram_t = jnp.where(keeps_st, fine_nt(b, cc), 0.0)
        b, cc = b.astype(BF16), cc.astype(BF16)
        lc = info_ref[0, 2, rows]
        lct = lc.T
        dt = info_ref[0, 1, rows]
        dt_x[...] = spread(dt, matrix)
        tail_x[...] = spread(jnp.exp2(lc[CHUNK - 1:CHUNK] - lc), matrix)
        lift = spread(jnp.exp2(lc), matrix)
        dyl[...] = (dy_ref[0, rows].astype(F32) * lift).astype(BF16)
        wide8 = lambda v: spread(jnp.exp2(jnp.broadcast_to(v, (8, STATE))), matrix)[0:1]
        gc = gl_ref[0, c].astype(F32) + wide8(afters[c + 1]) * later_ref[0].astype(F32)
        gcb16 = gc.astype(BF16)
        s_in = sl_ref[0, c].astype(F32) + wide8(befores[c]) * start_ref[0].astype(F32)
        s_out_start = wide8(befores[c + 1]) * start_ref[0].astype(F32)
        if c + 1 < NC:
            s_out = sl_ref[0, c + 1].astype(F32) + s_out_start
        else:
            s_out = sl_ref[0, NC].astype(F32) + s_out_start
        bnd = head_sums(jnp.broadcast_to(jnp.sum(gc * s_out, axis=0, keepdims=True), (8, DIN)), gather)[0:1]
        bg[...] = mm(jnp.concatenate([b, b], axis=1), halves(gc))
        dgt[...] = jnp.zeros((CHUNK, CHUNK), F32)
        for p in range(HEADS // 2):
            cols = slice(p * STATE, (p + 1) * STATE)
            v = cout_ref[0, rows, cols]
            sig = sigmoid(v)
            x = v * sig
            dtx, tlx = dt_x[:, cols], tail_x[:, cols]
            ux = x * dtx
            u16 = ux.astype(BF16)
            ub[:, cols] = (ux * tlx).astype(BF16)
            dy = dy_ref[0, rows, cols]
            dyf = dy.astype(F32)
            dy2 = doubled(dy)
            decays, mixes = [], []
            for h in (2 * p, 2 * p + 1):
                gap = lct[h:h + 1, :] - lc[:, h:h + 1]
                e = jnp.exp2(jnp.minimum(gap, 0.0))
                decays.append(e)
                mixes.append((gram_t * e).astype(BF16))
            du = mm(jnp.concatenate(mixes, axis=1), dy2)
            dmix = mm_nt(u16, dy2)
            dgt[...] = dgt[...] + (dmix[:, :CHUNK] * decays[0] + dmix[:, CHUNK:] * decays[1])
            du_state = tlx * bg[:, cols]
            sk = skip[:, cols]
            dyx = dyf * x
            gskip_ref[:, cols] = gskip_ref[:, cols] + jnp.sum(dyx, axis=0, keepdims=True)
            w[:, cols] = dyx * sk + u16.astype(F32) * du + ux * du_state
            du = du + du_state
            xdu[:, cols] = x * du
            dx = dtx * du + sk * dyf
            dconv[rows, cols] = dx * (sig * (1.0 + v * (1.0 - sig)))
        dg16 = jnp.where(keeps_st, dgt[...], 0.0).astype(BF16)
        db = mm(dg16, cc) + mm_nt(ub[...], gcb16)
        dc = mm_tn(dg16, b) + mm_nt(dyl[...], s_in.astype(BF16))
        v = cout_ref[0, rows, DIN:XBC]
        sig = sigmoid(v)
        dconv[rows, DIN:XBC] = jnp.concatenate([db, dc], axis=1) * (sig * (1.0 + v * (1.0 - sig)))
        dl = r_ref[0, rows] - head_sums(w[...], gather)
        da = bnd + tri_sum(tri_up, dl)
        d_dt = head_sums(xdu[...], gather, 2) + da * decay
        arg = info_ref[0, 0, rows]
        dstep = d_dt * sigmoid(arg)
        dstep_ref[0, rows] = dstep.astype(BF16)
        ghead_ref[0:1] = ghead_ref[0:1] + decay * jnp.sum(da * dt, axis=0, keepdims=True)
        ghead_ref[1:2] = ghead_ref[1:2] + jnp.sum(dstep, axis=0, keepdims=True)

    head_ref[0] = dconv[0:8]

    @pl.loop(0, XBC // TILE)
    def _(j):
        cols = pl.ds(pl.multiple_of(j * TILE, TILE), TILE)
        own = dconv[0:T, cols]
        gcb_ref[:, cols] = gcb_ref[:, cols] + jnp.sum(own, axis=0, keepdims=True)
        total = None
        for k in range(CONV):
            low = HALO - CONV + 1 + k
            gcw_ref[k:k + 1, cols] = gcw_ref[k:k + 1, cols] + jnp.sum(own * cin_ref[0, low:low + T, cols], axis=0, keepdims=True)
            term = cw_ref[k:k + 1, cols] * dconv[CONV - 1 - k:CONV - 1 - k + T, cols]
            total = term if total is None else total + term
        dcin_ref[0, :, cols] = total.astype(BF16)
        tail_ref[0, :, cols] = total[T - HALO:]


def k3(hp, cw, cin, cout, bc, info, sl, start, dy, r, gl, later):
    M, T, _ = cout.shape
    S = lambda shape, dt: (per_micro(shape), jax.ShapeDtypeStruct((M,) + shape, dt))
    W = lambda shape, dt: (whole(shape), jax.ShapeDtypeStruct(shape, dt))
    one = lambda a: (per_micro(a.shape[1:]), a)
    all_ = lambda a: (whole(a.shape), a)
    V = pltpu.VMEM
    return call(
        k3_body, (M,),
        [all_(hp), all_(cw), one(cin), one(cout), one(bc), one(info), one(sl), one(start), one(dy), one(r), one(gl), one(later)],
        [S((T, XBC), BF16), S((HALO, XBC), F32), S((8, XBC), F32), S((T, STATE), BF16), W((CONV, XBC), F32), W((1, XBC), F32),
         W((1, DIN), F32), W((2, STATE), F32)],
        [V((T + HALO, XBC), F32), V((CHUNK, DIN), F32), V((CHUNK, DIN), F32), V((CHUNK, DIN), BF16), V((CHUNK, DIN), BF16),
         V((CHUNK, CHUNK), F32), V((CHUNK, DIN), F32), V((CHUNK, DIN), F32), V((CHUNK, DIN), F32)],
        "scan_backward",
    )


def k4_body(tok_ref, cot_ref, ng_ref, w_ref, ws_ref, cw_ref, dgate_ref, dcin_ref, dstep_ref, tail_ref, next_ref,
            gtok_ref, ngr_ref, gtile_ref,
            dc, dn, norm_t):
    m = pl.program_id(0)
    T = tok_ref.shape[1]

    @pl.when(m == 0)
    def _():
        ngr_ref[...] = jnp.zeros_like(ngr_ref)

    src, scale, normed = norm_rows(tok_ref[0], ng_ref[...])
    norm_t[m] = normed.T
    dc[m, 0:T, 0:XBC] = dcin_ref[0]
    dc[m, :, XBC:] = dstep_ref[0]
    nxt = next_ref[0]
    row = iota((HALO, XBC), 0)
    tail = tail_ref[0]
    for s in range(CONV - 1):
        extra = jnp.zeros((1, XBC), F32)
        for k in range(s + 1):
            extra = extra + cw_ref[k:k + 1] * nxt[s - k:s - k + 1]
        tail = tail + jnp.where(row == HALO - CONV + 1 + s, extra, 0.0)
    dc[m, T - HALO:T, 0:XBC] = tail.astype(BF16)

    for i in range(D // TILE):
        cols = slice(i * TILE, (i + 1) * TILE)
        dn[:, cols] = (mm(dgate_ref[0], w_ref[0:DIN, cols]) + mm(dc[m, :, 0:XBC], w_ref[DIN:DIN + XBC, cols])
                       + mm(dstep_ref[0], ws_ref[:, cols]))
    d_normed = dn[...]
    unit = src * scale
    ngr_ref[...] += jnp.sum(d_normed * unit, axis=0, keepdims=True)
    f = d_normed * ng_ref[...]
    mean = jnp.mean(f * unit, axis=-1, keepdims=True)
    gtok_ref[0] = (cot_ref[0].astype(F32) + scale * (f - unit * mean)).astype(BF16)

    @pl.when(m == pl.num_programs(0) - 1)
    def _():
        rows = D // gtile_ref.shape[0]
        weight_tiles(gtile_ref, rows, norm_t, dc, 15)
        clear_tiles(gtile_ref, rows, 15)


def k4(tok, cot, ng, w, ws, cw, dgate, dcin, dstep, tail, nxt, dp, units):
    M, T, _ = tok.shape
    S = lambda shape, dt: (per_micro(shape), jax.ShapeDtypeStruct((M,) + shape, dt))
    W = lambda shape, dt: (whole(shape), jax.ShapeDtypeStruct(shape, dt))
    one = lambda a: (per_micro(a.shape[1:]), a)
    all_ = lambda a: (whole(a.shape), a)
    V = pltpu.VMEM
    return call(
        k4_body, (M,),
        [one(tok), one(cot), all_(ng), all_(w), all_(ws), all_(cw), one(dgate), one(dcin), one(dstep), one(tail), one(nxt)],
        [S((T, D), BF16), W((1, D), F32), W((dp, units, UNIT, STATE), BF16)],
        [V((M, T, XBC + STATE), BF16), V((T, D), F32), V((M, D, T), BF16)],
        "projection_backward",
    )


MESH = pl.DeviceIdType.MESH
PLANE = 4
QUARTER = DIN // PLANE
DMA = pltpu.SemaphoreType.DMA


def places():
    seq = lax.axis_index("seq")
    return lax.axis_index("dp"), seq, lax.rem(seq, PLANE), lax.div(seq, PLANE)


def greet(devices):
    barrier = pltpu.get_barrier_semaphore()
    for device in devices:
        pl.semaphore_signal(barrier, inc=1, device_id=device, device_id_type=MESH)
    pl.semaphore_wait(barrier, len(devices))


def remote(src, dst, send, recv, device):
    return pltpu.make_async_remote_copy(
        src_ref=src, dst_ref=dst, send_sem=send, recv_sem=recv, device_id=device, device_id_type=MESH)


def open_body(ndp, nseq, win_ref, ws_ref, wout_ref, tok_ref, w_ref, wsall_ref, wo_ref, halo_ref, send, recv, hsend, hrecv):
    dp, seq, _, _ = places()
    nxt, prev = lax.rem(seq + 1, nseq), lax.rem(seq + nseq - 1, nseq)
    others = [lax.rem(dp + d, ndp) for d in range(1, ndp)]
    greet([(o, seq) for o in others] + [(dp, nxt), (dp, prev)])
    T = tok_ref.shape[1]
    width, rows = win_ref.shape[1], wout_ref.shape[0]
    columns = pl.ds(pl.multiple_of(dp * width, width), width)
    own_rows = pl.ds(pl.multiple_of(dp * rows, rows), rows)
    moves = [(ws_ref, wsall_ref.at[:, columns]), (win_ref.at[0:DIN + XBC], w_ref.at[:, columns]), (wout_ref, wo_ref.at[own_rows])]
    copies = [remote(tok_ref.at[:, T - HALO:T], halo_ref, hsend, hrecv, (dp, nxt))]
    for i, o in enumerate(others):
        for k, (src, dst) in enumerate(moves):
            copies.append(remote(src, dst, send.at[i, k], recv.at[i, k], (o, seq)))
    for copy in copies:
        copy.start()
    w_ref[:, columns] = win_ref[0:DIN + XBC]
    wsall_ref[:, columns] = ws_ref[...]
    wo_ref[own_rows] = wout_ref[...]
    for copy in copies:
        copy.wait()


def open_kernel(ndp, nseq, win, ws, wout, tok):
    vmem = pl.BlockSpec(memory_space=pltpu.VMEM)
    M = tok.shape[0]
    shape = lambda *s: jax.ShapeDtypeStruct(s, BF16)
    return pl.pallas_call(
        functools.partial(open_body, ndp, nseq),
        in_specs=[vmem] * 3 + [pl.BlockSpec(memory_space=pl.ANY)],
        out_specs=[vmem] * 4,
        out_shape=[shape(DIN + XBC, D), shape(STATE, D), shape(DIN, D), shape(M, HALO, D)],
        scratch_shapes=[DMA((ndp - 1, 3)), DMA((ndp - 1, 3)), DMA, DMA],
        compiler_params=pltpu.CompilerParams(collective_id=1, has_side_effects=True, vmem_limit_bytes=VMEM_LIMIT),
        name="gather_weights",
    )(win, ws, wout, tok)


def states_body(nseq, upward, s_ref, tot_ref, out_ref, stage, got, tots, pre, back, hop, sems, rsems, tsem, trsem, zs, zr, bs, br):
    dp, seq, p, z = places()
    M = s_ref.shape[0]
    Z = nseq // PLANE
    base = z * PLANE
    peers = [lax.rem(p + d, PLANE) for d in range(PLANE)]
    zup, zdown = lax.rem(seq + PLANE, nseq), lax.rem(seq + nseq - PLANE, nseq)
    greet([(dp, base + peers[d]) for d in range(1, PLANE)] + [(dp, zup), (dp, zdown)])
    columns = lambda q: pl.ds(pl.multiple_of(q * QUARTER, QUARTER), QUARTER)
    tots[0] = tot_ref[...]
    tcopies = [remote(tot_ref, tots.at[d], tsem.at[d - 1], trsem.at[d - 1], (dp, base + peers[d])) for d in range(1, PLANE)]
    for copy in tcopies:
        copy.start()
    first = []
    for m in range(M):
        stage[m] = s_ref[m].astype(stage.dtype)
        row = []
        for d in range(1, PLANE):
            copy = remote(stage.at[m, :, columns(peers[d])], got.at[m, d], sems.at[m, d - 1], rsems.at[m, d - 1], (dp, base + peers[d]))
            copy.start()
            row.append(copy)
        first.append(row)
    for copy in tcopies:
        copy.wait()
    shift = peers[0] * QUARTER
    order = list(range(PLANE))[::-1] if upward else list(range(PLANE))
    towards = zdown if upward else zup
    head = (z == Z - 1) if upward else (z == 0)
    tail = (z == 0) if upward else (z == Z - 1)
    last = []
    for m in range(M):
        for copy in first[m]:
            copy.wait_recv()
        matrix = spread_matrix(shift, QUARTER)
        slots = [lax.rem(p - q + PLANE, PLANE) for q in order]
        keep = [spread(jnp.exp2(jnp.broadcast_to(tots[s, m:m + 1], (8, STATE))), matrix)[0:1] for s in slots]

        got[m, 0] = s_ref[m, :, columns(p)].astype(got.dtype)
        link = remote(hop.at[m], pre.at[m], zs.at[m], zr.at[m], (dp, towards))

        @pl.when(head)
        def _():
            pre[m] = jnp.zeros_like(pre[m])

        @pl.when(jnp.logical_not(head))
        def _():
            link.wait_recv()

        run = pre[m].astype(F32)
        for i, q in enumerate(order):
            back[m, slots[i]] = run.astype(back.dtype)
            run = keep[i] * run + got[m, slots[i]].astype(F32)
        hop[m] = run.astype(hop.dtype)

        @pl.when(jnp.logical_not(tail))
        def _():
            link.start()

        for d in range(1, PLANE):
            to = lax.rem(p + PLANE - d, PLANE)
            copy = remote(back.at[m, d], out_ref.at[m, :, columns(p)], bs.at[m, d - 1], br.at[m, d - 1], (dp, base + to))
            copy.start()
            last.append(copy)
        out_ref[m, :, columns(p)] = back[m, 0]
    for row in first:
        for copy in row:
            copy.wait_send()
    for copy in last:
        copy.wait()
    for m in range(M):
        link = remote(hop.at[m], pre.at[m], zs.at[m], zr.at[m], (dp, towards))

        @pl.when(jnp.logical_not(tail))
        def _():
            link.wait_send()


def exchange(nseq, upward, s, tot, kind):
    M = s.shape[0]
    V = pltpu.VMEM
    vmem = pl.BlockSpec(memory_space=pltpu.VMEM)
    quarter = (STATE, QUARTER)
    return pl.pallas_call(
        functools.partial(states_body, nseq, upward),
        in_specs=[vmem] * 2,
        out_specs=vmem,
        out_shape=jax.ShapeDtypeStruct(s.shape, kind),
        scratch_shapes=[V(s.shape, kind), V((M, PLANE) + quarter, kind), V((PLANE,) + tot.shape, F32), V((M,) + quarter, kind),
                        V((M, PLANE) + quarter, kind), V((M,) + quarter, kind),
                        DMA((M, 3)), DMA((M, 3)), DMA((3,)), DMA((3,)), DMA((M,)), DMA((M,)), DMA((M, 3)), DMA((M, 3))],
        compiler_params=pltpu.CompilerParams(collective_id=3 if upward else 2, has_side_effects=True, vmem_limit_bytes=VMEM_LIMIT),
        name="states_later" if upward else "states_earlier",
    )(s, tot)


SMALL = (("cw", CONV, XBC), ("cb", 1, XBC), ("ng", 1, D), ("og", 1, DIN), ("skip", 1, DIN), ("head", 2, STATE))
SMALL_ROWS = 104


def small_pieces():
    row, found = 0, []
    for index, (_, rows, width) in enumerate(SMALL):
        for r in range(rows):
            for j in range(width // STATE):
                found.append((index, r, j, row))
                row += 1
    return found


def strided(count, step, body):
    @pl.loop(0, count // step)
    def _(i):
        body(pl.multiple_of(i * step, step))


def chunk_of(count):
    return max(c for c in range(1, 13) if count % c == 0)


def reduce_body(ndp, nseq, counts, *refs):
    nb = len(counts)
    ins, smalls, out_refs, small_out = refs[:nb], refs[nb:nb + 6], refs[nb + 6:2 * nb + 6], refs[2 * nb + 6]
    (r0, w1, st1, r1, w2, st2, r2, st3, r3, sm, smr, smy, smx, smz,
     s0s, s0r, s1s, s1r, s2s, s2r, s3s, s3r, t3s, t3r, t2s, t2r, t1s, t1r, ms, mr) = refs[2 * nb + 7:]
    dp, seq, p, z = places()
    Z = nseq // PLANE
    x, y = lax.rem(p, 2), lax.div(p, 2)
    others = [lax.rem(dp + d, ndp) for d in range(1, ndp)]
    px, py = seq + 1 - 2 * x, seq + 2 - 4 * y
    pz = [(lax.rem(z + d, Z) * PLANE + p) for d in range(1, Z)]
    greet([(o, seq) for o in others] + [(dp, px), (dp, py)] + [(dp, q) for q in pz])
    groups = []
    for b, count in enumerate(counts):
        half = count // 2
        groups += [(b, 0, half, (x, px), (y, py)), (b, half, half, (y, py), (x, px))]
    G = len(groups)
    n = [g[2] for g in groups]
    base = [sum(n[:g]) for g in range(G)]

    def begin0(g):
        b, start, size, _, _ = groups[g]
        copies = []
        for i, o in enumerate(others):
            copies.append(remote(ins[b].at[o, pl.ds(start, size)], r0.at[i, pl.ds(base[g], size)], s0s.at[g, i], s0r.at[g, i], (o, seq)))
        for copy in copies:
            copy.start()
        return copies

    def after0(g):
        b, start, size, (bit, peer), _ = groups[g]
        h = size // 2
        o1 = base[g] // 2
        c = chunk_of(h)

        def total(i):
            v = ins[b][dp, pl.ds(start + i, c)].astype(F32)
            for k in range(ndp - 1):
                v = v + r0[k, pl.ds(base[g] + i, c)].astype(F32)
            return v

        def body(i):
            w1[pl.ds(o1 + i, c)] = total(bit * h + i)
            st1[pl.ds(o1 + i, c)] = total((1 - bit) * h + i).astype(BF16)
        strided(h, c, body)
        copy = remote(st1.at[pl.ds(o1, h)], r1.at[pl.ds(o1, h)], s1s.at[g], s1r.at[g], (dp, peer))
        copy.start()
        return [copy]

    def after1(g):
        _, _, size, _, (bit, peer) = groups[g]
        q = size // 4
        o1, o2 = base[g] // 2, base[g] // 4
        c = chunk_of(q)

        def body(i):
            keep, give = o1 + bit * q + i, o1 + (1 - bit) * q + i
            w2[pl.ds(o2 + i, c)] = w1[pl.ds(keep, c)] + r1[pl.ds(keep, c)].astype(F32)
            st2[pl.ds(o2 + i, c)] = (w1[pl.ds(give, c)] + r1[pl.ds(give, c)].astype(F32)).astype(BF16)
        strided(q, c, body)
        copy = remote(st2.at[pl.ds(o2, q)], r2.at[pl.ds(o2, q)], s2s.at[g], s2r.at[g], (dp, peer))
        copy.start()
        return [copy]

    def after2(g):
        size = groups[g][2]
        q = size // 4
        e = q // Z
        o2 = base[g] // 4
        c = chunk_of(q)

        def body(i):
            v = w2[pl.ds(o2 + i, c)] + r2[pl.ds(o2 + i, c)].astype(F32)
            w2[pl.ds(o2 + i, c)] = v
            st3[pl.ds(o2 + i, c)] = v.astype(BF16)
        strided(q, c, body)
        copies = []
        for d in range(1, Z):
            to = lax.rem(z + d, Z)
            copies.append(remote(st3.at[pl.ds(o2 + to * e, e)], r3.at[d - 1, pl.ds(o2 // Z, e)], s3s.at[g, d - 1], s3r.at[g, d - 1], (dp, pz[d - 1])))
        for copy in copies:
            copy.start()
        return copies

    def where_out(g):
        b, start, size, (b1, _), (b2, _) = groups[g]
        h, q = size // 2, size // 4
        e = q // Z
        out = out_refs[b]
        return out, start + b1 * h, start + b1 * h + b2 * q, start + b1 * h + b2 * q + z * e, h, q, e

    def after3(g):
        out, _, _, at, _, q, e = where_out(g)
        o2 = base[g] // 4
        v = w2[pl.ds(o2 + z * e, e)]
        for d in range(Z - 1):
            v = v + r3[d, pl.ds(o2 // Z, e)].astype(F32)
        out[pl.ds(at, e)] = v.astype(BF16)
        copies = [remote(out.at[pl.ds(at, e)], out.at[pl.ds(at, e)], t3s.at[g, d - 1], t3r.at[g, d - 1], (dp, pz[d - 1])) for d in range(1, Z)]
        for copy in copies:
            copy.start()
        return copies

    def after4(g):
        out, _, at, _, _, q, _ = where_out(g)
        copy = remote(out.at[pl.ds(at, q)], out.at[pl.ds(at, q)], t2s.at[g], t2r.at[g], (dp, groups[g][4][1]))
        copy.start()
        return [copy]

    def after5(g):
        out, at, _, _, h, _, _ = where_out(g)
        copy = remote(out.at[pl.ds(at, h)], out.at[pl.ds(at, h)], t1s.at[g], t1r.at[g], (dp, groups[g][3][1]))
        copy.start()
        return [copy]

    def small0():
        sm[...] = jnp.zeros_like(sm)
        for index, r, j, row in small_pieces():
            sm[row:row + 1] = smalls[index][r:r + 1, j * STATE:(j + 1) * STATE]
        copies = [remote(sm, smr.at[i], ms.at[i], mr.at[i], (o, seq)) for i, o in enumerate(others)]
        for copy in copies:
            copy.start()
        return copies

    def small_step(src, extra, dst, slots, peers):
        v = src[...]
        for ref in extra:
            v = v + ref
        dst[0] = v
        copies = [remote(dst.at[0], dst.at[1 + k], ms.at[slots + k], mr.at[slots + k], (dp, q)) for k, q in enumerate(peers)]
        for copy in copies:
            copy.start()
        return copies

    stages = [after0, after1, after2, after3, after4, after5]
    flying = [begin0(g) for g in range(G)]
    tiny = small0()
    done = []
    for stage_at, stage in enumerate(stages):
        for g in range(G):
            for copy in flying[g]:
                copy.wait_recv()
            done += flying[g]
            flying[g] = stage(g)
        if stage_at < 4:
            for copy in tiny:
                copy.wait_recv()
            done += tiny
            if stage_at == 0:
                tiny = small_step(sm, [smr[i] for i in range(ndp - 1)], smx, ndp - 1, [px])
            elif stage_at == 1:
                tiny = small_step(smx.at[0], [smx[1]], smy, ndp, [py])
            elif stage_at == 2:
                tiny = small_step(smy.at[0], [smy[1]], smz, ndp + 1, pz)
            else:
                v = None
                for k in range(Z):
                    slot = lax.rem(z - k + Z, Z)
                    v = smz[slot] if v is None else v + smz[slot]
                small_out[...] = v
    for g in range(G):
        for copy in flying[g]:
            copy.wait_recv()
        done += flying[g]
    for copy in done:
        copy.wait_send()


def all_reduce(ndp, nseq, parts, smalls):
    Z = nseq // PLANE
    counts = tuple(a.shape[1] for a in parts)
    total = sum(counts)
    G = 2 * len(counts)
    V = pltpu.VMEM
    vmem = pl.BlockSpec(memory_space=pltpu.VMEM)
    u = lambda *lead: tuple(lead) + (UNIT, STATE)
    nsm = ndp - 1 + 2 + Z - 1
    small = (SMALL_ROWS, STATE)
    return pl.pallas_call(
        functools.partial(reduce_body, ndp, nseq, counts),
        in_specs=[vmem] * (len(parts) + len(smalls)),
        out_specs=[vmem] * (len(parts) + 1),
        out_shape=[jax.ShapeDtypeStruct(a.shape[1:], BF16) for a in parts] + [jax.ShapeDtypeStruct(small, F32)],
        scratch_shapes=[
            V(u(ndp - 1, total), BF16), V(u(total // 2), F32), V(u(total // 2), BF16), V(u(total // 2), BF16),
            V(u(total // 4), F32), V(u(total // 4), BF16), V(u(total // 4), BF16), V(u(total // 4), BF16),
            V(u(Z - 1, total // 4 // Z), BF16),
            V(small, F32), V((ndp - 1,) + small, F32), V((2,) + small, F32), V((2,) + small, F32), V((Z,) + small, F32),
            DMA((G, ndp - 1)), DMA((G, ndp - 1)), DMA((G,)), DMA((G,)), DMA((G,)), DMA((G,)), DMA((G, Z - 1)), DMA((G, Z - 1)),
            DMA((G, Z - 1)), DMA((G, Z - 1)), DMA((G,)), DMA((G,)), DMA((G,)), DMA((G,)), DMA((nsm,)), DMA((nsm,))],
        compiler_params=pltpu.CompilerParams(collective_id=4, has_side_effects=True, vmem_limit_bytes=VMEM_LIMIT),
        name="reduce_gradients",
    )(*parts, *smalls)


def unpack_body(g1_ref, g2_ref, sm_ref, gin_ref, gout_ref, cw_ref, cb_ref, ng_ref, og_ref, head_ref):
    R = gin_ref.shape[1]
    U = R // UNIT
    tile = lambda ref, j: ref[j * U:(j + 1) * U].astype(F32).reshape(R, STATE)
    eye = jnp.where(iota((STATE, STATE), 0) == iota((STATE, STATE), 1), 1.0, 0.0).astype(BF16)
    turned = lambda ref, j: mm_nt(eye, ref[j * U:(j + 1) * U].reshape(R, STATE))
    for j in range(12):
        gin_ref[j * STATE:(j + 1) * STATE] = turned(g1_ref, j)
    for j in range(14):
        gin_ref[DIN + j * STATE:DIN + (j + 1) * STATE] = turned(g2_ref, j)
    gin_ref[DIN + XBC:] = turned(g2_ref, 14)[:HEADS]
    for half in range(2):
        for j in range(D // STATE):
            gout_ref[half * R:(half + 1) * R, j * STATE:(j + 1) * STATE] = tile(g1_ref, 12 + half * 6 + j)
    outs = {0: cw_ref, 1: cb_ref, 2: ng_ref, 3: og_ref}
    low, high = iota((1, STATE), 1) < HEAD_DIM, iota((1, STATE), 1)
    lane = iota((1, STATE), 1)
    skip = jnp.zeros((1, STATE), F32)
    for index, r, j, row in small_pieces():
        v = sm_ref[row:row + 1]
        if index in outs:
            outs[index][r:r + 1, j * STATE:(j + 1) * STATE] = v
        elif index == 4:
            left = jnp.sum(jnp.where(low, v, 0.0), axis=1, keepdims=True)
            right = jnp.sum(jnp.where(low, 0.0, v), axis=1, keepdims=True)
            skip = skip + jnp.where(lane == 2 * j, left, 0.0) + jnp.where(lane == 2 * j + 1, right, 0.0)
        else:
            head_ref[r + 1:r + 2] = v
    head_ref[0:1] = skip


def unpack(g1, g2, sm, R):
    vmem = pl.BlockSpec(memory_space=pltpu.VMEM)
    sds = lambda *s: jax.ShapeDtypeStruct(s, F32)
    return pl.pallas_call(
        unpack_body,
        in_specs=[vmem] * 3,
        out_specs=[vmem] * 7,
        out_shape=[sds(PROJ, R), sds(2 * R, D), sds(CONV, XBC), sds(1, XBC), sds(1, D), sds(1, DIN), sds(3, STATE)],
        compiler_params=pltpu.CompilerParams(vmem_limit_bytes=VMEM_LIMIT),
        name="unpack_gradients",
    )(g1, g2, sm)


def per_device(ndp, nseq, tokens, in_weight, out_weight, conv_weight, conv_bias, norm_gain, out_gain, skip_gain, rate_code, step_code, cotangent):
    micro, groups, T, _ = tokens.shape
    M = micro * groups
    tok = tokens.reshape(M, T, D)
    cot = cotangent.reshape(M, T, D)
    seq = lax.axis_index("seq")
    turned = in_weight.T
    steps = jnp.pad(turned[DIN + XBC:], ((0, STATE - HEADS), (0, 0)))
    if in_weight.shape[0] % STATE == 0:
        w, ws, wo, halo = open_kernel(ndp, nseq, turned, steps, out_weight, tok)
    else:
        w, ws, wo = [lax.all_gather(v, "dp", axis=at, tiled=True) for v, at in ((turned[:DIN + XBC], 1), (steps, 1), (out_weight, 0))]
        halo = lax.ppermute(tok[:, T - HALO:], "seq", [(i, i + 1) for i in range(nseq - 1)])
    pad = lambda v: jnp.pad(v.astype(F32), (0, STATE - HEADS))
    hp = jnp.stack([pad(rate_code), pad(step_code), pad(skip_gain)])
    ng, og, cb = norm_gain[None], out_gain[None], conv_bias[None]
    gate, cin, cout, bc, ypart, info, sl, sdev, totals = k1(tok, halo, w, ws, conv_weight, cb, ng, hp)
    start = exchange(nseq, False, sdev, totals, KIND)
    mixed, dgate, dy, r, gl, gdev, ogr, gt1 = k2(tok, cot, ng, og, wo, hp, gate, ypart, bc, info, sl, start, ndp, units(ndp, nseq, 24))
    later = exchange(nseq, True, gdev, totals, KIND)
    dcin, tail, head, dstep, gcw, gcb, gskip, ghead = k3(hp, conv_weight, cin, cout, bc, info, sl, start, dy, r, gl, later)
    nxt = lax.ppermute(head, "seq", [(i, i - 1) for i in range(1, nseq)])
    gtok, ngr, gt2 = k4(tok, cot, ng, w, ws, conv_weight, dgate, dcin, dstep, tail, nxt, ndp, units(ndp, nseq, 16))
    g1, g2, sm = all_reduce(ndp, nseq, (gt1, gt2), (gcw, gcb, ngr, ogr, gskip, ghead))
    g_in, g_out, cwg, cbg, ngg, ogg, heads = unpack(g1, g2, sm, D // ndp)
    return (mixed.reshape(tokens.shape), gtok.reshape(tokens.shape), g_in.T, g_out, cwg, cbg[0], ngg[0], ogg[0],
            heads[0, :HEADS], heads[1, :HEADS], heads[2, :HEADS])


def units(ndp, nseq, tiles):
    need, step = tiles * (D // ndp // UNIT), 2 * nseq
    return -(-need // step) * step


def solution(mesh):
    rows, split = P("dp", None), P(None, "dp", "seq", None)
    return jax.shard_map(
        functools.partial(per_device, mesh.shape["dp"], mesh.shape["seq"]),
        mesh=mesh,
        in_specs=(split, rows, rows) + (P(),) * 7 + (split,),
        out_specs=(split, split, rows, rows) + (P(),) * 7,
        check_vma=False,
    )
```

```python
import functools

import jax
import jax.numpy as jnp
from jax import lax
from jax.experimental import pallas as pl
from jax.experimental.pallas import tpu as pltpu
from jax.sharding import PartitionSpec as P

D = 768
DIN = 1536
HEADS = 24
HEAD_DIM = 64
STATE = 128
CONV = 4
XBC = 1792
PROJ = 3352
EPS = 1e-05
LOG2E = 1.4426950408889634
CHUNK = 128
TILE = 256
HALO = 16
UNIT = 16
KIND = jnp.float32
F32 = jnp.float32
BF16 = jnp.bfloat16
VMEM_LIMIT = 62 * 1024 * 1024


def mm(a, b):
    return lax.dot_general(a, b, (((1,), (0,)), ((), ())), preferred_element_type=F32)


def mm_nt(a, b):
    return lax.dot_general(a, b, (((1,), (1,)), ((), ())), preferred_element_type=F32)


def mm_tn(a, b):
    return lax.dot_general(a, b, (((0,), (0,)), ((), ())), preferred_element_type=F32)


def split2(v):
    hi = v.astype(BF16)
    return hi, (v - hi.astype(F32)).astype(BF16)


def split3(v):
    hi = v.astype(BF16)
    rest = v - hi.astype(F32)
    mid = rest.astype(BF16)
    return hi, mid, (rest - mid.astype(F32)).astype(BF16)


def iota(shape, dim):
    return lax.broadcasted_iota(jnp.int32, shape, dim)


def spread_matrix(start, width):
    head = iota((2 * STATE, width), 0) & (STATE - 1)
    column = (iota((2 * STATE, width), 1) + start) >> 6
    return jnp.where(head == column, 1.0, 0.0).astype(BF16)


def gather_matrix():
    return jnp.where((iota((DIN, STATE), 0) >> 6) == iota((DIN, STATE), 1), 1.0, 0.0).astype(BF16)


def spread(v, matrix):
    return mm(jnp.concatenate(split2(v), axis=1), matrix)


def head_sums(v, matrix, parts=3):
    pieces = split3(v) if parts == 3 else split2(v)
    total = mm(pieces[0], matrix)
    for piece in pieces[1:]:
        total = total + mm(piece, matrix)
    return total


def fine_nt(a, b):
    ah, al = split2(a)
    bh, bl = split2(b)
    return mm_nt(jnp.concatenate([ah, ah, al], axis=1), jnp.concatenate([bh, bl, bh], axis=1))


def halves(v):
    return jnp.concatenate(split2(v), axis=0)


def triangle(upper):
    row, column = iota((CHUNK, CHUNK), 0), iota((CHUNK, CHUNK), 1)
    keep = column >= row if upper else column <= row
    return jnp.where(keep, 1.0, 0.0).astype(BF16)


def tri_sum(tri, v):
    return mm(jnp.concatenate([tri] * 3, axis=1), jnp.concatenate(split3(v), axis=0))


def head_params(hp_ref):
    hp = hp_ref[...]
    decay = -jnp.exp(-4.0 + 0.25 * hp[0:1])
    bias = -9.0 + 0.25 * hp[1:2]
    return decay, bias, hp


def sigmoid(v):
    return 1.0 / (1.0 + jnp.exp(-v))


def norm_rows(tok, gain):
    src = tok.astype(F32)
    scale = lax.rsqrt(jnp.mean(src * src, axis=-1, keepdims=True) + EPS)
    return src, scale, (src * scale * gain).astype(BF16)


def pair_masks():
    low = iota((CHUNK, STATE), 1) < HEAD_DIM
    return low, jnp.logical_not(low)


def doubled(v):
    low, high = pair_masks()
    wide = v.astype(F32)
    return jnp.concatenate([jnp.where(low, wide, 0.0).astype(BF16), jnp.where(high, wide, 0.0).astype(BF16)], axis=0)


def k1_body(tok_ref, halo_ref, w_ref, ws_ref, cw_ref, cb_ref, ng_ref, hp_ref,
            gate_ref, cin_ref, cout_ref, bc_ref, ypart_ref, info_ref, sl_ref, sdev_ref, tot_ref, cum_ref, chalo_ref,
            cpad, an, u, ub, dt2, tw2):
    T = tok_ref.shape[1]
    NC = T // CHUNK
    decay, bias, hp = head_params(hp_ref)
    decay2 = decay * LOG2E
    gain = ng_ref[...]
    first = lax.axis_index("seq") == 0
    an[0:HALO] = jnp.where(first, 0.0, norm_rows(halo_ref[0], gain)[2].astype(F32)).astype(BF16)
    an[HALO:] = norm_rows(tok_ref[0], gain)[2]
    arg = mm_nt(an[HALO:], ws_ref[...]) + bias
    dt = jnp.maximum(arg, 0.0) + jnp.log1p(jnp.exp(-jnp.abs(arg)))
    info_ref[0, 0] = arg
    info_ref[0, 1] = dt
    dt2[...] = jnp.concatenate(split2(dt), axis=1)
    tri = triangle(False)
    total = jnp.zeros((1, STATE), F32)
    ends = []
    for c in range(NC):
        rows = slice(c * CHUNK, (c + 1) * CHUNK)
        lc = tri_sum(tri, dt[rows] * decay2)
        info_ref[0, 2, rows] = lc
        ends.append(lc[CHUNK - 1:CHUNK])
        total = total + ends[-1]
        tw2[rows] = jnp.concatenate(split2(jnp.exp2(lc[CHUNK - 1:CHUNK] - lc)), axis=1)

    tot_ref[pl.ds(pl.program_id(0), 1)] = total
    before, after = jnp.zeros((1, STATE), F32), jnp.zeros((1, STATE), F32)
    for c in range(NC + 1):
        cum_ref[0, 0, c:c + 1] = before
        cum_ref[0, 1, NC - c:NC - c + 1] = after
        if c < NC:
            before, after = before + ends[c], after + ends[NC - 1 - c]

    @pl.loop(0, DIN // TILE)
    def _(j):
        cols = pl.ds(pl.multiple_of(j * TILE, TILE), TILE)
        gate_ref[0, :, cols] = mm_nt(an[HALO:], w_ref[cols, :])

    def conv_tile(j, cols):
        wcols = pl.ds(pl.multiple_of(DIN + j * TILE, TILE), TILE)
        raw = mm_nt(an[...], w_ref[wcols, :])
        cpad[...] = raw
        cin_ref[0, :, cols] = raw[HALO:]
        chalo_ref[0, :, cols] = raw[:HALO]
        out = cb_ref[:, cols]
        for k in range(CONV):
            out = out + cw_ref[k:k + 1, cols] * cpad[HALO - CONV + 1 + k:HALO - CONV + 1 + k + T]
        cout_ref[0, :, cols] = out
        return out * sigmoid(out)

    @pl.loop(0, DIN // TILE)
    def _(j):
        cols = pl.ds(pl.multiple_of(j * TILE, TILE), TILE)
        x = conv_tile(j, cols)
        matrix = spread_matrix(j * TILE, TILE)
        ux = x * mm(dt2[...], matrix)
        u[:, cols] = ux.astype(BF16)
        hi, lo = split2(ux * mm(tw2[...], matrix))
        for c in range(NC):
            rows = slice(c * CHUNK, (c + 1) * CHUNK)
            ub[c, 0:CHUNK, cols] = hi[rows]
            ub[c, CHUNK:, cols] = lo[rows]
        skip_tile = spread(jnp.broadcast_to(hp[2:3], (8, STATE)), matrix)[0:1]
        ypart_ref[0, :, cols] = x * skip_tile

    bc_ref[0] = conv_tile(DIN // TILE, pl.ds(DIN, TILE))

    causal = iota((CHUNK, CHUNK), 0) >= iota((CHUNK, CHUNK), 1)
    sdev_ref[0] = jnp.zeros((STATE, DIN), F32)

    @pl.loop(0, NC)
    def _(c):
        rows = pl.ds(pl.multiple_of(c * CHUNK, CHUNK), CHUNK)
        b = bc_ref[0, rows, 0:STATE]
        gram = jnp.where(causal, fine_nt(bc_ref[0, rows, STATE:2 * STATE], b), 0.0)
        b16 = b.astype(BF16)
        lc = info_ref[0, 2, rows]
        lct = lc.T
        sl_ref[0, c] = sdev_ref[0]
        total = jnp.exp2(jnp.broadcast_to(lc[CHUNK - 1:CHUNK], (8, STATE)))
        keep = spread(total, spread_matrix(0, DIN))[0:1]
        sdev_ref[0] = keep * sdev_ref[0] + mm_tn(jnp.concatenate([b16, b16], axis=0), ub[c])
        for p in range(HEADS // 2):
            cols = slice(p * STATE, (p + 1) * STATE)
            mixes = []
            for h in (2 * p, 2 * p + 1):
                gap = lc[:, h:h + 1] - lct[h:h + 1, :]
                mixes.append((gram * jnp.exp2(jnp.minimum(gap, 0.0))).astype(BF16))
            ypart_ref[0, rows, cols] = ypart_ref[0, rows, cols] + mm(jnp.concatenate(mixes, axis=1), doubled(u[rows, cols]))

    sl_ref[0, NC] = sdev_ref[0]


def whole(shape):
    rank = len(shape)
    return pl.BlockSpec(shape, lambda m: (0,) * rank)


def per_micro(shape, buffers=None):
    rank = len(shape)
    mode = None if buffers is None else pl.Buffered(buffers)
    return pl.BlockSpec((1,) + shape, lambda m: (m,) + (0,) * rank, pipeline_mode=mode)


def call(body, grid, ins, outs, scratch, name):
    return pl.pallas_call(
        body,
        grid=grid,
        in_specs=[s for s, _ in ins],
        out_specs=[s for s, _ in outs],
        out_shape=[o for _, o in outs],
        scratch_shapes=scratch,
        compiler_params=pltpu.CompilerParams(vmem_limit_bytes=VMEM_LIMIT, dimension_semantics=("arbitrary",) * len(grid)),
        name=name,
    )(*[a for _, a in ins])


def k1(tok, halo, w, ws, cw, cb, ng, hp):
    M, T, _ = tok.shape
    NC = T // CHUNK
    S = lambda shape, dt: (per_micro(shape), jax.ShapeDtypeStruct((M,) + shape, dt))
    return call(
        k1_body, (M,),
        [(per_micro((T, D)), tok), (per_micro((HALO, D)), halo), (whole(w.shape), w), (whole(ws.shape), ws),
         (whole(cw.shape), cw), (whole(cb.shape), cb), (whole(ng.shape), ng), (whole(hp.shape), hp)],
        [S((T, DIN), F32), S((T, XBC), F32), S((T, XBC), F32), S((T, 2 * STATE), F32), S((T, DIN), F32),
         S((3, T, STATE), F32), S((NC + 1, STATE, DIN), F32), S((STATE, DIN), F32),
         (whole((M, STATE)), jax.ShapeDtypeStruct((M, STATE), F32)), S((2, NC + 1, STATE), F32), S((HALO, XBC), F32)],
        [pltpu.VMEM((HALO + T, TILE), F32), pltpu.VMEM((HALO + T, D), BF16), pltpu.VMEM((T, DIN), BF16), pltpu.VMEM((NC, 2 * CHUNK, DIN), BF16),
         pltpu.VMEM((T, 2 * STATE), BF16), pltpu.VMEM((T, 2 * STATE), BF16)],
        "forward_local",
    )


def chunk_totals(info_ref, NC):
    return [info_ref[0, 2, (c + 1) * CHUNK - 1:(c + 1) * CHUNK] for c in range(NC)]


def product_sum(left, right, cols):
    total = mm(left[0], right[0, :, cols])
    for m in range(1, left.shape[0]):
        total = total + mm(left[m], right[m, :, cols])
    return total


def put_tile(gtile_ref, d, tile, part):
    count = part.shape[0] // UNIT
    gtile_ref[d, pl.ds(tile * count, count)] = part.reshape(count, UNIT, STATE)


def clear_tiles(gtile_ref, rows, tiles):
    low, high = tiles * (rows // UNIT), gtile_ref.shape[1]
    if high > low:
        gtile_ref[:, low:] = jnp.zeros((gtile_ref.shape[0], high - low, UNIT, STATE), BF16)


def weight_tiles(gtile_ref, rows, left, right, count):
    @pl.loop(0, count)
    def _(j):
        part = product_sum(left, right, pl.ds(pl.multiple_of(j * STATE, STATE), STATE)).astype(BF16)
        for d in range(gtile_ref.shape[0]):
            put_tile(gtile_ref, d, j, part[d * rows:(d + 1) * rows])


def k2_body(tok_ref, cot_ref, ng_ref, og_ref, wo_ref, hp_ref, gate_ref, ypart_ref, bc_ref, info_ref, sl_ref, start_ref,
            mixed_ref, dgate_ref, dy_ref, r_ref, gl_ref, gdev_ref, ogr_ref, branch_t_ref, norm_t_ref,
            y, dbr, branch, oscale):
    m = pl.program_id(0)
    T = tok_ref.shape[1]
    NC = T // CHUNK
    matrix = spread_matrix(0, DIN)
    gather = gather_matrix()
    src, _, normed = norm_rows(tok_ref[0], ng_ref[...])
    norm_t_ref[0] = normed.T

    @pl.when(m == 0)
    def _():
        ogr_ref[...] = jnp.zeros_like(ogr_ref)

    totals = chunk_totals(info_ref, NC)
    before = jnp.zeros((1, STATE), F32)
    for c in range(NC):
        rows = slice(c * CHUNK, (c + 1) * CHUNK)
        keep = spread(jnp.exp2(jnp.broadcast_to(before, (8, STATE))), matrix)[0:1]
        before = before + totals[c]
        state = halves(sl_ref[0, c].astype(F32) + keep * start_ref[0].astype(F32))
        c16 = bc_ref[0, rows, STATE:2 * STATE].astype(BF16)
        lift = spread(jnp.exp2(info_ref[0, 2, rows]), matrix)
        yc = ypart_ref[0, rows] + lift * mm(jnp.concatenate([c16, c16], axis=1), state)
        y[rows] = yc
        g = gate_ref[0, rows]
        gated = yc * (g * sigmoid(g))
        scale = lax.rsqrt(jnp.mean(gated * gated, axis=-1, keepdims=True) + EPS)
        oscale[rows] = jnp.broadcast_to(scale, (CHUNK, STATE))
        branch[rows] = (gated * scale * og_ref[...]).astype(BF16)
    branch_t_ref[0] = branch[...].T
    cot = cot_ref[0]
    for j in range(D // TILE):
        cols = slice(j * TILE, (j + 1) * TILE)
        mixed_ref[0, :, cols] = (tok_ref[0, :, cols].astype(F32) + mm(branch[...], wo_ref[:, cols])).astype(BF16)

    @pl.loop(0, DIN // TILE)
    def _(j):
        cols = pl.ds(pl.multiple_of(j * TILE, TILE), TILE)
        dbr[:, cols] = mm_nt(cot, wo_ref[cols, :])

    gdev_ref[0] = jnp.zeros((STATE, DIN), F32)

    @pl.loop(0, NC)
    def _(i):
        c = NC - 1 - i
        rows = pl.ds(pl.multiple_of(c * CHUNK, CHUNK), CHUNK)
        g = gate_ref[0, rows]
        yc = y[rows]
        db = dbr[rows]
        scale = oscale[rows][:, 0:1]
        sig = sigmoid(g)
        act = g * sig
        gated = yc * act
        unit = gated * scale
        ogr_ref[...] += jnp.sum(db * unit, axis=0, keepdims=True)
        e = db * og_ref[...]
        mean = jnp.mean(e * unit, axis=-1, keepdims=True)
        dgated = scale * (e - unit * mean)
        dgate_ref[0, rows] = (dgated * yc * (sig * (1.0 + g * (1.0 - sig)))).astype(BF16)
        high, low = split2(dgated * act)
        dyf = high.astype(F32) + low.astype(F32)
        dy_ref[0, rows] = dyf
        r_ref[0, rows] = head_sums(dyf * yc, gather)
        lc = info_ref[0, 2, rows]
        lifted = halves(dyf * spread(jnp.exp2(lc), matrix))
        c16 = bc_ref[0, rows, STATE:2 * STATE].astype(BF16)
        gl_ref[0, c] = gdev_ref[0]
        total = jnp.exp2(jnp.broadcast_to(lc[CHUNK - 1:CHUNK], (8, STATE)))
        keep = spread(total, matrix)[0:1]
        gdev_ref[0] = keep * gdev_ref[0] + mm_tn(jnp.concatenate([c16, c16], axis=0), lifted)


def early_grads_body(norm_t, branch_t, dgate, cot, gtile_ref):
    dp = gtile_ref.shape[0]
    rows = D // dp
    weight_tiles(gtile_ref, rows, norm_t, dgate, DIN // STATE)
    clear_tiles(gtile_ref, rows, 24)

    @pl.loop(0, D // STATE)
    def _(j):
        part = product_sum(branch_t, cot, pl.ds(pl.multiple_of(j * STATE, STATE), STATE)).astype(BF16)
        for d in range(dp):
            for half in range(2):
                low = (2 * d + half) * rows
                put_tile(gtile_ref, d, 12 + half * 6 + j, part[low:low + rows])


def early_grads(norm_t, branch_t, dgate, cot, dp, units):
    vmem = pl.BlockSpec(memory_space=pltpu.VMEM)
    return pl.pallas_call(
        early_grads_body,
        in_specs=[vmem] * 4,
        out_specs=vmem,
        out_shape=jax.ShapeDtypeStruct((dp, units, UNIT, STATE), BF16),
        compiler_params=pltpu.CompilerParams(vmem_limit_bytes=VMEM_LIMIT),
        name="early_gradients",
    )(norm_t, branch_t, dgate, cot)


def k2(tok, cot, ng, og, wo, hp, gate, ypart, bc, info, sl, start):
    M, T, _ = tok.shape
    NC = T // CHUNK
    S = lambda shape, dt: (per_micro(shape), jax.ShapeDtypeStruct((M,) + shape, dt))
    W = lambda shape, dt: (whole(shape), jax.ShapeDtypeStruct(shape, dt))
    one = lambda a, n=1: (per_micro(a.shape[1:], n), a)
    all_ = lambda a: (whole(a.shape), a)
    return call(
        k2_body, (M,),
        [one(tok), one(cot), all_(ng), all_(og), all_(wo), all_(hp), one(gate), one(ypart, 1), one(bc), one(info), one(sl), one(start, 1)],
        [S((T, D), BF16), S((T, DIN), BF16), S((T, DIN), F32), S((T, STATE), F32), S((NC, STATE, DIN), F32),
         S((STATE, DIN), F32), W((1, DIN), F32), S((DIN, T), BF16), S((D, T), BF16)],
        [pltpu.VMEM((T, DIN), F32), pltpu.VMEM((T, DIN), F32), pltpu.VMEM((T, DIN), BF16), pltpu.VMEM((T, STATE), F32)],
        "gate_and_out",
    )


MESH = pl.DeviceIdType.MESH
PLANE = 4
QUARTER = DIN // PLANE
DMA = pltpu.SemaphoreType.DMA


def places():
    seq = lax.axis_index("seq")
    return lax.axis_index("dp"), seq, lax.rem(seq, PLANE), lax.div(seq, PLANE)


def greet(devices):
    barrier = pltpu.get_barrier_semaphore()
    for device in devices:
        pl.semaphore_signal(barrier, inc=1, device_id=device, device_id_type=MESH)
    pl.semaphore_wait(barrier, len(devices))


def remote(src, dst, send, recv, device):
    return pltpu.make_async_remote_copy(
        src_ref=src, dst_ref=dst, send_sem=send, recv_sem=recv, device_id=device, device_id_type=MESH)


def open_body(ndp, nseq, win_ref, ws_ref, wout_ref, tok_ref, w_ref, wsall_ref, wo_ref, halo_ref, send, recv, hsend, hrecv):
    dp, seq, _, _ = places()
    nxt, prev = lax.rem(seq + 1, nseq), lax.rem(seq + nseq - 1, nseq)
    others = [lax.rem(dp + d, ndp) for d in range(1, ndp)]
    greet([(o, seq) for o in others] + [(dp, nxt), (dp, prev)])
    T = tok_ref.shape[1]
    width, rows = win_ref.shape[1], wout_ref.shape[0]
    columns = pl.ds(pl.multiple_of(dp * width, width), width)
    own_rows = pl.ds(pl.multiple_of(dp * rows, rows), rows)
    moves = [(ws_ref, wsall_ref.at[:, columns]), (win_ref.at[0:DIN + XBC], w_ref.at[:, columns]), (wout_ref, wo_ref.at[own_rows])]
    copies = [remote(tok_ref.at[:, T - HALO:T], halo_ref, hsend, hrecv, (dp, nxt))]
    for i, o in enumerate(others):
        for k, (src, dst) in enumerate(moves):
            copies.append(remote(src, dst, send.at[i, k], recv.at[i, k], (o, seq)))
    for copy in copies:
        copy.start()
    w_ref[:, columns] = win_ref[0:DIN + XBC]
    wsall_ref[:, columns] = ws_ref[...]
    wo_ref[own_rows] = wout_ref[...]
    for copy in copies:
        copy.wait()


def open_kernel(ndp, nseq, win, ws, wout, tok):
    vmem = pl.BlockSpec(memory_space=pltpu.VMEM)
    M = tok.shape[0]
    shape = lambda *s: jax.ShapeDtypeStruct(s, BF16)
    return pl.pallas_call(
        functools.partial(open_body, ndp, nseq),
        in_specs=[vmem] * 3 + [pl.BlockSpec(memory_space=pl.ANY)],
        out_specs=[vmem] * 4,
        out_shape=[shape(DIN + XBC, D), shape(STATE, D), shape(DIN, D), shape(M, HALO, D)],
        scratch_shapes=[DMA((ndp - 1, 3)), DMA((ndp - 1, 3)), DMA, DMA],
        compiler_params=pltpu.CompilerParams(collective_id=1, has_side_effects=True, vmem_limit_bytes=VMEM_LIMIT),
        name="gather_weights",
    )(win, ws, wout, tok)


def states_body(nseq, upward, s_ref, tot_ref, out_ref, stage, got, tots, pre, back, hop, sems, rsems, tsem, trsem, zs, zr, bs, br):
    dp, seq, p, z = places()
    M = s_ref.shape[0]
    Z = nseq // PLANE
    base = z * PLANE
    peers = [lax.rem(p + d, PLANE) for d in range(PLANE)]
    zup, zdown = lax.rem(seq + PLANE, nseq), lax.rem(seq + nseq - PLANE, nseq)
    greet([(dp, base + peers[d]) for d in range(1, PLANE)] + [(dp, zup), (dp, zdown)])
    columns = lambda q: pl.ds(pl.multiple_of(q * QUARTER, QUARTER), QUARTER)
    tots[0] = tot_ref[...]
    tcopies = [remote(tot_ref, tots.at[d], tsem.at[d - 1], trsem.at[d - 1], (dp, base + peers[d])) for d in range(1, PLANE)]
    for copy in tcopies:
        copy.start()
    first = []
    for m in range(M):
        stage[m] = s_ref[m].astype(stage.dtype)
        row = []
        for d in range(1, PLANE):
            copy = remote(stage.at[m, :, columns(peers[d])], got.at[m, d], sems.at[m, d - 1], rsems.at[m, d - 1], (dp, base + peers[d]))
            copy.start()
            row.append(copy)
        first.append(row)
    for copy in tcopies:
        copy.wait()
    shift = peers[0] * QUARTER
    order = list(range(PLANE))[::-1] if upward else list(range(PLANE))
    towards = zdown if upward else zup
    head = (z == Z - 1) if upward else (z == 0)
    tail = (z == 0) if upward else (z == Z - 1)
    last = []
    for m in range(M):
        for copy in first[m]:
            copy.wait_recv()
        matrix = spread_matrix(shift, QUARTER)
        slots = [lax.rem(p - q + PLANE, PLANE) for q in order]
        keep = [spread(jnp.exp2(jnp.broadcast_to(tots[s, m:m + 1], (8, STATE))), matrix)[0:1] for s in slots]

        got[m, 0] = s_ref[m, :, columns(p)].astype(got.dtype)
        link = remote(hop.at[m], pre.at[m], zs.at[m], zr.at[m], (dp, towards))

        @pl.when(head)
        def _():
            pre[m] = jnp.zeros_like(pre[m])

        @pl.when(jnp.logical_not(head))
        def _():
            link.wait_recv()

        run = pre[m].astype(F32)
        for i, q in enumerate(order):
            back[m, slots[i]] = run.astype(back.dtype)
            run = keep[i] * run + got[m, slots[i]].astype(F32)
        hop[m] = run.astype(hop.dtype)

        @pl.when(jnp.logical_not(tail))
        def _():
            link.start()

        for d in range(1, PLANE):
            to = lax.rem(p + PLANE - d, PLANE)
            copy = remote(back.at[m, d], out_ref.at[m, :, columns(p)], bs.at[m, d - 1], br.at[m, d - 1], (dp, base + to))
            copy.start()
            last.append(copy)
        out_ref[m, :, columns(p)] = back[m, 0]
    for row in first:
        for copy in row:
            copy.wait_send()
    for copy in last:
        copy.wait()
    for m in range(M):
        link = remote(hop.at[m], pre.at[m], zs.at[m], zr.at[m], (dp, towards))

        @pl.when(jnp.logical_not(tail))
        def _():
            link.wait_send()


def exchange(nseq, upward, s, tot, kind):
    M = s.shape[0]
    V = pltpu.VMEM
    vmem = pl.BlockSpec(memory_space=pltpu.VMEM)
    quarter = (STATE, QUARTER)
    return pl.pallas_call(
        functools.partial(states_body, nseq, upward),
        in_specs=[vmem] * 2,
        out_specs=vmem,
        out_shape=jax.ShapeDtypeStruct(s.shape, kind),
        scratch_shapes=[V(s.shape, kind), V((M, PLANE) + quarter, kind), V((PLANE,) + tot.shape, F32), V((M,) + quarter, kind),
                        V((M, PLANE) + quarter, kind), V((M,) + quarter, kind),
                        DMA((M, 3)), DMA((M, 3)), DMA((3,)), DMA((3,)), DMA((M,)), DMA((M,)), DMA((M, 3)), DMA((M, 3))],
        compiler_params=pltpu.CompilerParams(collective_id=3 if upward else 2, has_side_effects=True, vmem_limit_bytes=VMEM_LIMIT),
        name="states_later" if upward else "states_earlier",
    )(s, tot)


SMALL = (("cw", CONV, XBC), ("cb", 1, XBC), ("ng", 1, D), ("og", 1, DIN), ("skip", 1, DIN), ("head", 2, STATE))
SMALL_ROWS = 104


def small_pieces():
    row, found = 0, []
    for index, (_, rows, width) in enumerate(SMALL):
        for r in range(rows):
            for j in range(width // STATE):
                found.append((index, r, j, row))
                row += 1
    return found


def strided(count, body):
    step = max(s for s in range(1, 13) if count % s == 0)

    @pl.loop(0, count // step)
    def _(i):
        body(pl.multiple_of(i * step, step), step)


GROUPS = 4


def units(ndp, nseq, tiles):
    need, step = tiles * (D // ndp // UNIT), GROUPS * nseq
    return -(-need // step) * step


def reducer_scratch(ndp, nseq, count):
    Z = nseq // PLANE
    u = lambda n, *lead: tuple(lead) + (n, UNIT, STATE)
    V = pltpu.VMEM
    pairs = [DMA((GROUPS, ndp - 1))] * 2 + [DMA((GROUPS,))] * 4 + [DMA((GROUPS, Z - 1))] * 4 + [DMA((GROUPS,))] * 4
    return [V(u(count, ndp - 1), BF16), V(u(count // 2), F32), V(u(count // 2), BF16), V(u(count // 2), BF16),
            V(u(count // 4), F32), V(u(count // 4), BF16), V(u(count // 4), BF16), V(u(count // 4), BF16),
            V(u(count // 4 // Z, Z - 1), BF16)] + pairs


class Reducer:
    def __init__(self, ndp, nseq, src, out, scratch):
        self.ndp, self.Z = ndp, nseq // PLANE
        self.src, self.out = src, out
        (self.r0, self.w1, self.st1, self.r1, self.w2, self.st2, self.r2, self.st3, self.r3) = scratch[:9]
        self.sems = [(scratch[9 + 2 * k], scratch[10 + 2 * k]) for k in range(7)]
        self.dp, self.seq, self.p, self.z = places()
        x, y = lax.rem(self.p, 2), lax.div(self.p, 2)
        self.others = [lax.rem(self.dp + d, ndp) for d in range(1, ndp)]
        self.pz = [lax.rem(self.z + d, self.Z) * PLANE + self.p for d in range(1, self.Z)]
        sides = ((x, self.seq + 1 - 2 * x), (y, self.seq + 2 - 4 * y))
        self.sides = [sides if g % 2 == 0 else sides[::-1] for g in range(GROUPS)]
        self.size = src.shape[1] // GROUPS
        self.half, self.quarter = self.size // 2, self.size // 4
        self.piece = self.quarter // self.Z

    def partners(self):
        (_, px), (_, py) = self.sides[0]
        return [(o, self.seq) for o in self.others] + [(self.dp, q) for q in (px, py)] + [(self.dp, q) for q in self.pz]

    def copies(self, stage, g):
        sizes, at = self.size, g * self.size
        o1, o2, o3 = g * self.half, g * self.quarter, g * self.piece
        send, recv = self.sems[stage]
        (b1, peer1), (b2, peer2) = self.sides[g]
        half_at = at + b1 * self.half
        quarter_at = half_at + b2 * self.quarter
        piece_at = quarter_at + self.z * self.piece
        if stage == 0:
            return [remote(self.src.at[o, pl.ds(at, sizes)], self.r0.at[i, pl.ds(at, sizes)], send.at[g, i], recv.at[g, i], (o, self.seq))
                    for i, o in enumerate(self.others)]
        if stage == 1:
            span = pl.ds(o1, self.half)
            return [remote(self.st1.at[span], self.r1.at[span], send.at[g], recv.at[g], (self.dp, peer1))]
        if stage == 2:
            span = pl.ds(o2, self.quarter)
            return [remote(self.st2.at[span], self.r2.at[span], send.at[g], recv.at[g], (self.dp, peer2))]
        if stage == 3:
            return [remote(self.st3.at[pl.ds(o2 + lax.rem(self.z + d, self.Z) * self.piece, self.piece)], self.r3.at[d - 1, pl.ds(o3, self.piece)],
                           send.at[g, d - 1], recv.at[g, d - 1], (self.dp, self.pz[d - 1])) for d in range(1, self.Z)]
        if stage == 4:
            span = pl.ds(piece_at, self.piece)
            return [remote(self.out.at[span], self.out.at[span], send.at[g, d - 1], recv.at[g, d - 1], (self.dp, self.pz[d - 1]))
                    for d in range(1, self.Z)]
        span, peer = (pl.ds(quarter_at, self.quarter), peer2) if stage == 5 else (pl.ds(half_at, self.half), peer1)
        return [remote(self.out.at[span], self.out.at[span], send.at[g], recv.at[g], (self.dp, peer))]

    def stage(self, stage, g):
        if stage > 0:
            for copy in self.copies(stage - 1, g):
                copy.wait_recv()
        if stage == 7:
            return
        (b1, _), (b2, _) = self.sides[g]
        at, o1, o2, o3 = g * self.size, g * self.half, g * self.quarter, g * self.piece
        if stage == 1:
            def total(i, c):
                v = self.src[self.dp, pl.ds(at + i, c)].astype(F32)
                for k in range(self.ndp - 1):
                    v = v + self.r0[k, pl.ds(at + i, c)].astype(F32)
                return v

            def body(i, c):
                self.w1[pl.ds(o1 + i, c)] = total(b1 * self.half + i, c)
                self.st1[pl.ds(o1 + i, c)] = total((1 - b1) * self.half + i, c).astype(BF16)
            strided(self.half, body)
        elif stage == 2:
            def body(i, c):
                keep, give = pl.ds(o1 + b2 * self.quarter + i, c), pl.ds(o1 + (1 - b2) * self.quarter + i, c)
                self.w2[pl.ds(o2 + i, c)] = self.w1[keep] + self.r1[keep].astype(F32)
                self.st2[pl.ds(o2 + i, c)] = (self.w1[give] + self.r1[give].astype(F32)).astype(BF16)
            strided(self.quarter, body)
        elif stage == 3:
            def body(i, c):
                span = pl.ds(o2 + i, c)
                v = self.w2[span] + self.r2[span].astype(F32)
                self.w2[span] = v
                self.st3[span] = v.astype(BF16)
            strided(self.quarter, body)
        elif stage == 4:
            v = self.w2[pl.ds(o2 + self.z * self.piece, self.piece)]
            for d in range(self.Z - 1):
                v = v + self.r3[d, pl.ds(o3, self.piece)].astype(F32)
            self.out[pl.ds(at + b1 * self.half + b2 * self.quarter + self.z * self.piece, self.piece)] = v.astype(BF16)
        for copy in self.copies(stage, g):
            copy.start()

    def ticks(self):
        def tick(k):
            if k == 0:
                for g in range(GROUPS):
                    self.stage(0, g)
                return
            for stage, groups in ((k, (0, 1)), (k - 1, (2, 3))):
                if 1 <= stage <= 7:
                    for g in groups:
                        self.stage(stage, g)
        return [functools.partial(tick, k) for k in range(9)]

    def finish(self):
        for stage in range(7):
            for g in range(GROUPS):
                for copy in self.copies(stage, g):
                    copy.wait_send()


def small_scratch(ndp, nseq):
    Z = nseq // PLANE
    V = pltpu.VMEM
    shape = (SMALL_ROWS, STATE)
    count = ndp - 1 + 2 + Z - 1
    return [V((ndp,) + shape, F32), V((2,) + shape, F32), V((2,) + shape, F32), V((Z,) + shape, F32), DMA((count,)), DMA((count,))]


class SmallReducer:
    def __init__(self, ndp, nseq, out, scratch):
        self.out = out
        self.bufs, (self.send, self.recv) = scratch[:4], scratch[4:6]
        dp, seq, p, z = places()
        Z = nseq // PLANE
        x, y = lax.rem(p, 2), lax.div(p, 2)
        self.z, self.Z = z, Z
        self.peers = [[(lax.rem(dp + d, ndp), seq) for d in range(1, ndp)], [(dp, seq + 1 - 2 * x)], [(dp, seq + 2 - 4 * y)],
                      [(dp, lax.rem(z + d, Z) * PLANE + p) for d in range(1, Z)]]
        self.at, self.begun, self.over, self.started = 0, False, False, []

    def send_all(self):
        buf = self.bufs[self.at]
        base = sum(len(q) for q in self.peers[:self.at])
        self.flying = [remote(buf.at[0], buf.at[1 + k], self.send.at[base + k], self.recv.at[base + k], device)
                       for k, device in enumerate(self.peers[self.at])]
        for copy in self.flying:
            copy.start()
        self.started += self.flying

    def begin(self, groups):
        buf = self.bufs[0]
        buf[0] = jnp.zeros(buf.shape[1:], F32)
        for index, r, j, row in small_pieces():
            v = groups[index][0][r:r + 1, j * STATE:(j + 1) * STATE]
            for other in groups[index][1:]:
                v = v + other[r:r + 1, j * STATE:(j + 1) * STATE]
            buf[0, row:row + 1] = v
        self.begun = True
        self.send_all()

    def advance(self):
        if self.over:
            return
        for copy in self.flying:
            copy.wait_recv()
        buf = self.bufs[self.at]
        if self.at < 3:
            v = buf[0]
            for k in range(1, buf.shape[0]):
                v = v + buf[k]
            self.at += 1
            self.bufs[self.at][0] = v
            self.send_all()
            return
        v = None
        for k in range(self.Z):
            piece = buf[lax.rem(self.z - k + self.Z, self.Z)]
            v = piece if v is None else v + piece
        self.out[...] = v
        self.over = True

    def finish(self):
        for copy in self.started:
            copy.wait_send()


def unpack_body(g1_ref, g2_ref, sm_ref, gin_ref, gout_ref, cw_ref, cb_ref, ng_ref, og_ref, head_ref):
    R = gin_ref.shape[1]
    U = R // UNIT
    tile = lambda ref, j: ref[j * U:(j + 1) * U].astype(F32).reshape(R, STATE)
    eye = jnp.where(iota((STATE, STATE), 0) == iota((STATE, STATE), 1), 1.0, 0.0).astype(BF16)
    turned = lambda ref, j: mm_nt(eye, ref[j * U:(j + 1) * U].reshape(R, STATE))
    for j in range(12):
        gin_ref[j * STATE:(j + 1) * STATE] = turned(g1_ref, j)
    for j in range(14):
        gin_ref[DIN + j * STATE:DIN + (j + 1) * STATE] = turned(g2_ref, j)
    gin_ref[DIN + XBC:] = turned(g2_ref, 14)[:HEADS]
    for half in range(2):
        for j in range(D // STATE):
            gout_ref[half * R:(half + 1) * R, j * STATE:(j + 1) * STATE] = tile(g1_ref, 12 + half * 6 + j)
    outs = {0: cw_ref, 1: cb_ref, 2: ng_ref, 3: og_ref}
    low, high = iota((1, STATE), 1) < HEAD_DIM, iota((1, STATE), 1)
    lane = iota((1, STATE), 1)
    skip = jnp.zeros((1, STATE), F32)
    for index, r, j, row in small_pieces():
        v = sm_ref[row:row + 1]
        if index in outs:
            outs[index][r:r + 1, j * STATE:(j + 1) * STATE] = v
        elif index == 4:
            left = jnp.sum(jnp.where(low, v, 0.0), axis=1, keepdims=True)
            right = jnp.sum(jnp.where(low, 0.0, v), axis=1, keepdims=True)
            skip = skip + jnp.where(lane == 2 * j, left, 0.0) + jnp.where(lane == 2 * j + 1, right, 0.0)
        else:
            head_ref[r + 1:r + 2] = v
    head_ref[0:1] = skip


def unpack(g1, g2, sm, R):
    vmem = pl.BlockSpec(memory_space=pltpu.VMEM)
    sds = lambda *s: jax.ShapeDtypeStruct(s, F32)
    return pl.pallas_call(
        unpack_body,
        in_specs=[vmem] * 3,
        out_specs=[vmem] * 7,
        out_shape=[sds(PROJ, R), sds(2 * R, D), sds(CONV, XBC), sds(1, XBC), sds(1, D), sds(1, DIN), sds(3, STATE)],
        compiler_params=pltpu.CompilerParams(vmem_limit_bytes=VMEM_LIMIT),
        name="unpack_gradients",
    )(g1, g2, sm)
def k3_body(ndp, nseq, hp_ref, cw_ref, chalo_ref, cum_ref, cin_ref, cout_ref, bc_ref, info_ref, sl_ref, sl_next_ref, start_ref, dy_ref, r_ref,
            gl_ref, later_ref, g1_ref,
            dcin_ref, tail_ref, head_ref, dstep_ref, gcw_ref, gcb_ref, gskip_ref, ghead_ref, sum1_ref,
            dconv, w, xdu, ub, dyl, dgt, dt_x, tail_x, bg, landing, *comm):
    m, i = pl.program_id(0), pl.program_id(1)
    NC = pl.num_programs(1)
    c = NC - 1 - i
    step = m * NC + i
    steps = pl.num_programs(0) * NC
    reducer = Reducer(ndp, nseq, g1_ref, landing, comm)
    ticks = reducer.ticks()
    for k, tick in enumerate(ticks[:-1]):

        @pl.when(step == k)
        def _():
            if k == 0:
                greet(reducer.partners())
            tick()

    decay, _, hp = head_params(hp_ref)
    matrix = spread_matrix(0, DIN)
    gather = gather_matrix()
    skip = spread(jnp.broadcast_to(hp[2:3], (8, STATE)), matrix)[0:1]

    @pl.when(step == 0)
    def _():
        gcw_ref[...] = jnp.zeros_like(gcw_ref)
        gcb_ref[...] = jnp.zeros_like(gcb_ref)
        gskip_ref[...] = jnp.zeros_like(gskip_ref)
        ghead_ref[...] = jnp.zeros_like(ghead_ref)

    @pl.when(i == 0)
    def _():
        dconv[CHUNK:] = jnp.zeros((8, XBC), F32)

    @pl.when(i > 0)
    def _():
        dconv[CHUNK:] = dconv[0:8]

    tri_up = triangle(True)
    b32 = bc_ref[0, :, 0:STATE]
    c32 = bc_ref[0, :, STATE:2 * STATE]
    keeps_st = iota((CHUNK, CHUNK), 0) <= iota((CHUNK, CHUNK), 1)
    gram_t = jnp.where(keeps_st, fine_nt(c32, b32).T, 0.0)
    b, cc = b32.astype(BF16), c32.astype(BF16)
    lc = info_ref[0, 2]
    lct = lc.T
    dt = info_ref[0, 1]
    dt_x[...] = spread(dt, matrix)
    tail_x[...] = spread(jnp.exp2(lc[CHUNK - 1:CHUNK] - lc), matrix)
    dyl[...] = (dy_ref[0] * spread(jnp.exp2(lc), matrix)).astype(BF16)
    wide8 = lambda v: spread(jnp.exp2(jnp.broadcast_to(v, (8, STATE))), matrix)[0:1]
    gc = gl_ref[0, 0] + wide8(cum_ref[0, 1, pl.ds(c + 1, 1)]) * later_ref[0].astype(F32)
    s_in = sl_ref[0, 0] + wide8(cum_ref[0, 0, pl.ds(c, 1)]) * start_ref[0].astype(F32)
    s_out = sl_next_ref[0, 0] + wide8(cum_ref[0, 0, pl.ds(c + 1, 1)]) * start_ref[0].astype(F32)
    gc2 = halves(gc)
    gcb16 = gc2[0:STATE]
    bnd = head_sums(jnp.broadcast_to(jnp.sum(gc * s_out, axis=0, keepdims=True), (8, DIN)), gather)[0:1]
    bg[...] = mm(jnp.concatenate([b, b], axis=1), gc2)
    dgt[...] = jnp.zeros((CHUNK, CHUNK), F32)
    for p in range(HEADS // 2):
        cols = slice(p * STATE, (p + 1) * STATE)
        v = cout_ref[0, :, cols]
        sig = sigmoid(v)
        x = v * sig
        dtx, tlx = dt_x[:, cols], tail_x[:, cols]
        ux = x * dtx
        u16 = ux.astype(BF16)
        ub[:, cols] = (ux * tlx).astype(BF16)
        dyf = dy_ref[0, :, cols]
        dy_high, dy_low = split2(dyf)
        dy2 = doubled(dy_high)
        decays, mixes = [], []
        for h in (2 * p, 2 * p + 1):
            gap = lct[h:h + 1, :] - lc[:, h:h + 1]
            e = jnp.exp2(jnp.minimum(gap, 0.0))
            decays.append(e)
            mixes.append((gram_t * e).astype(BF16))
        mix = jnp.concatenate(mixes, axis=1)
        du = mm(mix, dy2) + mm(mix, doubled(dy_low))
        dmix = mm_nt(u16, dy2)
        dgt[...] = dgt[...] + (dmix[:, :CHUNK] * decays[0] + dmix[:, CHUNK:] * decays[1])
        du_state = tlx * bg[:, cols]
        sk = skip[:, cols]
        dyx = dyf * x
        gskip_ref[:, cols] = gskip_ref[:, cols] + jnp.sum(dyx, axis=0, keepdims=True)
        w[:, cols] = dyx * sk + u16.astype(F32) * du + ux * du_state
        du = du + du_state
        xdu[:, cols] = x * du
        dx = dtx * du + sk * dyf
        dconv[0:CHUNK, cols] = dx * (sig * (1.0 + v * (1.0 - sig)))
    dg16 = jnp.where(keeps_st, dgt[...], 0.0).astype(BF16)
    db = mm(dg16, cc) + mm_nt(ub[...], gcb16)
    dc = mm_tn(dg16, b) + mm_nt(dyl[...], s_in.astype(BF16))
    v = cout_ref[0, :, DIN:XBC]
    sig = sigmoid(v)
    dconv[0:CHUNK, DIN:XBC] = jnp.concatenate([db, dc], axis=1) * (sig * (1.0 + v * (1.0 - sig)))
    dl = r_ref[0] - head_sums(w[...], gather)
    da = bnd + tri_sum(tri_up, dl)
    d_dt = head_sums(xdu[...], gather, 2) + da * decay
    dstep = d_dt * sigmoid(info_ref[0, 0])
    dstep_ref[0] = dstep.astype(BF16)
    ghead_ref[0:1] = ghead_ref[0:1] + decay * jnp.sum(da * dt, axis=0, keepdims=True)
    ghead_ref[1:2] = ghead_ref[1:2] + jnp.sum(dstep, axis=0, keepdims=True)

    @pl.loop(0, XBC // TILE)
    def _(j):
        cols = pl.ds(pl.multiple_of(j * TILE, TILE), TILE)
        gcb_ref[:, cols] = gcb_ref[:, cols] + jnp.sum(dconv[0:CHUNK, cols], axis=0, keepdims=True)
        own = cin_ref[0, :, cols]
        total = None
        for k in range(CONV):
            ahead = dconv[CONV - 1 - k:CONV - 1 - k + CHUNK, cols]
            gcw_ref[k:k + 1, cols] = gcw_ref[k:k + 1, cols] + jnp.sum(own * ahead, axis=0, keepdims=True)
            term = cw_ref[k:k + 1, cols] * ahead
            total = term if total is None else total + term
        dcin_ref[0, :, cols] = total.astype(BF16)

        @pl.when(i == 0)
        def _():
            tail_ref[0, :, cols] = total[CHUNK - HALO:]

    @pl.when(i == NC - 1)
    def _():
        head_ref[0] = dconv[0:8]
        for k in range(CONV - 1):
            for n in range(CONV - 1 - k):
                low = HALO - CONV + 1 + k + n
                gcw_ref[k:k + 1] = gcw_ref[k:k + 1] + chalo_ref[0, low:low + 1] * dconv[n:n + 1]

    @pl.when(step == steps - 1)
    def _():
        for tick in ticks[-1:]:
            tick()
        reducer.finish()

        def body(at, c):
            sum1_ref[pl.ds(at, c)] = landing[pl.ds(at, c)]
        strided(landing.shape[0], body)


def k3(ndp, nseq, hp, cw, chalo, cum, cin, cout, bc, info, sl, start, dy, r, gl, later, g1):
    M, T, _ = cout.shape
    NC = T // CHUNK
    at = lambda m, i: NC - 1 - i
    const = lambda a: (pl.BlockSpec(a.shape, lambda m, i: (0,) * a.ndim), a)
    micro = lambda a: (pl.BlockSpec((1,) + a.shape[1:], lambda m, i: (m,) + (0,) * (a.ndim - 1)), a)
    chunk = lambda a: (pl.BlockSpec((1, CHUNK) + a.shape[2:], lambda m, i: (m, at(m, i), 0)), a)
    entry = lambda a, ahead: (pl.BlockSpec((1, 1) + a.shape[2:], lambda m, i: (m, at(m, i) + ahead, 0, 0)), a)
    inner = (pl.BlockSpec((1, 3, CHUNK, STATE), lambda m, i: (m, 0, at(m, i), 0)), info)
    sds = jax.ShapeDtypeStruct
    C = lambda width, dt: (pl.BlockSpec((1, CHUNK, width), lambda m, i: (m, at(m, i), 0)), sds((M, T, width), dt))
    S = lambda rows: (pl.BlockSpec((1, rows, XBC), lambda m, i: (m, 0, 0)), sds((M, rows, XBC), F32))
    W = lambda shape, dt: (pl.BlockSpec(shape, lambda m, i: (0,) * len(shape)), sds(shape, dt))
    V = pltpu.VMEM
    ins = [const(hp), const(cw), micro(chalo), micro(cum), chunk(cin), chunk(cout), chunk(bc), inner, entry(sl, 0), entry(sl, 1), micro(start),
           chunk(dy), chunk(r), entry(gl, 0), micro(later), const(g1)]
    outs = [C(XBC, BF16), S(HALO), S(8), C(STATE, BF16), W((CONV, XBC), F32), W((1, XBC), F32), W((1, DIN), F32), W((2, STATE), F32),
            W(g1.shape[1:], BF16)]
    return pl.pallas_call(
        functools.partial(k3_body, ndp, nseq),
        grid=(M, NC),
        in_specs=[b for b, _ in ins],
        out_specs=[b for b, _ in outs],
        out_shape=[o for _, o in outs],
        scratch_shapes=[V((CHUNK + 8, XBC), F32), V((CHUNK, DIN), F32), V((CHUNK, DIN), F32), V((CHUNK, DIN), BF16), V((CHUNK, DIN), BF16),
                        V((CHUNK, CHUNK), F32), V((CHUNK, DIN), F32), V((CHUNK, DIN), F32), V((CHUNK, DIN), F32), V(g1.shape[1:], BF16)] + reducer_scratch(ndp, nseq, g1.shape[1]),
        compiler_params=pltpu.CompilerParams(vmem_limit_bytes=VMEM_LIMIT, dimension_semantics=("arbitrary",) * 2, collective_id=4,
                                             has_side_effects=True),
        name="scan_backward",
    )(*[a for _, a in ins])


def k4_body(ndp, nseq, M, tok_ref, cot_ref, ng_ref, w_ref, ws_ref, cw_ref, dgate_ref, dcin_ref, dstep_ref, tail_ref, head_ref, *refs):
    smalls, rest = refs[:5], refs[5:]
    gtok_ref, sum2_ref, small_out, g2, nxt, dc, norm_t, ngr, hsem, hrsem = rest[:10]
    count = len(reducer_scratch(ndp, nseq, g2.shape[1]))
    reducer = Reducer(ndp, nseq, g2, sum2_ref, rest[10:10 + count])
    tiny = SmallReducer(ndp, nseq, small_out, rest[10 + count:])
    T = tok_ref.shape[1]
    dp, seq, _, _ = places()
    following, prev = lax.rem(seq + 1, nseq), lax.rem(seq + nseq - 1, nseq)
    greet(reducer.partners() + [(dp, following), (dp, prev)])
    halo = remote(head_ref, nxt, hsem, hrsem, (dp, prev))
    halo.start()
    rows = D // ndp
    for m in range(M):
        norm_t[m] = norm_rows(tok_ref[m], ng_ref[...])[2].T
        dc[m, 0:T - HALO, 0:XBC] = dcin_ref[m, 0:T - HALO]
        dc[m, :, XBC:] = dstep_ref[m]
    clear_tiles(g2, rows, 15)
    halo.wait()
    last = seq == nseq - 1
    row = iota((HALO, XBC), 0)
    for m in range(M):
        tail = tail_ref[m]
        for s in range(CONV - 1):
            extra = jnp.zeros((1, XBC), F32)
            for k in range(s + 1):
                extra = extra + cw_ref[k:k + 1] * nxt[m, s - k:s - k + 1]
            tail = tail + jnp.where(jnp.logical_and(row == HALO - CONV + 1 + s, jnp.logical_not(last)), extra, 0.0)
        dc[m, T - HALO:T, 0:XBC] = tail.astype(BF16)
    weight_tiles(g2, rows, norm_t, dc, 15)
    ngr[...] = jnp.zeros_like(ngr)
    ticks = reducer.ticks()

    def backward(m, part):
        if part < D // TILE:
            cols = slice(part * TILE, (part + 1) * TILE)
            dn[:, cols] = (mm(dgate_ref[m], w_ref[0:DIN, cols]) + mm(dc[m, :, 0:XBC], w_ref[DIN:DIN + XBC, cols])
                           + mm(dstep_ref[m], ws_ref[:, cols]))
        else:
            src, scale, _ = norm_rows(tok_ref[m], ng_ref[...])
            unit = src * scale
            d_normed = dn[...]
            ngr[...] += jnp.sum(d_normed * unit, axis=0, keepdims=True)
            f = d_normed * ng_ref[...]
            mean = jnp.mean(f * unit, axis=-1, keepdims=True)
            gtok_ref[m] = (cot_ref[m].astype(F32) + scale * (f - unit * mean)).astype(BF16)

    dn = rest[-1]
    parts = [(m, part) for m in range(M) for part in range(D // TILE + 1)]
    per = -(-len(parts) // (len(ticks) - 2))
    ticks[0]()
    for k, tick in enumerate(ticks[1:]):
        for m, part in parts[:per]:
            backward(m, part)
        parts = parts[per:]
        tick()
        if not parts and not tiny.begun:
            tiny.begin([[r[...] for r in group] for group in small_groups(smalls, ngr, M)])
        elif tiny.begun:
            tiny.advance()
    while not tiny.over:
        tiny.advance()
    tiny.finish()
    reducer.finish()


def small_groups(smalls, ngr, M):
    gcw, gcb, gskip, ghead = smalls[:4]
    return [[gcw], [gcb], [ngr], list(smalls[4:4 + 1]), [gskip], [ghead]]


def k4(ndp, nseq, tok, cot, ng, w, ws, cw, dgate, dcin, dstep, tail, head, gcw, gcb, gskip, ghead, ogr):
    M, T, _ = tok.shape
    V = pltpu.VMEM
    sds = jax.ShapeDtypeStruct
    vmem = pl.BlockSpec(memory_space=pltpu.VMEM)
    count = units(ndp, nseq, 15)
    args = (tok, cot, ng, w, ws, cw, dgate, dcin, dstep, tail, head, gcw, gcb, gskip, ghead, ogr)
    return pl.pallas_call(
        functools.partial(k4_body, ndp, nseq, M),
        in_specs=[vmem] * len(args),
        out_specs=[vmem] * 3,
        out_shape=[sds((M, T, D), BF16), sds((count, UNIT, STATE), BF16), sds((SMALL_ROWS, STATE), F32)],
        scratch_shapes=[V((ndp, count, UNIT, STATE), BF16), V(head.shape, F32), V((M, T, XBC + STATE), BF16), V((M, D, T), BF16), V((1, D), F32),
                        DMA, DMA] + reducer_scratch(ndp, nseq, count) + small_scratch(ndp, nseq) + [V((T, D), F32)],
        compiler_params=pltpu.CompilerParams(collective_id=5, has_side_effects=True, vmem_limit_bytes=VMEM_LIMIT),
        name="projection_backward",
    )(*args)


def per_device(ndp, nseq, tokens, in_weight, out_weight, conv_weight, conv_bias, norm_gain, out_gain, skip_gain, rate_code, step_code, cotangent):
    micro, groups, T, _ = tokens.shape
    M = micro * groups
    tok = tokens.reshape(M, T, D)
    cot = cotangent.reshape(M, T, D)
    seq = lax.axis_index("seq")
    turned = in_weight.T
    steps = jnp.pad(turned[DIN + XBC:], ((0, STATE - HEADS), (0, 0)))
    if in_weight.shape[0] % STATE == 0:
        w, ws, wo, halo = open_kernel(ndp, nseq, turned, steps, out_weight, tok)
    else:
        w, ws, wo = [lax.all_gather(v, "dp", axis=at, tiled=True) for v, at in ((turned[:DIN + XBC], 1), (steps, 1), (out_weight, 0))]
        halo = lax.ppermute(tok[:, T - HALO:], "seq", [(i, i + 1) for i in range(nseq - 1)])
    pad = lambda v: jnp.pad(v.astype(F32), (0, STATE - HEADS))
    hp = jnp.stack([pad(rate_code), pad(step_code), pad(skip_gain)])
    ng, og, cb = norm_gain[None], out_gain[None], conv_bias[None]
    gate, cin, cout, bc, ypart, info, sl, sdev, totals, cum, chalo = k1(tok, halo, w, ws, conv_weight, cb, ng, hp)
    start = exchange(nseq, False, sdev, totals, KIND)
    mixed, dgate, dy, r, gl, gdev, ogr, branch_t, norm_t = k2(tok, cot, ng, og, wo, hp, gate, ypart, bc, info, sl, start)
    g1 = early_grads(norm_t, branch_t, dgate, cot, ndp, units(ndp, nseq, 24))
    later = exchange(nseq, True, gdev, totals, KIND)
    dcin, tail, head, dstep, gcw, gcb, gskip, ghead, sum1 = k3(
        ndp, nseq, hp, conv_weight, chalo, cum, cin, cout, bc, info, sl, start, dy, r, gl, later, g1)
    gtok, sum2, sm = k4(ndp, nseq, tok, cot, ng, w, ws, conv_weight, dgate, dcin, dstep, tail, head, gcw, gcb, gskip, ghead, ogr)
    g_in, g_out, cwg, cbg, ngg, ogg, heads = unpack(sum1, sum2, sm, D // ndp)
    return (mixed.reshape(tokens.shape), gtok.reshape(tokens.shape), g_in.T, g_out, cwg, cbg[0], ngg[0], ogg[0],
            heads[0, :HEADS], heads[1, :HEADS], heads[2, :HEADS])


def solution(mesh):
    rows, split = P("dp", None), P(None, "dp", "seq", None)
    return jax.shard_map(
        functools.partial(per_device, mesh.shape["dp"], mesh.shape["seq"]),
        mesh=mesh,
        in_specs=(split, rows, rows) + (P(),) * 7 + (split,),
        out_specs=(split, split, rows, rows) + (P(),) * 7,
        check_vma=False,
    )
```

```python
import functools

import jax
import jax.numpy as jnp
from jax import lax
from jax.experimental import pallas as pl
from jax.experimental.pallas import tpu as pltpu
from jax.sharding import PartitionSpec as P

D = 768
DIN = 1536
HEADS = 24
HEAD_DIM = 64
STATE = 128
CONV = 4
XBC = 1792
PROJ = 3352
EPS = 1e-05
LOG2E = 1.4426950408889634
CHUNK = 128
TILE = 256
HALO = 16
UNIT = 16
KIND = jnp.bfloat16
HOP_KIND = jnp.float32
F32 = jnp.float32
BF16 = jnp.bfloat16
VMEM_LIMIT = 62 * 1024 * 1024


def mm(a, b):
    return lax.dot_general(a, b, (((1,), (0,)), ((), ())), preferred_element_type=F32)


def mm_nt(a, b):
    return lax.dot_general(a, b, (((1,), (1,)), ((), ())), preferred_element_type=F32)


def mm_tn(a, b):
    return lax.dot_general(a, b, (((0,), (0,)), ((), ())), preferred_element_type=F32)


def split2(v):
    hi = v.astype(BF16)
    return hi, (v - hi.astype(F32)).astype(BF16)


def split3(v):
    hi = v.astype(BF16)
    rest = v - hi.astype(F32)
    mid = rest.astype(BF16)
    return hi, mid, (rest - mid.astype(F32)).astype(BF16)


def iota(shape, dim):
    return lax.broadcasted_iota(jnp.int32, shape, dim)


def spread_matrix(start, width):
    head = iota((2 * STATE, width), 0) & (STATE - 1)
    column = (iota((2 * STATE, width), 1) + start) >> 6
    return jnp.where(head == column, 1.0, 0.0).astype(BF16)


def gather_matrix():
    return jnp.where((iota((DIN, STATE), 0) >> 6) == iota((DIN, STATE), 1), 1.0, 0.0).astype(BF16)


def spread(v, matrix):
    return mm(jnp.concatenate(split2(v), axis=1), matrix)


def head_sums(v, matrix, parts=3):
    pieces = split3(v) if parts == 3 else split2(v)
    total = mm(pieces[0], matrix)
    for piece in pieces[1:]:
        total = total + mm(piece, matrix)
    return total


def fine_nt(a, b):
    ah, al = split2(a)
    bh, bl = split2(b)
    return mm_nt(jnp.concatenate([ah, ah, al], axis=1), jnp.concatenate([bh, bl, bh], axis=1))


def halves(v):
    return jnp.concatenate(split2(v), axis=0)


def triangle(upper):
    row, column = iota((CHUNK, CHUNK), 0), iota((CHUNK, CHUNK), 1)
    keep = column >= row if upper else column <= row
    return jnp.where(keep, 1.0, 0.0).astype(BF16)


def tri_sum(tri, v):
    return mm(jnp.concatenate([tri] * 3, axis=1), jnp.concatenate(split3(v), axis=0))


def head_params(hp_ref):
    hp = hp_ref[...]
    decay = -jnp.exp(-4.0 + 0.25 * hp[0:1])
    bias = -9.0 + 0.25 * hp[1:2]
    return decay, bias, hp


def sigmoid(v):
    return 1.0 / (1.0 + jnp.exp(-v))


def norm_rows(tok, gain):
    src = tok.astype(F32)
    scale = lax.rsqrt(jnp.mean(src * src, axis=-1, keepdims=True) + EPS)
    return src, scale, (src * scale * gain).astype(BF16)


def pair_masks():
    low = iota((CHUNK, STATE), 1) < HEAD_DIM
    return low, jnp.logical_not(low)


def doubled(v):
    low, high = pair_masks()
    wide = v.astype(F32)
    return jnp.concatenate([jnp.where(low, wide, 0.0).astype(BF16), jnp.where(high, wide, 0.0).astype(BF16)], axis=0)


def product_sum(left, right, cols):
    total = mm(left[0], right[0, :, cols])
    for m in range(1, left.shape[0]):
        total = total + mm(left[m], right[m, :, cols])
    return total


def put_tile(gtile_ref, d, tile, part):
    count = part.shape[0] // UNIT
    gtile_ref[d, pl.ds(tile * count, count)] = part.reshape(count, UNIT, STATE)


def clear_tiles(gtile_ref, rows, tiles):
    low, high = tiles * (rows // UNIT), gtile_ref.shape[1]
    if high > low:
        gtile_ref[:, low:] = jnp.zeros((gtile_ref.shape[0], high - low, UNIT, STATE), BF16)


def weight_tiles(gtile_ref, rows, left, right, count):
    @pl.loop(0, count)
    def _(j):
        part = product_sum(left, right, pl.ds(pl.multiple_of(j * STATE, STATE), STATE)).astype(BF16)
        for d in range(gtile_ref.shape[0]):
            put_tile(gtile_ref, d, j, part[d * rows:(d + 1) * rows])


MESH = pl.DeviceIdType.MESH
PLANE = 4
QUARTER = DIN // PLANE
DMA = pltpu.SemaphoreType.DMA


def places():
    seq = lax.axis_index("seq")
    return lax.axis_index("dp"), seq, lax.rem(seq, PLANE), lax.div(seq, PLANE)


def greet(devices, beside=()):
    barrier = pltpu.get_barrier_semaphore()
    for device in devices:
        pl.semaphore_signal(barrier, inc=1, device_id=device, device_id_type=MESH)
    count = len(devices)
    for there, seq in beside:

        @pl.when(there)
        def _():
            pl.semaphore_signal(barrier, inc=1, device_id=(lax.axis_index("dp"), seq), device_id_type=MESH)
        count = count + jnp.where(there, 1, 0)
    pl.semaphore_wait(barrier, count)


def remote(src, dst, send, recv, device):
    return pltpu.make_async_remote_copy(
        src_ref=src, dst_ref=dst, send_sem=send, recv_sem=recv, device_id=device, device_id_type=MESH)


def open_body(ndp, nseq, win_ref, ws_ref, wout_ref, tok_ref, w_ref, wsall_ref, wo_ref, halo_ref, send, recv, hsend, hrecv):
    dp, seq, _, _ = places()
    nxt, prev = lax.rem(seq + 1, nseq), lax.rem(seq + nseq - 1, nseq)
    others = [lax.rem(dp + d, ndp) for d in range(1, ndp)]
    greet([(o, seq) for o in others] + [(dp, nxt), (dp, prev)])
    T = tok_ref.shape[1]
    width, rows = win_ref.shape[1], wout_ref.shape[0]
    columns = pl.ds(pl.multiple_of(dp * width, width), width)
    own_rows = pl.ds(pl.multiple_of(dp * rows, rows), rows)
    moves = [(ws_ref, wsall_ref.at[:, columns]), (win_ref.at[0:DIN + XBC], w_ref.at[:, columns]), (wout_ref, wo_ref.at[own_rows])]
    copies = [remote(tok_ref.at[:, T - HALO:T], halo_ref, hsend, hrecv, (dp, nxt))]
    for i, o in enumerate(others):
        for k, (src, dst) in enumerate(moves):
            copies.append(remote(src, dst, send.at[i, k], recv.at[i, k], (o, seq)))
    for copy in copies:
        copy.start()
    w_ref[:, columns] = win_ref[0:DIN + XBC]
    wsall_ref[:, columns] = ws_ref[...]
    wo_ref[own_rows] = wout_ref[...]
    for copy in copies:
        copy.wait()


def open_kernel(ndp, nseq, win, ws, wout, tok):
    vmem = pl.BlockSpec(memory_space=pltpu.VMEM)
    M = tok.shape[0]
    shape = lambda *s: jax.ShapeDtypeStruct(s, BF16)
    return pl.pallas_call(
        functools.partial(open_body, ndp, nseq),
        in_specs=[vmem] * 3 + [pl.BlockSpec(memory_space=pl.ANY)],
        out_specs=[vmem] * 4,
        out_shape=[shape(DIN + XBC, D), shape(STATE, D), shape(DIN, D), shape(M, HALO, D)],
        scratch_shapes=[DMA((ndp - 1, 3)), DMA((ndp - 1, 3)), DMA, DMA],
        compiler_params=pltpu.CompilerParams(collective_id=1, has_side_effects=True, vmem_limit_bytes=VMEM_LIMIT),
        name="gather_weights",
    )(win, ws, wout, tok)


SMALL = (("cw", CONV, XBC), ("cb", 1, XBC), ("ng", 1, D), ("og", 1, DIN), ("skip", 1, DIN), ("head", 2, STATE))
SMALL_ROWS = 104


def small_pieces():
    row, found = 0, []
    for index, (_, rows, width) in enumerate(SMALL):
        for r in range(rows):
            for j in range(width // STATE):
                found.append((index, r, j, row))
                row += 1
    return found


def strided(count, body):
    step = max(s for s in range(1, 13) if count % s == 0)

    @pl.loop(0, count // step)
    def _(i):
        body(pl.multiple_of(i * step, step), step)


GROUPS = 4


def units(ndp, nseq, tiles):
    need, step = tiles * (D // ndp // UNIT), GROUPS * nseq
    return -(-need // step) * step


def reducer_scratch(ndp, nseq, count):
    Z = nseq // PLANE
    u = lambda n, *lead: tuple(lead) + (n, UNIT, STATE)
    V = pltpu.VMEM
    pairs = [DMA((GROUPS, ndp - 1))] * 2 + [DMA((GROUPS,))] * 4 + [DMA((GROUPS, Z - 1))] * 4 + [DMA((GROUPS,))] * 4
    return [V(u(count, ndp - 1), BF16), V(u(count // 2), F32), V(u(count // 2), BF16), V(u(count // 2), BF16),
            V(u(count // 4), F32), V(u(count // 4), BF16), V(u(count // 4), BF16), V(u(count // 4), BF16),
            V(u(count // 4 // Z, Z - 1), BF16)] + pairs


class Reducer:
    def __init__(self, ndp, nseq, src, out, scratch):
        self.ndp, self.Z = ndp, nseq // PLANE
        self.src, self.out = src, out
        (self.r0, self.w1, self.st1, self.r1, self.w2, self.st2, self.r2, self.st3, self.r3) = scratch[:9]
        self.sems = [(scratch[9 + 2 * k], scratch[10 + 2 * k]) for k in range(7)]
        self.dp, self.seq, self.p, self.z = places()
        x, y = lax.rem(self.p, 2), lax.div(self.p, 2)
        self.others = [lax.rem(self.dp + d, ndp) for d in range(1, ndp)]
        self.pz = [lax.rem(self.z + d, self.Z) * PLANE + self.p for d in range(1, self.Z)]
        sides = ((x, self.seq + 1 - 2 * x), (y, self.seq + 2 - 4 * y))
        self.sides = [sides if g % 2 == 0 else sides[::-1] for g in range(GROUPS)]
        self.size = src.shape[1] // GROUPS
        self.half, self.quarter = self.size // 2, self.size // 4
        self.piece = self.quarter // self.Z

    def partners(self):
        (_, px), (_, py) = self.sides[0]
        return [(o, self.seq) for o in self.others] + [(self.dp, q) for q in (px, py)] + [(self.dp, q) for q in self.pz]

    def copies(self, stage, g):
        sizes, at = self.size, g * self.size
        o1, o2, o3 = g * self.half, g * self.quarter, g * self.piece
        send, recv = self.sems[stage]
        (b1, peer1), (b2, peer2) = self.sides[g]
        half_at = at + b1 * self.half
        quarter_at = half_at + b2 * self.quarter
        piece_at = quarter_at + self.z * self.piece
        if stage == 0:
            return [remote(self.src.at[o, pl.ds(at, sizes)], self.r0.at[i, pl.ds(at, sizes)], send.at[g, i], recv.at[g, i], (o, self.seq))
                    for i, o in enumerate(self.others)]
        if stage == 1:
            span = pl.ds(o1, self.half)
            return [remote(self.st1.at[span], self.r1.at[span], send.at[g], recv.at[g], (self.dp, peer1))]
        if stage == 2:
            span = pl.ds(o2, self.quarter)
            return [remote(self.st2.at[span], self.r2.at[span], send.at[g], recv.at[g], (self.dp, peer2))]
        if stage == 3:
            return [remote(self.st3.at[pl.ds(o2 + lax.rem(self.z + d, self.Z) * self.piece, self.piece)], self.r3.at[d - 1, pl.ds(o3, self.piece)],
                           send.at[g, d - 1], recv.at[g, d - 1], (self.dp, self.pz[d - 1])) for d in range(1, self.Z)]
        if stage == 4:
            span = pl.ds(piece_at, self.piece)
            return [remote(self.out.at[span], self.out.at[span], send.at[g, d - 1], recv.at[g, d - 1], (self.dp, self.pz[d - 1]))
                    for d in range(1, self.Z)]
        span, peer = (pl.ds(quarter_at, self.quarter), peer2) if stage == 5 else (pl.ds(half_at, self.half), peer1)
        return [remote(self.out.at[span], self.out.at[span], send.at[g], recv.at[g], (self.dp, peer))]

    def stage(self, stage, g):
        if stage > 0:
            for copy in self.copies(stage - 1, g):
                copy.wait_recv()
        if stage == 7:
            return
        (b1, _), (b2, _) = self.sides[g]
        at, o1, o2, o3 = g * self.size, g * self.half, g * self.quarter, g * self.piece
        if stage == 1:
            def total(i, c):
                v = self.src[self.dp, pl.ds(at + i, c)].astype(F32)
                for k in range(self.ndp - 1):
                    v = v + self.r0[k, pl.ds(at + i, c)].astype(F32)
                return v

            def body(i, c):
                self.w1[pl.ds(o1 + i, c)] = total(b1 * self.half + i, c)
                self.st1[pl.ds(o1 + i, c)] = total((1 - b1) * self.half + i, c).astype(BF16)
            strided(self.half, body)
        elif stage == 2:
            def body(i, c):
                keep, give = pl.ds(o1 + b2 * self.quarter + i, c), pl.ds(o1 + (1 - b2) * self.quarter + i, c)
                self.w2[pl.ds(o2 + i, c)] = self.w1[keep] + self.r1[keep].astype(F32)
                self.st2[pl.ds(o2 + i, c)] = (self.w1[give] + self.r1[give].astype(F32)).astype(BF16)
            strided(self.quarter, body)
        elif stage == 3:
            def body(i, c):
                span = pl.ds(o2 + i, c)
                v = self.w2[span] + self.r2[span].astype(F32)
                self.w2[span] = v
                self.st3[span] = v.astype(BF16)
            strided(self.quarter, body)
        elif stage == 4:
            v = self.w2[pl.ds(o2 + self.z * self.piece, self.piece)]
            for d in range(self.Z - 1):
                v = v + self.r3[d, pl.ds(o3, self.piece)].astype(F32)
            self.out[pl.ds(at + b1 * self.half + b2 * self.quarter + self.z * self.piece, self.piece)] = v.astype(BF16)
        for copy in self.copies(stage, g):
            copy.start()

    def ticks(self):
        def tick(k):
            if k == 0:
                for g in range(GROUPS):
                    self.stage(0, g)
                return
            for stage, groups in ((k, (0, 1)), (k - 1, (2, 3))):
                if 1 <= stage <= 7:
                    for g in groups:
                        self.stage(stage, g)
        return [functools.partial(tick, k) for k in range(9)]

    def finish(self):
        for stage in range(7):
            for g in range(GROUPS):
                for copy in self.copies(stage, g):
                    copy.wait_send()


def small_scratch(ndp, nseq):
    Z = nseq // PLANE
    V = pltpu.VMEM
    shape = (SMALL_ROWS, STATE)
    count = ndp - 1 + 2 + Z - 1
    return [V((ndp,) + shape, F32), V((2,) + shape, F32), V((2,) + shape, F32), V((Z,) + shape, F32), DMA((count,)), DMA((count,))]


class SmallReducer:
    def __init__(self, ndp, nseq, out, scratch):
        self.out = out
        self.bufs, (self.send, self.recv) = scratch[:4], scratch[4:6]
        dp, seq, p, z = places()
        Z = nseq // PLANE
        x, y = lax.rem(p, 2), lax.div(p, 2)
        self.z, self.Z = z, Z
        self.peers = [[(lax.rem(dp + d, ndp), seq) for d in range(1, ndp)], [(dp, seq + 1 - 2 * x)], [(dp, seq + 2 - 4 * y)],
                      [(dp, lax.rem(z + d, Z) * PLANE + p) for d in range(1, Z)]]
        self.at, self.begun, self.over, self.started = 0, False, False, []

    def send_all(self):
        buf = self.bufs[self.at]
        base = sum(len(q) for q in self.peers[:self.at])
        self.flying = [remote(buf.at[0], buf.at[1 + k], self.send.at[base + k], self.recv.at[base + k], device)
                       for k, device in enumerate(self.peers[self.at])]
        for copy in self.flying:
            copy.start()
        self.started += self.flying

    def begin(self, groups):
        buf = self.bufs[0]
        buf[0] = jnp.zeros(buf.shape[1:], F32)
        for index, r, j, row in small_pieces():
            v = groups[index][0][r:r + 1, j * STATE:(j + 1) * STATE]
            for other in groups[index][1:]:
                v = v + other[r:r + 1, j * STATE:(j + 1) * STATE]
            buf[0, row:row + 1] = v
        self.begun = True
        self.send_all()

    def advance(self):
        if self.over:
            return
        for copy in self.flying:
            copy.wait_recv()
        buf = self.bufs[self.at]
        if self.at < 3:
            v = buf[0]
            for k in range(1, buf.shape[0]):
                v = v + buf[k]
            self.at += 1
            self.bufs[self.at][0] = v
            self.send_all()
            return
        v = None
        for k in range(self.Z):
            piece = buf[lax.rem(self.z - k + self.Z, self.Z)]
            v = piece if v is None else v + piece
        self.out[...] = v
        self.over = True

    def finish(self):
        for copy in self.started:
            copy.wait_send()


def unpack_body(g1_ref, g2_ref, sm_ref, gin_ref, gout_ref, cw_ref, cb_ref, ng_ref, og_ref, head_ref):
    R = gin_ref.shape[1]
    U = R // UNIT
    tile = lambda ref, j: ref[j * U:(j + 1) * U].astype(F32).reshape(R, STATE)
    eye = jnp.where(iota((STATE, STATE), 0) == iota((STATE, STATE), 1), 1.0, 0.0).astype(BF16)
    turned = lambda ref, j: mm_nt(eye, ref[j * U:(j + 1) * U].reshape(R, STATE))
    for j in range(12):
        gin_ref[j * STATE:(j + 1) * STATE] = turned(g1_ref, j)
    for j in range(14):
        gin_ref[DIN + j * STATE:DIN + (j + 1) * STATE] = turned(g2_ref, j)
    gin_ref[DIN + XBC:] = turned(g2_ref, 14)[:HEADS]
    for half in range(2):
        for j in range(D // STATE):
            gout_ref[half * R:(half + 1) * R, j * STATE:(j + 1) * STATE] = tile(g1_ref, 12 + half * 6 + j)
    outs = {0: cw_ref, 1: cb_ref, 2: ng_ref, 3: og_ref}
    low, high = iota((1, STATE), 1) < HEAD_DIM, iota((1, STATE), 1)
    lane = iota((1, STATE), 1)
    skip = jnp.zeros((1, STATE), F32)
    for index, r, j, row in small_pieces():
        v = sm_ref[row:row + 1]
        if index in outs:
            outs[index][r:r + 1, j * STATE:(j + 1) * STATE] = v
        elif index == 4:
            left = jnp.sum(jnp.where(low, v, 0.0), axis=1, keepdims=True)
            right = jnp.sum(jnp.where(low, 0.0, v), axis=1, keepdims=True)
            skip = skip + jnp.where(lane == 2 * j, left, 0.0) + jnp.where(lane == 2 * j + 1, right, 0.0)
        else:
            head_ref[r + 1:r + 2] = v
    head_ref[0:1] = skip


def unpack(g1, g2, sm, R):
    vmem = pl.BlockSpec(memory_space=pltpu.VMEM)
    sds = lambda *s: jax.ShapeDtypeStruct(s, F32)
    return pl.pallas_call(
        unpack_body,
        in_specs=[vmem] * 3,
        out_specs=[vmem] * 7,
        out_shape=[sds(PROJ, R), sds(2 * R, D), sds(CONV, XBC), sds(1, XBC), sds(1, D), sds(1, DIN), sds(3, STATE)],
        compiler_params=pltpu.CompilerParams(vmem_limit_bytes=VMEM_LIMIT),
        name="unpack_gradients",
    )(g1, g2, sm)
VMEM = pl.BlockSpec(memory_space=pltpu.VMEM)
ANY = pl.BlockSpec(memory_space=pl.ANY)


class Refs:
    pass


def run(name, body, ins, outs, scratch, carried=(), collective_id=None):
    names = list(ins) + list(outs) + list(scratch)
    aliases = {list(ins).index(k): list(outs).index(k) for k in carried}

    def kernel(*refs):
        r = Refs()
        for k, ref in zip(names, refs):
            setattr(r, k, ref)
        body(r)

    params = dict(vmem_limit_bytes=VMEM_LIMIT)
    if collective_id is not None:
        params.update(collective_id=collective_id, has_side_effects=True)
    got = pl.pallas_call(
        kernel,
        in_specs=[s for s, _ in ins.values()],
        out_specs=[s for s, _ in outs.values()],
        out_shape=[s for _, s in outs.values()],
        scratch_shapes=list(scratch.values()),
        input_output_aliases=aliases,
        compiler_params=pltpu.CompilerParams(**params),
        name=name,
    )(*[a for _, a in ins.values()])
    return dict(zip(outs, got))


class Mover:
    def __init__(self, sems):
        self.sems, self.count, self.flying = sems, 0, []

    def start(self, src, dst, late=True):
        copy = pltpu.make_async_copy(src, dst, self.sems.at[self.count])
        self.count += 1
        copy.start()
        if late:
            self.flying.append(copy)
        return copy

    def finish(self):
        for copy in self.flying:
            copy.wait()


def exchange_scratch(nseq):
    V = pltpu.VMEM
    quarter = (STATE, QUARTER)
    return dict(x_out=V((STATE, DIN), KIND), x_got=V((PLANE,) + quarter, KIND), x_tots=V((PLANE, 8, STATE), F32), x_pre=V(quarter, HOP_KIND),
                x_hop=V(quarter, HOP_KIND), x_back=V((PLANE,) + quarter, KIND), x_stage=V((STATE, DIN), KIND),
                x_ts=DMA((3,)), x_tr=DMA((3,)), x_s=DMA((3,)), x_r=DMA((3,)), x_zs=DMA, x_zr=DMA, x_bs=DMA((3,)), x_br=DMA((3,)))


class Exchange:
    def __init__(self, nseq, upward, state, totals, r):
        self.nseq, self.upward, self.state, self.totals, self.r = nseq, upward, state, totals, r
        self.dp, self.seq, self.p, self.z = places()
        self.Z = nseq // PLANE
        self.base = self.z * PLANE
        self.peers = [lax.rem(self.p + d, PLANE) for d in range(PLANE)]
        up, down = lax.rem(self.seq + PLANE, nseq), lax.rem(self.seq + nseq - PLANE, nseq)
        self.greeted = [(self.dp, self.base + q) for q in self.peers[1:]]
        self.beside = ((self.z < self.Z - 1, up), (self.z > 0, down))
        self.towards = down if upward else up
        self.place = self.Z - 1 - self.z if upward else self.z
        self.steps = self.Z + 2
        self.at = 0

    def columns(self, q):
        return pl.ds(pl.multiple_of(q * QUARTER, QUARTER), QUARTER)

    def first(self):
        r = self.r
        source = self.state if r.x_stage.dtype == F32 else r.x_stage
        found = []
        for d in range(1, PLANE):
            to = (self.dp, self.base + self.peers[d])
            found.append(remote(self.totals, r.x_tots.at[d], r.x_ts.at[d - 1], r.x_tr.at[d - 1], to))
            found.append(remote(source.at[:, self.columns(self.peers[d])], r.x_got.at[d], r.x_s.at[d - 1], r.x_r.at[d - 1], to))
        return found

    def link(self):
        r = self.r
        return remote(r.x_hop, r.x_pre, r.x_zs, r.x_zr, (self.dp, self.towards))

    def last(self):
        r = self.r
        return [remote(r.x_back.at[d], r.x_out.at[:, self.columns(self.p)], r.x_bs.at[d - 1], r.x_br.at[d - 1],
                       (self.dp, self.base + lax.rem(self.p + PLANE - d, PLANE))) for d in range(1, PLANE)]

    def begin(self):
        r = self.r
        if r.x_stage.dtype != F32:
            r.x_stage[...] = self.state[...].astype(KIND)
        for copy in self.first():
            copy.start()
        r.x_tots[0] = self.totals[...]
        r.x_got[0] = self.state[:, self.columns(self.p)].astype(KIND)

    def combine(self, k):
        r = self.r
        if k == 0:
            for copy in self.first():
                copy.wait_recv()

        @pl.when(self.place == k)
        def _():
            if k == 0:
                r.x_pre[...] = jnp.zeros_like(r.x_pre)
            else:
                self.link().wait_recv()
            matrix = spread_matrix(self.p * QUARTER, QUARTER)
            order = range(PLANE - 1, -1, -1) if self.upward else range(PLANE)
            total = r.x_pre[...].astype(F32)
            for q in order:
                slot = lax.rem(self.p - q + PLANE, PLANE)
                r.x_back[slot] = total.astype(KIND)
                total = spread(jnp.exp2(r.x_tots[slot]), matrix)[0:1] * total + r.x_got[slot].astype(F32)
            if k < self.Z - 1:
                r.x_hop[...] = total.astype(HOP_KIND)
                self.link().start()
            for copy in self.last():
                copy.start()
            r.x_out[:, self.columns(self.p)] = r.x_back[0]

    def end(self):
        for copy in self.last():
            copy.wait_recv()
        for copy in self.first() + self.last():
            copy.wait_send()

        @pl.when(self.place < self.Z - 1)
        def _():
            self.link().wait_send()

    def step(self, k):
        if k == 0:
            self.begin()
        elif k <= self.Z:
            self.combine(k - 1)
        else:
            self.end()

    def tick(self):
        if self.at < self.steps:
            self.step(self.at)
            self.at += 1

    def finish(self):
        while self.at < self.steps:
            self.tick()


class NoExchange:
    def tick(self):
        pass

    finish = tick


def chunks(T):
    return [(c, slice(c * CHUNK, (c + 1) * CHUNK)) for c in range(T // CHUNK)]


SHARED1 = ("cin", "cout", "bc", "info", "sl", "cum", "chalo")


def k1_body(nseq, m, ahead, r):
    T = r.gate_v.shape[0]
    NC = T // CHUNK
    moves = Mover(r.sems)
    loads = [moves.start(r.tok.at[m], r.tok_v, late=False), moves.start(r.w, r.w_v, late=False)]
    trade = NoExchange()
    if ahead:
        trade = Exchange(nseq, False, r.x_state, r.x_totals, r)
        greet(trade.greeted, trade.beside)
    trade.tick()
    decay, bias, hp = head_params(r.hp)
    decay2 = decay * LOG2E
    gain = r.ng[...]
    first = lax.axis_index("seq") == 0
    r.an[0:HALO] = jnp.where(first, 0.0, norm_rows(r.halo[m], gain)[2].astype(F32)).astype(BF16)
    loads[0].wait()
    r.an[HALO:] = norm_rows(r.tok_v[...], gain)[2]
    arg = mm_nt(r.an[HALO:], r.ws[...]) + bias
    dt = jnp.maximum(arg, 0.0) + jnp.log1p(jnp.exp(-jnp.abs(arg)))
    r.info_v[0] = arg
    r.info_v[1] = dt
    r.dt2[...] = jnp.concatenate(split2(dt), axis=1)
    tri = triangle(False)
    ends = []
    for c, rows in chunks(T):
        lc = tri_sum(tri, dt[rows] * decay2)
        r.info_v[2, rows] = lc
        ends.append(lc[CHUNK - 1:CHUNK])
        r.tw2[rows] = jnp.concatenate(split2(jnp.exp2(lc[CHUNK - 1:CHUNK] - lc)), axis=1)
    before, after = jnp.zeros((1, STATE), F32), jnp.zeros((1, STATE), F32)
    for c in range(NC + 1):
        r.cum_v[0, c:c + 1] = before
        r.cum_v[1, NC - c:NC - c + 1] = after
        if c < NC:
            before, after = before + ends[c], after + ends[NC - 1 - c]
    r.totals[...] = jnp.broadcast_to(before, (8, STATE))
    moves.start(r.info_v, r.info.at[m])
    moves.start(r.cum_v, r.cum.at[m])
    loads[1].wait()

    def conv_tile(j, cols):
        wcols = pl.ds(pl.multiple_of(DIN + j * TILE, TILE), TILE)
        raw = mm_nt(r.an[...], r.w_v[wcols, :])
        r.cpad[...] = raw
        r.cin_v[:, cols] = raw[HALO:]
        r.chalo_v[:, cols] = raw[:HALO]
        out = r.cb[:, cols]
        for k in range(CONV):
            out = out + r.cw[k:k + 1, cols] * r.cpad[HALO - CONV + 1 + k:HALO - CONV + 1 + k + T]
        r.cout_v[:, cols] = out
        return out * sigmoid(out)

    @pl.loop(0, DIN // TILE)
    def _(j):
        cols = pl.ds(pl.multiple_of(j * TILE, TILE), TILE)
        x = conv_tile(j, cols)
        matrix = spread_matrix(j * TILE, TILE)
        ux = x * mm(r.dt2[...], matrix)
        r.u[:, cols] = ux.astype(BF16)
        hi, lo = split2(ux * mm(r.tw2[...], matrix))
        for c, rows in chunks(T):
            r.ub[c, 0:CHUNK, cols] = hi[rows]
            r.ub[c, CHUNK:, cols] = lo[rows]
        skip_tile = spread(jnp.broadcast_to(hp[2:3], (8, STATE)), matrix)[0:1]
        r.ypart_v[:, cols] = x * skip_tile

    r.bc_v[...] = conv_tile(DIN // TILE, pl.ds(DIN, TILE))
    moves.start(r.cin_v, r.cin.at[m])
    moves.start(r.cout_v, r.cout.at[m])
    moves.start(r.chalo_v, r.chalo.at[m])
    moves.start(r.bc_v, r.bc.at[m])
    trade.tick()
    matrix = spread_matrix(0, DIN)
    state = jnp.zeros((STATE, DIN), F32)
    for c, rows in chunks(T):
        b16 = r.bc_v[rows, 0:STATE].astype(BF16)
        r.sl_v[c] = state
        keep = spread(jnp.exp2(jnp.broadcast_to(ends[c], (8, STATE))), matrix)[0:1]
        state = keep * state + mm_tn(jnp.concatenate([b16, b16], axis=0), r.ub[c])
    r.sl_v[NC] = state
    r.sdev[...] = state
    moves.start(r.sl_v, r.sl.at[m])

    @pl.loop(0, DIN // TILE)
    def _(j):
        cols = pl.ds(pl.multiple_of(j * TILE, TILE), TILE)
        r.gate_v[:, cols] = mm_nt(r.an[HALO:], r.w_v[cols, :])
    moves.start(r.gate_v, r.gate)
    trade.tick()

    causal = iota((CHUNK, CHUNK), 0) >= iota((CHUNK, CHUNK), 1)
    for c, rows in chunks(T):
        gram = jnp.where(causal, fine_nt(r.bc_v[rows, STATE:2 * STATE], r.bc_v[rows, 0:STATE]), 0.0)
        lc = r.info_v[2, rows]
        lct = lc.T
        for p in range(HEADS // 2):
            cols = slice(p * STATE, (p + 1) * STATE)
            mixes = []
            for h in (2 * p, 2 * p + 1):
                gap = lc[:, h:h + 1] - lct[h:h + 1, :]
                mixes.append((gram * jnp.exp2(jnp.minimum(gap, 0.0))).astype(BF16))
            r.ypart_v[rows, cols] = r.ypart_v[rows, cols] + mm(jnp.concatenate(mixes, axis=1), doubled(r.u[rows, cols]))
        moves.start(r.ypart_v.at[rows], r.ypart.at[rows])
        trade.tick()
    trade.finish()
    if ahead:
        moves.start(r.x_out, r.starts.at[m - 1])
    moves.finish()


def k1(nseq, m, carried, tok, halo, w, ws, cw, cb, ng, hp, sdev=None, totals=None):
    M, T, _ = tok.shape
    NC = T // CHUNK
    V = pltpu.VMEM
    sds = jax.ShapeDtypeStruct
    ahead = m > 0
    ins = dict(tok=(ANY, tok), w=(ANY, w), halo=(VMEM, halo), ws=(VMEM, ws), cw=(VMEM, cw), cb=(VMEM, cb), ng=(VMEM, ng), hp=(VMEM, hp))
    shapes = dict(cin=(T, XBC), cout=(T, XBC), bc=(T, 2 * STATE), info=(3, T, STATE), sl=(NC + 1, STATE, DIN), cum=(2, NC + 1, STATE),
                  chalo=(HALO, XBC))
    outs = {k: (ANY, sds((M,) + shapes[k], F32)) for k in SHARED1}
    outs.update(gate=(ANY, sds((T, DIN), F32)), ypart=(ANY, sds((T, DIN), F32)), sdev=(VMEM, sds((STATE, DIN), F32)),
                totals=(VMEM, sds((8, STATE), F32)))
    scratch = dict(tok_v=V((T, D), BF16), w_v=V(w.shape, BF16), cpad=V((HALO + T, TILE), F32), an=V((HALO + T, D), BF16), u=V((T, DIN), BF16),
                   ub=V((NC, 2 * CHUNK, DIN), BF16), dt2=V((T, 2 * STATE), BF16), tw2=V((T, 2 * STATE), BF16),
                   gate_v=V((T, DIN), F32), ypart_v=V((T, DIN), F32), sems=DMA((20 + NC,)), **{k + "_v": V(shapes[k], F32) for k in SHARED1})
    if ahead:
        ins.update({k: (ANY, carried[k]) for k in SHARED1}, x_state=(VMEM, sdev), x_totals=(VMEM, totals))
        outs.update(starts=(ANY, sds((M, STATE, DIN), KIND)))
        if m > 1:
            ins.update(starts=(ANY, carried["starts"]))
        scratch.update(exchange_scratch(nseq))
    keep = [k for k in SHARED1 + ("starts",) if k in ins]
    return run("forward_local", functools.partial(k1_body, nseq, m, ahead), ins, outs, scratch, keep, collective_id=1 + m if ahead else None)


SHARED2 = ("mixed", "dgate", "dy", "rows_dot", "gl")


def k2_body(nseq, M, m, kind, r):
    T = r.gate_v.shape[0]
    NC = T // CHUNK
    moves = Mover(r.sems)
    loads = {}
    for k, src in (("start", r.starts_in.at[m]), ("info", r.info.at[m]), ("cum", r.cum.at[m]), ("bc", r.bc.at[m]), ("sl", r.sl.at[m, 0:NC]),
                   ("ypart", r.ypart), ("gate", r.gate), ("tok", r.tok.at[m]), ("wo", r.wo), ("cot", r.cot.at[m])):
        loads[k] = moves.start(src, getattr(r, k + "_v"), late=False)
    upward = kind == "later"
    trade = Exchange(nseq, upward, r.x_state, r.x_totals, r)
    greet(trade.greeted, trade.beside)
    trade.tick()
    matrix = spread_matrix(0, DIN)
    gather = gather_matrix()
    loads["tok"].wait()
    r.norm_t[...] = norm_rows(r.tok_v[...], r.ng[...])[2].T
    loads["cot"].wait()
    loads["wo"].wait()

    @pl.loop(0, DIN // TILE)
    def _(j):
        cols = pl.ds(pl.multiple_of(j * TILE, TILE), TILE)
        r.dbr[:, cols] = mm_nt(r.cot_v[...], r.wo_v[cols, :])

    for k in ("start", "info", "cum", "bc", "sl", "ypart", "gate"):
        loads[k].wait()
    trade.tick()
    for c, rows in chunks(T):
        keep = spread(jnp.exp2(jnp.broadcast_to(r.cum_v[0, c:c + 1], (8, STATE))), matrix)[0:1]
        state = halves(r.sl_v[c] + keep * r.start_v[...].astype(F32))
        c16 = r.bc_v[rows, STATE:2 * STATE].astype(BF16)
        lift = spread(jnp.exp2(r.info_v[2, rows]), matrix)
        yc = r.ypart_v[rows] + lift * mm(jnp.concatenate([c16, c16], axis=1), state)
        r.ypart_v[rows] = yc
        g = r.gate_v[rows]
        gated = yc * (g * sigmoid(g))
        scale = lax.rsqrt(jnp.mean(gated * gated, axis=-1, keepdims=True) + EPS)
        r.oscale[rows] = jnp.broadcast_to(scale, (CHUNK, STATE))
        r.branch[rows] = (gated * scale * r.og[...]).astype(BF16)
        if c % 2 == 1:
            trade.tick()
    r.branch_t[...] = r.branch[...].T
    for j in range(D // TILE):
        cols = slice(j * TILE, (j + 1) * TILE)
        r.mixed_v[:, cols] = (r.tok_v[:, cols].astype(F32) + mm(r.branch[...], r.wo_v[:, cols])).astype(BF16)
    moves.start(r.mixed_v, r.mixed.at[m])
    trade.tick()
    r.ogr[...] = jnp.zeros_like(r.ogr)
    r.gdev[...] = jnp.zeros_like(r.gdev)
    for c, rows in reversed(chunks(T)):
        g = r.gate_v[rows]
        yc = r.ypart_v[rows]
        db = r.dbr[rows]
        scale = r.oscale[rows][:, 0:1]
        sig = sigmoid(g)
        act = g * sig
        gated = yc * act
        unit = gated * scale
        r.ogr[...] += jnp.sum(db * unit, axis=0, keepdims=True)
        e = db * r.og[...]
        mean = jnp.mean(e * unit, axis=-1, keepdims=True)
        dgated = scale * (e - unit * mean)
        r.dgate_v[rows] = (dgated * yc * (sig * (1.0 + g * (1.0 - sig)))).astype(BF16)
        high, low = split2(dgated * act)
        dyf = high.astype(F32) + low.astype(F32)
        r.dy_v[rows] = dyf
        r.rows_dot_v[rows] = head_sums(dyf * yc, gather)
        lc = r.info_v[2, rows]
        lifted = halves(dyf * spread(jnp.exp2(lc), matrix))
        c16 = r.bc_v[rows, STATE:2 * STATE].astype(BF16)
        r.gl_v[c] = r.gdev[...]
        keep = spread(jnp.exp2(jnp.broadcast_to(lc[CHUNK - 1:CHUNK], (8, STATE))), matrix)[0:1]
        r.gdev[...] = keep * r.gdev[...] + mm_tn(jnp.concatenate([c16, c16], axis=0), lifted)
        moves.start(r.dy_v.at[rows], r.dy.at[m, rows])
        moves.start(r.gl_v.at[c], r.gl.at[m, c])
        trade.tick()
    moves.start(r.dgate_v, r.dgate.at[m])
    moves.start(r.rows_dot_v, r.rows_dot.at[m])
    if m == M - 1:
        early_grads(r)
    trade.finish()
    if upward:
        moves.start(r.x_out, r.laters.at[m - 1])
    else:
        moves.start(r.x_out, r.starts.at[M - 1])
    moves.finish()


def early_grads(r):
    dp = r.g1.shape[0]
    rows = D // dp
    r.extra.finish()
    clear_tiles(r.g1, rows, 24)

    def summed(lefts, rights, cols):
        total = None
        for left, right in zip(lefts, rights):
            part = mm(left[...], right[:, cols])
            total = part if total is None else total + part
        return total.astype(BF16)

    @pl.loop(0, DIN // TILE)
    def _(j):
        part = summed(r.norm_ts + [r.norm_t], r.dgates + [r.dgate_v], pl.ds(pl.multiple_of(j * TILE, TILE), TILE))
        for d in range(dp):
            for k in range(TILE // STATE):
                put_tile(r.g1, d, j * (TILE // STATE) + k, part[d * rows:(d + 1) * rows, k * STATE:(k + 1) * STATE])

    @pl.loop(0, D // TILE)
    def _(j):
        part = summed(r.branch_ts + [r.branch_t], r.cots + [r.cot_v], pl.ds(pl.multiple_of(j * TILE, TILE), TILE))
        for d in range(dp):
            for half in range(2):
                low = (2 * d + half) * rows
                for k in range(TILE // STATE):
                    put_tile(r.g1, d, 12 + half * 6 + j * (TILE // STATE) + k, part[low:low + rows, k * STATE:(k + 1) * STATE])


def k2(ndp, nseq, m, one, before, tok, cot, ng, og, wo, state, totals, count):
    M, T, _ = tok.shape
    NC = T // CHUNK
    V = pltpu.VMEM
    sds = jax.ShapeDtypeStruct
    kind = "earlier" if m == 0 else "later"
    ins = dict(tok=(ANY, tok), cot=(ANY, cot), wo=(ANY, wo), ng=(VMEM, ng), og=(VMEM, og), info=(ANY, one["info"]), cum=(ANY, one["cum"]),
               bc=(ANY, one["bc"]), sl=(ANY, one["sl"]), ypart=(ANY, one["ypart"]), gate=(ANY, one["gate"]),
               x_state=(VMEM, state), x_totals=(VMEM, totals))
    shapes = dict(mixed=((T, D), BF16), dgate=((T, DIN), BF16), dy=((T, DIN), F32), rows_dot=((T, STATE), F32), gl=((NC, STATE, DIN), F32))
    outs = {k: (ANY, sds((M,) + s, t)) for k, (s, t) in shapes.items()}
    outs.update(gdev=(VMEM, sds((STATE, DIN), F32)), ogr=(VMEM, sds((1, DIN), F32)))
    scratch = dict(tok_v=V((T, D), BF16), cot_v=V((T, D), BF16), wo_v=V(wo.shape, BF16), info_v=V((3, T, STATE), F32), cum_v=V((2, NC + 1, STATE), F32),
                   bc_v=V((T, 2 * STATE), F32), sl_v=V((NC, STATE, DIN), F32), ypart_v=V((T, DIN), F32), gate_v=V((T, DIN), F32),
                   start_v=V((STATE, DIN), KIND), dbr=V((T, DIN), F32), branch=V((T, DIN), BF16), oscale=V((T, STATE), F32),
                   sems=DMA((20 + 2 * NC,)), **{k + "_v": V(s, t) for k, (s, t) in shapes.items()})
    scratch.update(exchange_scratch(nseq))
    last = m == M - 1
    turned = dict(branch_t=sds((DIN, T), BF16), norm_t=sds((D, T), BF16))
    if last:
        scratch.update({k: V(s.shape, s.dtype) for k, s in turned.items()})
        outs.update(g1=(VMEM, sds((ndp, count, UNIT, STATE), BF16)))
        for i, b in enumerate(before):
            for k in turned:
                ins[k + str(i)] = (VMEM, b[k])
            scratch["dgate_e%d" % i] = V((T, DIN), BF16)
            scratch["cot_e%d" % i] = V((T, D), BF16)
    else:
        outs.update({k: (VMEM, s) for k, s in turned.items()})
    keep = []
    if m == 0:
        ins.update(starts=(ANY, one["starts"]))
        outs.update(starts=(ANY, sds(one["starts"].shape, KIND)))
        keep += ["starts"]
    else:
        ins.update({k: (ANY, before[-1][k]) for k in SHARED2}, starts_in=(ANY, one["starts"]))
        outs.update(laters=(ANY, sds((M, STATE, DIN), KIND)))
        keep += list(SHARED2)
        if m > 1:
            ins.update(laters=(ANY, before[-1]["laters"]))
            keep += ["laters"]

    def body(r):
        if m == 0:
            r.starts_in = r.starts
        if last:
            named = lambda k: [getattr(r, k + str(i)) for i in range(len(before))]
            r.norm_ts, r.branch_ts, r.dgates, r.cots = named("norm_t"), named("branch_t"), named("dgate_e"), named("cot_e")
            extra = Mover(r.esems)
            copies = []
            for i in range(len(before)):
                copies += [extra.start(r.dgate.at[i], r.dgates[i]), extra.start(r.cot.at[i], r.cots[i])]
            r.extra = extra
        k2_body(nseq, M, m, kind, r)

    if last:
        scratch.update(esems=DMA((2 * M,)))
    return run("gate_and_out", body, ins, outs, scratch, keep, collective_id=1 + M + m)
def k3_body(ndp, nseq, micros, parts, hp_ref, cw_ref, chalo_ref, cum_ref, cin_ref, cout_ref, bc_ref, info_ref, sl_ref, sl_next_ref, start_ref, dy_ref, r_ref,
            gl_ref, later_ref, g1_ref, x_state, x_totals,
            dcin_ref, tail_ref, head_ref, dstep_ref, gcw_ref, gcb_ref, gskip_ref, ghead_ref, sum1_ref,
            dconv, w, xdu, ub, dyl, dgt, dt_x, tail_x, bg, later_v, landing, *rest):
    m, i = pl.program_id(0), pl.program_id(1)
    NC = pl.num_programs(1)
    c = NC - 1 - i
    step = m * NC + i
    steps = pl.num_programs(0) * NC
    traded = exchange_scratch(nseq)
    r = Refs()
    for name, ref in zip(traded, rest):
        setattr(r, name, ref)
    trade = Exchange(nseq, True, x_state, x_totals, r)
    reducer = Reducer(ndp, nseq, g1_ref, landing, rest[len(traded):])
    ticks = reducer.ticks()
    M, own_steps = micros, (micros - 1) * parts
    turns = {}
    for k in range(trade.steps):
        turns.setdefault(min(k * 2 * own_steps // (trade.steps - 1), 2 * own_steps), []).append(k)

    def traded_at(turn):
        if turn in turns:

            @pl.when(step == turn // 2)
            def _():
                for k in turns[turn]:
                    trade.step(k)

    @pl.when(step == 0)
    def _():
        greet(reducer.partners() + trade.greeted, trade.beside)

    for turn in range(0, 2 * own_steps + 1, 2):
        traded_at(turn)
    for k, tick in enumerate(ticks[:-1]):

        @pl.when(step == k)
        def _():
            tick()

    @pl.when(jnp.logical_and(i == 0, m < M - 1))
    def _():
        later_v[...] = later_ref[0]

    @pl.when(jnp.logical_and(i == 0, m == M - 1))
    def _():
        later_v[...] = r.x_out[...]

    decay, _, hp = head_params(hp_ref)
    matrix = spread_matrix(0, DIN)
    gather = gather_matrix()
    skip = spread(jnp.broadcast_to(hp[2:3], (8, STATE)), matrix)[0:1]

    @pl.when(step == 0)
    def _():
        gcw_ref[...] = jnp.zeros_like(gcw_ref)
        gcb_ref[...] = jnp.zeros_like(gcb_ref)
        gskip_ref[...] = jnp.zeros_like(gskip_ref)
        ghead_ref[...] = jnp.zeros_like(ghead_ref)

    @pl.when(i == 0)
    def _():
        dconv[CHUNK:] = jnp.zeros((8, XBC), F32)

    @pl.when(i > 0)
    def _():
        dconv[CHUNK:] = dconv[0:8]

    tri_up = triangle(True)
    b32 = bc_ref[0, :, 0:STATE]
    c32 = bc_ref[0, :, STATE:2 * STATE]
    keeps_st = iota((CHUNK, CHUNK), 0) <= iota((CHUNK, CHUNK), 1)
    gram_t = jnp.where(keeps_st, fine_nt(c32, b32).T, 0.0)
    b, cc = b32.astype(BF16), c32.astype(BF16)
    lc = info_ref[0, 2]
    lct = lc.T
    dt = info_ref[0, 1]
    dt_x[...] = spread(dt, matrix)
    tail_x[...] = spread(jnp.exp2(lc[CHUNK - 1:CHUNK] - lc), matrix)
    dyl[...] = (dy_ref[0] * spread(jnp.exp2(lc), matrix)).astype(BF16)
    wide8 = lambda v: spread(jnp.exp2(jnp.broadcast_to(v, (8, STATE))), matrix)[0:1]
    gc = gl_ref[0, 0] + wide8(cum_ref[0, 1, pl.ds(c + 1, 1)]) * later_v[...].astype(F32)
    s_in = sl_ref[0, 0] + wide8(cum_ref[0, 0, pl.ds(c, 1)]) * start_ref[0].astype(F32)
    s_out = sl_next_ref[0, 0] + wide8(cum_ref[0, 0, pl.ds(c + 1, 1)]) * start_ref[0].astype(F32)
    gc2 = halves(gc)
    gcb16 = gc2[0:STATE]
    bnd = head_sums(jnp.broadcast_to(jnp.sum(gc * s_out, axis=0, keepdims=True), (8, DIN)), gather)[0:1]
    bg[...] = mm(jnp.concatenate([b, b], axis=1), gc2)
    dgt[...] = jnp.zeros((CHUNK, CHUNK), F32)
    for p in range(HEADS // 2):
        cols = slice(p * STATE, (p + 1) * STATE)
        v = cout_ref[0, :, cols]
        sig = sigmoid(v)
        x = v * sig
        dtx, tlx = dt_x[:, cols], tail_x[:, cols]
        ux = x * dtx
        u16 = ux.astype(BF16)
        ub[:, cols] = (ux * tlx).astype(BF16)
        dyf = dy_ref[0, :, cols]
        dy_high, dy_low = split2(dyf)
        dy2 = doubled(dy_high)
        decays, mixes = [], []
        for h in (2 * p, 2 * p + 1):
            gap = lct[h:h + 1, :] - lc[:, h:h + 1]
            e = jnp.exp2(jnp.minimum(gap, 0.0))
            decays.append(e)
            mixes.append((gram_t * e).astype(BF16))
        mix = jnp.concatenate(mixes, axis=1)
        du = mm(mix, dy2) + mm(mix, doubled(dy_low))
        dmix = mm_nt(u16, dy2)
        dgt[...] = dgt[...] + (dmix[:, :CHUNK] * decays[0] + dmix[:, CHUNK:] * decays[1])
        du_state = tlx * bg[:, cols]
        sk = skip[:, cols]
        dyx = dyf * x
        gskip_ref[:, cols] = gskip_ref[:, cols] + jnp.sum(dyx, axis=0, keepdims=True)
        w[:, cols] = dyx * sk + u16.astype(F32) * du + ux * du_state
        du = du + du_state
        xdu[:, cols] = x * du
        dx = dtx * du + sk * dyf
        dconv[0:CHUNK, cols] = dx * (sig * (1.0 + v * (1.0 - sig)))
    dg16 = jnp.where(keeps_st, dgt[...], 0.0).astype(BF16)
    db = mm(dg16, cc) + mm_nt(ub[...], gcb16)
    dc = mm_tn(dg16, b) + mm_nt(dyl[...], s_in.astype(BF16))
    v = cout_ref[0, :, DIN:XBC]
    sig = sigmoid(v)
    dconv[0:CHUNK, DIN:XBC] = jnp.concatenate([db, dc], axis=1) * (sig * (1.0 + v * (1.0 - sig)))
    dl = r_ref[0] - head_sums(w[...], gather)
    da = bnd + tri_sum(tri_up, dl)
    d_dt = head_sums(xdu[...], gather, 2) + da * decay
    dstep = d_dt * sigmoid(info_ref[0, 0])
    dstep_ref[0] = dstep.astype(BF16)
    ghead_ref[0:1] = ghead_ref[0:1] + decay * jnp.sum(da * dt, axis=0, keepdims=True)
    ghead_ref[1:2] = ghead_ref[1:2] + jnp.sum(dstep, axis=0, keepdims=True)

    @pl.loop(0, XBC // TILE)
    def _(j):
        cols = pl.ds(pl.multiple_of(j * TILE, TILE), TILE)
        gcb_ref[:, cols] = gcb_ref[:, cols] + jnp.sum(dconv[0:CHUNK, cols], axis=0, keepdims=True)
        own = cin_ref[0, :, cols]
        total = None
        for k in range(CONV):
            ahead = dconv[CONV - 1 - k:CONV - 1 - k + CHUNK, cols]
            gcw_ref[k:k + 1, cols] = gcw_ref[k:k + 1, cols] + jnp.sum(own * ahead, axis=0, keepdims=True)
            term = cw_ref[k:k + 1, cols] * ahead
            total = term if total is None else total + term
        dcin_ref[0, :, cols] = total.astype(BF16)

        @pl.when(i == 0)
        def _():
            tail_ref[0, :, cols] = total[CHUNK - HALO:]

    @pl.when(i == NC - 1)
    def _():
        head_ref[0] = dconv[0:8]
        for k in range(CONV - 1):
            for n in range(CONV - 1 - k):
                low = HALO - CONV + 1 + k + n
                gcw_ref[k:k + 1] = gcw_ref[k:k + 1] + chalo_ref[0, low:low + 1] * dconv[n:n + 1]

    for turn in range(1, 2 * own_steps, 2):
        traded_at(turn)

    @pl.when(step == steps - 1)
    def _():
        for tick in ticks[-1:]:
            tick()
        reducer.finish()

        def body(at, c):
            sum1_ref[pl.ds(at, c)] = landing[pl.ds(at, c)]
        strided(landing.shape[0], body)


def k3(ndp, nseq, hp, cw, chalo, cum, cin, cout, bc, info, sl, start, dy, r, gl, later, g1, x_state, x_totals):
    M, T, _ = cout.shape
    NC = T // CHUNK
    at = lambda m, i: NC - 1 - i
    const = lambda a: (pl.BlockSpec(a.shape, lambda m, i: (0,) * a.ndim), a)
    micro = lambda a: (pl.BlockSpec((1,) + a.shape[1:], lambda m, i: (m,) + (0,) * (a.ndim - 1)), a)
    chunk = lambda a: (pl.BlockSpec((1, CHUNK) + a.shape[2:], lambda m, i: (m, at(m, i), 0)), a)
    entry = lambda a, ahead: (pl.BlockSpec((1, 1) + a.shape[2:], lambda m, i: (m, at(m, i) + ahead, 0, 0)), a)
    inner = (pl.BlockSpec((1, 3, CHUNK, STATE), lambda m, i: (m, 0, at(m, i), 0)), info)
    sds = jax.ShapeDtypeStruct
    C = lambda width, dt: (pl.BlockSpec((1, CHUNK, width), lambda m, i: (m, at(m, i), 0)), sds((M, T, width), dt))
    S = lambda rows: (pl.BlockSpec((1, rows, XBC), lambda m, i: (m, 0, 0)), sds((M, rows, XBC), F32))
    W = lambda shape, dt: (pl.BlockSpec(shape, lambda m, i: (0,) * len(shape)), sds(shape, dt))
    V = pltpu.VMEM
    ins = [const(hp), const(cw), micro(chalo), micro(cum), chunk(cin), chunk(cout), chunk(bc), inner, entry(sl, 0), entry(sl, 1), micro(start),
           chunk(dy), chunk(r), entry(gl, 0), micro(later), const(g1), const(x_state), const(x_totals)]
    outs = [C(XBC, BF16), S(HALO), S(8), C(STATE, BF16), W((CONV, XBC), F32), W((1, XBC), F32), W((1, DIN), F32), W((2, STATE), F32),
            W(g1.shape[1:], BF16)]
    return pl.pallas_call(
        functools.partial(k3_body, ndp, nseq, M, NC),
        grid=(M, NC),
        in_specs=[b for b, _ in ins],
        out_specs=[b for b, _ in outs],
        out_shape=[o for _, o in outs],
        scratch_shapes=[V((CHUNK + 8, XBC), F32), V((CHUNK, DIN), F32), V((CHUNK, DIN), F32), V((CHUNK, DIN), BF16), V((CHUNK, DIN), BF16),
                        V((CHUNK, CHUNK), F32), V((CHUNK, DIN), F32), V((CHUNK, DIN), F32), V((CHUNK, DIN), F32), V((STATE, DIN), KIND), V(g1.shape[1:], BF16)] + list(exchange_scratch(nseq).values()) + reducer_scratch(ndp, nseq, g1.shape[1]),
        compiler_params=pltpu.CompilerParams(vmem_limit_bytes=VMEM_LIMIT, dimension_semantics=("arbitrary",) * 2, collective_id=10,
                                             has_side_effects=True),
        name="scan_backward",
    )(*[a for _, a in ins])


def k4_body(ndp, nseq, M, tok_ref, cot_ref, ng_ref, w_ref, ws_ref, cw_ref, dgate_ref, dcin_ref, dstep_ref, tail_ref, head_ref, *refs):
    smalls, rest = refs[:4 + M], refs[4 + M:]
    gtok_ref, sum2_ref, small_out, g2, nxt, dc, norm_t, ngr, hsem, hrsem = rest[:10]
    count = len(reducer_scratch(ndp, nseq, g2.shape[1]))
    reducer = Reducer(ndp, nseq, g2, sum2_ref, rest[10:10 + count])
    tiny = SmallReducer(ndp, nseq, small_out, rest[10 + count:])
    T = tok_ref.shape[1]
    dp, seq, _, _ = places()
    following, prev = lax.rem(seq + 1, nseq), lax.rem(seq + nseq - 1, nseq)
    greet(reducer.partners() + [(dp, following), (dp, prev)])
    halo = remote(head_ref, nxt, hsem, hrsem, (dp, prev))
    halo.start()
    rows = D // ndp
    for m in range(M):
        norm_t[m] = norm_rows(tok_ref[m], ng_ref[...])[2].T
        dc[m, 0:T - HALO, 0:XBC] = dcin_ref[m, 0:T - HALO]
        dc[m, :, XBC:] = dstep_ref[m]
    clear_tiles(g2, rows, 15)
    halo.wait()
    last = seq == nseq - 1
    row = iota((HALO, XBC), 0)
    for m in range(M):
        tail = tail_ref[m]
        for s in range(CONV - 1):
            extra = jnp.zeros((1, XBC), F32)
            for k in range(s + 1):
                extra = extra + cw_ref[k:k + 1] * nxt[m, s - k:s - k + 1]
            tail = tail + jnp.where(jnp.logical_and(row == HALO - CONV + 1 + s, jnp.logical_not(last)), extra, 0.0)
        dc[m, T - HALO:T, 0:XBC] = tail.astype(BF16)
    weight_tiles(g2, rows, norm_t, dc, 15)
    ngr[...] = jnp.zeros_like(ngr)
    ticks = reducer.ticks()

    def backward(m, part):
        if part < D // TILE:
            cols = slice(part * TILE, (part + 1) * TILE)
            dn[:, cols] = (mm(dgate_ref[m], w_ref[0:DIN, cols]) + mm(dc[m, :, 0:XBC], w_ref[DIN:DIN + XBC, cols])
                           + mm(dstep_ref[m], ws_ref[:, cols]))
        else:
            src, scale, _ = norm_rows(tok_ref[m], ng_ref[...])
            unit = src * scale
            d_normed = dn[...]
            ngr[...] += jnp.sum(d_normed * unit, axis=0, keepdims=True)
            f = d_normed * ng_ref[...]
            mean = jnp.mean(f * unit, axis=-1, keepdims=True)
            gtok_ref[m] = (cot_ref[m].astype(F32) + scale * (f - unit * mean)).astype(BF16)

    dn = rest[-1]
    parts = [(m, part) for m in range(M) for part in range(D // TILE + 1)]
    per = -(-len(parts) // (len(ticks) - 2))
    ticks[0]()
    for k, tick in enumerate(ticks[1:]):
        for m, part in parts[:per]:
            backward(m, part)
        parts = parts[per:]
        tick()
        if not parts and not tiny.begun:
            tiny.begin([[r[...] for r in group] for group in small_groups(smalls, ngr, M)])
        elif tiny.begun:
            tiny.advance()
    while not tiny.over:
        tiny.advance()
    tiny.finish()
    reducer.finish()


def small_groups(smalls, ngr, M):
    gcw, gcb, gskip, ghead = smalls[:4]
    return [[gcw], [gcb], [ngr], list(smalls[4:4 + M]), [gskip], [ghead]]


def k4(ndp, nseq, tok, cot, ng, w, ws, cw, dgate, dcin, dstep, tail, head, gcw, gcb, gskip, ghead, ogrs):
    M, T, _ = tok.shape
    V = pltpu.VMEM
    sds = jax.ShapeDtypeStruct
    vmem = pl.BlockSpec(memory_space=pltpu.VMEM)
    count = units(ndp, nseq, 15)
    args = (tok, cot, ng, w, ws, cw, dgate, dcin, dstep, tail, head, gcw, gcb, gskip, ghead, *ogrs)
    return pl.pallas_call(
        functools.partial(k4_body, ndp, nseq, M),
        in_specs=[vmem] * len(args),
        out_specs=[vmem] * 3,
        out_shape=[sds((M, T, D), BF16), sds((count, UNIT, STATE), BF16), sds((SMALL_ROWS, STATE), F32)],
        scratch_shapes=[V((ndp, count, UNIT, STATE), BF16), V(head.shape, F32), V((M, T, XBC + STATE), BF16), V((M, D, T), BF16), V((1, D), F32),
                        DMA, DMA] + reducer_scratch(ndp, nseq, count) + small_scratch(ndp, nseq) + [V((T, D), F32)],
        compiler_params=pltpu.CompilerParams(collective_id=11, has_side_effects=True, vmem_limit_bytes=VMEM_LIMIT),
        name="projection_backward",
    )(*args)


def per_device(ndp, nseq, tokens, in_weight, out_weight, conv_weight, conv_bias, norm_gain, out_gain, skip_gain, rate_code, step_code, cotangent):
    micro, groups, T, _ = tokens.shape
    M = micro * groups
    tok = tokens.reshape(M, T, D)
    cot = cotangent.reshape(M, T, D)
    seq = lax.axis_index("seq")
    turned = in_weight.T
    steps = jnp.pad(turned[DIN + XBC:], ((0, STATE - HEADS), (0, 0)))
    if in_weight.shape[0] % STATE == 0:
        w, ws, wo, halo = open_kernel(ndp, nseq, turned, steps, out_weight, tok)
    else:
        w, ws, wo = [lax.all_gather(v, "dp", axis=at, tiled=True) for v, at in ((turned[:DIN + XBC], 1), (steps, 1), (out_weight, 0))]
        halo = lax.ppermute(tok[:, T - HALO:], "seq", [(i, i + 1) for i in range(nseq - 1)])
    pad = lambda v: jnp.pad(v.astype(F32), (0, STATE - HEADS))
    hp = jnp.stack([pad(rate_code), pad(step_code), pad(skip_gain)])
    ng, og, cb = norm_gain[None], out_gain[None], conv_bias[None]
    first, second = [], []
    for m in range(M):
        last = first[-1] if first else {}
        first.append(k1(nseq, m, last, tok, halo, w, ws, conv_weight, cb, ng, hp, last.get("sdev"), last.get("totals")))
    shared = {k: first[-1][k] for k in SHARED1}
    starts = first[-1]["starts"]
    for m in range(M):
        one = dict(shared, gate=first[m]["gate"], ypart=first[m]["ypart"], starts=starts)
        traded = (first[-1]["sdev"], first[-1]["totals"]) if m == 0 else (second[-1]["gdev"], first[m - 1]["totals"])
        second.append(k2(ndp, nseq, m, one, second, tok, cot, ng, og, wo, *traded, units(ndp, nseq, 24)))
        starts = second[0]["starts"]
    s = dict(shared, starts=starts, laters=second[-1]["laters"], g1=second[-1]["g1"], **{k: second[-1][k] for k in SHARED2})
    dcin, tail, head, dstep, gcw, gcb, gskip, ghead, sum1 = k3(
        ndp, nseq, hp, conv_weight, s["chalo"], s["cum"], s["cin"], s["cout"], s["bc"], s["info"], s["sl"], s["starts"], s["dy"],
        s["rows_dot"], s["gl"], s["laters"], s["g1"], second[-1]["gdev"], first[-1]["totals"])
    mixed = s["mixed"]
    gtok, sum2, sm = k4(ndp, nseq, tok, cot, ng, w, ws, conv_weight, s["dgate"], dcin, dstep, tail, head, gcw, gcb, gskip, ghead,
                        [b["ogr"] for b in second])
    g_in, g_out, cwg, cbg, ngg, ogg, heads = unpack(sum1, sum2, sm, D // ndp)
    return (mixed.reshape(tokens.shape), gtok.reshape(tokens.shape), g_in.T, g_out, cwg, cbg[0], ngg[0], ogg[0],
            heads[0, :HEADS], heads[1, :HEADS], heads[2, :HEADS])


def solution(mesh):
    rows, split = P("dp", None), P(None, "dp", "seq", None)
    return jax.shard_map(
        functools.partial(per_device, mesh.shape["dp"], mesh.shape["seq"]),
        mesh=mesh,
        in_specs=(split, rows, rows) + (P(),) * 7 + (split,),
        out_specs=(split, split, rows, rows) + (P(),) * 7,
        check_vma=False,
    )
```

```python
import functools

import jax
import jax.numpy as jnp
from jax import lax
from jax.experimental import pallas as pl
from jax.experimental.pallas import tpu as pltpu
from jax.sharding import PartitionSpec as P

D = 768
DIN = 1536
HEADS = 24
HEAD_DIM = 64
STATE = 128
CONV = 4
XBC = 1792
PROJ = 3352
EPS = 1e-05
LOG2E = 1.4426950408889634
CHUNK = 128
TILE = 256
HALO = 16
UNIT = 16
KIND = jnp.float32
HOP_KIND = jnp.bfloat16
F32 = jnp.float32
BF16 = jnp.bfloat16
VMEM_LIMIT = 62 * 1024 * 1024


def mm(a, b):
    return lax.dot_general(a, b, (((1,), (0,)), ((), ())), preferred_element_type=F32)


def mm_nt(a, b):
    return lax.dot_general(a, b, (((1,), (1,)), ((), ())), preferred_element_type=F32)


def mm_tn(a, b):
    return lax.dot_general(a, b, (((0,), (0,)), ((), ())), preferred_element_type=F32)


def split2(v):
    hi = v.astype(BF16)
    return hi, (v - hi.astype(F32)).astype(BF16)


def split3(v):
    hi = v.astype(BF16)
    rest = v - hi.astype(F32)
    mid = rest.astype(BF16)
    return hi, mid, (rest - mid.astype(F32)).astype(BF16)


def iota(shape, dim):
    return lax.broadcasted_iota(jnp.int32, shape, dim)


def spread_matrix(start, width):
    head = iota((2 * STATE, width), 0) & (STATE - 1)
    column = (iota((2 * STATE, width), 1) + start) >> 6
    return jnp.where(head == column, 1.0, 0.0).astype(BF16)


def gather_matrix():
    return jnp.where((iota((DIN, STATE), 0) >> 6) == iota((DIN, STATE), 1), 1.0, 0.0).astype(BF16)


def spread(v, matrix):
    return mm(jnp.concatenate(split2(v), axis=1), matrix)


def head_sums(v, matrix, parts=3):
    pieces = split3(v) if parts == 3 else split2(v)
    total = mm(pieces[0], matrix)
    for piece in pieces[1:]:
        total = total + mm(piece, matrix)
    return total


def fine_nt(a, b):
    ah, al = split2(a)
    bh, bl = split2(b)
    return mm_nt(jnp.concatenate([ah, ah, al], axis=1), jnp.concatenate([bh, bl, bh], axis=1))


def halves(v):
    return jnp.concatenate(split2(v), axis=0)


def triangle(upper):
    row, column = iota((CHUNK, CHUNK), 0), iota((CHUNK, CHUNK), 1)
    keep = column >= row if upper else column <= row
    return jnp.where(keep, 1.0, 0.0).astype(BF16)


def tri_sum(tri, v):
    return mm(jnp.concatenate([tri] * 3, axis=1), jnp.concatenate(split3(v), axis=0))


PARAMS = {"ng": (0, D), "og": (6, DIN), "cb": (18, XBC), "head": (32, 3 * STATE)}


def param(ref, name):
    row, width = PARAMS[name]
    return jnp.concatenate([ref[row + i:row + i + 1] for i in range(width // STATE)], axis=1)


def head_params(params_ref):
    row = PARAMS["head"][0]
    hp = params_ref[row:row + 3]
    decay = -jnp.exp(-4.0 + 0.25 * hp[0:1])
    bias = -9.0 + 0.25 * hp[1:2]
    return decay, bias, hp


def sigmoid(v):
    return 0.5 * jnp.tanh(0.5 * v) + 0.5


def norm_rows(tok, gain):
    src = tok.astype(F32)
    scale = lax.rsqrt(jnp.mean(src * src, axis=-1, keepdims=True) + EPS)
    return src, scale, (src * scale * gain).astype(BF16)


def doubled(v):
    low = jnp.where(iota((1, STATE), 1) < HEAD_DIM, 1.0, 0.0)
    return jnp.concatenate([v * low.astype(BF16), v * (1.0 - low).astype(BF16)], axis=0)


def product_sum(left, right, cols):
    total = mm(left[0], right[0, :, cols])
    for m in range(1, left.shape[0]):
        total = total + mm(left[m], right[m, :, cols])
    return total


def put_tile(gtile_ref, d, tile, part):
    count = part.shape[0] // UNIT
    gtile_ref[d, pl.ds(tile * count, count)] = part.reshape(count, UNIT, STATE)


def clear_tiles(gtile_ref, rows, tiles):
    low, high = tiles * (rows // UNIT), gtile_ref.shape[1]
    if high > low:
        gtile_ref[:, low:] = jnp.zeros((gtile_ref.shape[0], high - low, UNIT, STATE), BF16)


def weight_tiles(gtile_ref, rows, left, right, first, end):
    def tiles(j, count):
        cols = pl.ds(pl.multiple_of(j * STATE, STATE), count * STATE)
        part = product_sum(left, right, cols).astype(BF16)
        for d in range(gtile_ref.shape[0]):
            for k in range(count):
                put_tile(gtile_ref, d, j + k, part[d * rows:(d + 1) * rows, k * STATE:(k + 1) * STATE])

    pairs = (end - first) // 2

    @pl.loop(0, pairs)
    def _(j):
        tiles(first + 2 * j, 2)

    if first + 2 * pairs < end:
        tiles(end - 1, 1)


MESH = pl.DeviceIdType.MESH
PLANE = 4
QUARTER = DIN // PLANE
DMA = pltpu.SemaphoreType.DMA


def places():
    seq = lax.axis_index("seq")
    return lax.axis_index("dp"), seq, lax.rem(seq, PLANE), lax.div(seq, PLANE)


def greet(devices):
    barrier = pltpu.get_barrier_semaphore()
    for device in devices:
        pl.semaphore_signal(barrier, inc=1, device_id=device, device_id_type=MESH)
    pl.semaphore_wait(barrier, len(devices))


def remote(src, dst, send, recv, device):
    return pltpu.make_async_remote_copy(
        src_ref=src, dst_ref=dst, send_sem=send, recv_sem=recv, device_id=device, device_id_type=MESH)


def open_body(ndp, nseq, win_ref, wout_ref, tok_ref, w_ref, wsall_ref, wo_ref, halo_ref, ws_ref, send, recv, hsend, hrecv):
    dp, seq, _, _ = places()
    nxt, prev = lax.rem(seq + 1, nseq), lax.rem(seq + nseq - 1, nseq)
    others = [lax.rem(dp + d, ndp) for d in range(1, ndp)]
    ws_ref[...] = jnp.zeros_like(ws_ref)
    ws_ref[0:HEADS] = win_ref[DIN + XBC:PROJ]
    greet([(o, seq) for o in others] + [(dp, nxt), (dp, prev)])
    T = tok_ref.shape[1]
    width, rows = win_ref.shape[1], wout_ref.shape[0]
    columns = pl.ds(pl.multiple_of(dp * width, width), width)
    own_rows = pl.ds(pl.multiple_of(dp * rows, rows), rows)
    moves = [(ws_ref, wsall_ref.at[:, columns]), (win_ref.at[0:DIN + XBC], w_ref.at[:, columns]), (wout_ref, wo_ref.at[own_rows])]
    copies = [remote(tok_ref.at[:, T - HALO:T], halo_ref, hsend, hrecv, (dp, nxt))]
    for i, o in enumerate(others):
        for k, (src, dst) in enumerate(moves):
            copies.append(remote(src, dst, send.at[i, k], recv.at[i, k], (o, seq)))
    for copy in copies:
        copy.start()
    w_ref[:, columns] = win_ref[0:DIN + XBC]
    wsall_ref[:, columns] = ws_ref[...]
    wo_ref[own_rows] = wout_ref[...]
    for copy in copies:
        copy.wait()


def open_kernel(ndp, nseq, win, wout, tok):
    vmem = pl.BlockSpec(memory_space=pltpu.VMEM)
    M = tok.shape[0]
    shape = lambda *s: jax.ShapeDtypeStruct(s, BF16)
    return pl.pallas_call(
        functools.partial(open_body, ndp, nseq),
        in_specs=[vmem] * 2 + [pl.BlockSpec(memory_space=pl.ANY)],
        out_specs=[vmem] * 4,
        out_shape=[shape(DIN + XBC, D), shape(STATE, D), shape(DIN, D), shape(M, HALO, D)],
        scratch_shapes=[pltpu.VMEM((STATE, win.shape[1]), BF16), DMA((ndp - 1, 3)), DMA((ndp - 1, 3)), DMA, DMA],
        compiler_params=pltpu.CompilerParams(collective_id=1, has_side_effects=True, vmem_limit_bytes=VMEM_LIMIT),
        name="gather_weights",
    )(win, wout, tok)


SMALL = (("cw", CONV, XBC), ("cb", 1, XBC), ("ng", 1, D), ("og", 1, DIN), ("skip", 1, DIN), ("head", 2, STATE))
SMALL_ROWS = 104


def small_pieces():
    row, found = 0, []
    for index, (_, rows, width) in enumerate(SMALL):
        for r in range(rows):
            for j in range(width // STATE):
                found.append((index, r, j, row))
                row += 1
    return found


def strided(count, body):
    step = max(s for s in range(1, 13) if count % s == 0)

    @pl.loop(0, count // step)
    def _(i):
        body(pl.multiple_of(i * step, step), step)


GROUPS = 4


def units(ndp, nseq, tiles):
    need, step = tiles * (D // ndp // UNIT), GROUPS * nseq
    return -(-need // step) * step


def reducer_scratch(ndp, nseq, count):
    Z = nseq // PLANE
    u = lambda n, *lead: tuple(lead) + (n, UNIT, STATE)
    V = pltpu.VMEM
    pairs = [DMA((GROUPS, ndp - 1))] * 2 + [DMA((GROUPS,))] * 4 + [DMA((GROUPS, Z - 1))] * 4 + [DMA((GROUPS,))] * 4
    return [V(u(count, ndp - 1), BF16), V(u(count // 2), F32), V(u(count // 2), BF16), V(u(count // 2), BF16),
            V(u(count // 4), F32), V(u(count // 4), BF16), V(u(count // 4), BF16), V(u(count // 4), BF16),
            V(u(count // 4 // Z, Z - 1), BF16)] + pairs


class Reducer:
    def __init__(self, ndp, nseq, src, out, scratch, wait_only=7):
        self.wait_only = wait_only
        self.ndp, self.Z = ndp, nseq // PLANE
        self.src, self.out = src, out
        (self.r0, self.w1, self.st1, self.r1, self.w2, self.st2, self.r2, self.st3, self.r3) = scratch[:9]
        self.sems = [(scratch[9 + 2 * k], scratch[10 + 2 * k]) for k in range(7)]
        self.dp, self.seq, self.p, self.z = places()
        x, y = lax.rem(self.p, 2), lax.div(self.p, 2)
        self.others = [lax.rem(self.dp + d, ndp) for d in range(1, ndp)]
        self.pz = [lax.rem(self.z + d, self.Z) * PLANE + self.p for d in range(1, self.Z)]
        sides = ((x, self.seq + 1 - 2 * x), (y, self.seq + 2 - 4 * y))
        self.sides = [sides if g % 2 == 0 else sides[::-1] for g in range(GROUPS)]
        self.size = src.shape[1] // GROUPS
        self.half, self.quarter = self.size // 2, self.size // 4
        self.piece = self.quarter // self.Z

    def partners(self):
        (_, px), (_, py) = self.sides[0]
        return [(o, self.seq) for o in self.others] + [(self.dp, q) for q in (px, py)] + [(self.dp, q) for q in self.pz]

    def copies(self, stage, g):
        sizes, at = self.size, g * self.size
        o1, o2, o3 = g * self.half, g * self.quarter, g * self.piece
        send, recv = self.sems[stage]
        (b1, peer1), (b2, peer2) = self.sides[g]
        half_at = at + b1 * self.half
        quarter_at = half_at + b2 * self.quarter
        piece_at = quarter_at + self.z * self.piece
        if stage == 0:
            return [remote(self.src.at[o, pl.ds(at, sizes)], self.r0.at[i, pl.ds(at, sizes)], send.at[g, i], recv.at[g, i], (o, self.seq))
                    for i, o in enumerate(self.others)]
        if stage == 1:
            span = pl.ds(o1, self.half)
            return [remote(self.st1.at[span], self.r1.at[span], send.at[g], recv.at[g], (self.dp, peer1))]
        if stage == 2:
            span = pl.ds(o2, self.quarter)
            return [remote(self.st2.at[span], self.r2.at[span], send.at[g], recv.at[g], (self.dp, peer2))]
        if stage == 3:
            return [remote(self.st3.at[pl.ds(o2 + lax.rem(self.z + d, self.Z) * self.piece, self.piece)], self.r3.at[d - 1, pl.ds(o3, self.piece)],
                           send.at[g, d - 1], recv.at[g, d - 1], (self.dp, self.pz[d - 1])) for d in range(1, self.Z)]
        if stage == 4:
            span = pl.ds(piece_at, self.piece)
            return [remote(self.out.at[span], self.out.at[span], send.at[g, d - 1], recv.at[g, d - 1], (self.dp, self.pz[d - 1]))
                    for d in range(1, self.Z)]
        span, peer = (pl.ds(quarter_at, self.quarter), peer2) if stage == 5 else (pl.ds(half_at, self.half), peer1)
        return [remote(self.out.at[span], self.out.at[span], send.at[g], recv.at[g], (self.dp, peer))]

    def stage(self, stage, g):
        if stage > 0:
            for copy in self.copies(stage - 1, g):
                copy.wait_recv()
        if stage == self.wait_only:
            return
        (b1, _), (b2, _) = self.sides[g]
        at, o1, o2, o3 = g * self.size, g * self.half, g * self.quarter, g * self.piece
        if stage == 1:
            def total(i, c):
                v = self.src[self.dp, pl.ds(at + i, c)].astype(F32)
                for k in range(self.ndp - 1):
                    v = v + self.r0[k, pl.ds(at + i, c)].astype(F32)
                return v

            def body(i, c):
                self.w1[pl.ds(o1 + i, c)] = total(b1 * self.half + i, c)
                self.st1[pl.ds(o1 + i, c)] = total((1 - b1) * self.half + i, c).astype(BF16)
            strided(self.half, body)
        elif stage == 2:
            def body(i, c):
                keep, give = pl.ds(o1 + b2 * self.quarter + i, c), pl.ds(o1 + (1 - b2) * self.quarter + i, c)
                self.w2[pl.ds(o2 + i, c)] = self.w1[keep] + self.r1[keep].astype(F32)
                self.st2[pl.ds(o2 + i, c)] = (self.w1[give] + self.r1[give].astype(F32)).astype(BF16)
            strided(self.quarter, body)
        elif stage == 3:
            def body(i, c):
                span = pl.ds(o2 + i, c)
                v = self.w2[span] + self.r2[span].astype(F32)
                self.w2[span] = v
                self.st3[span] = v.astype(BF16)
            strided(self.quarter, body)
        elif stage == 4:
            v = self.w2[pl.ds(o2 + self.z * self.piece, self.piece)]
            for d in range(self.Z - 1):
                v = v + self.r3[d, pl.ds(o3, self.piece)].astype(F32)
            self.out[pl.ds(at + b1 * self.half + b2 * self.quarter + self.z * self.piece, self.piece)] = v.astype(BF16)
        for copy in self.copies(stage, g):
            copy.start()

    def at(self, k, table):
        for stage in range(self.wait_only + 1):
            for row, groups in ((0, (0, 1)), (1, (2, 3))):
                if table[row][stage] == k:
                    for g in groups:
                        self.stage(stage, g)

    def halves(self, src, out, sems):
        found = []
        for g in range(GROUPS):
            (b1, peer), _ = self.sides[g]
            span = pl.ds(g * self.size + b1 * self.half, self.half)
            found.append(remote(src.at[span], out.at[span], sems[0].at[g], sems[1].at[g], (self.dp, peer)))
        return found

    def own_halves(self, src, out):
        for g in range(GROUPS):
            (b1, _), _ = self.sides[g]
            at = g * self.size + b1 * self.half

            def body(i, c):
                out[pl.ds(at + i, c)] = src[pl.ds(at + i, c)]
            strided(self.half, body)

    def finish(self):
        for stage in range(self.wait_only):
            for g in range(GROUPS):
                for copy in self.copies(stage, g):
                    copy.wait_send()


def small_scratch(ndp, nseq):
    Z = nseq // PLANE
    V = pltpu.VMEM
    shape = (SMALL_ROWS, STATE)
    count = ndp - 1 + 2 + Z - 1
    return [V((ndp,) + shape, F32), V((2,) + shape, F32), V((2,) + shape, F32), V((Z,) + shape, F32), DMA((count,)), DMA((count,))]


class SmallReducer:
    def __init__(self, ndp, nseq, out, scratch):
        self.out = out
        self.bufs, (self.send, self.recv) = scratch[:4], scratch[4:6]
        dp, seq, p, z = places()
        Z = nseq // PLANE
        x, y = lax.rem(p, 2), lax.div(p, 2)
        self.z, self.Z = z, Z
        self.peers = [[(lax.rem(dp + d, ndp), seq) for d in range(1, ndp)], [(dp, seq + 1 - 2 * x)], [(dp, seq + 2 - 4 * y)],
                      [(dp, lax.rem(z + d, Z) * PLANE + p) for d in range(1, Z)]]
        self.at, self.begun, self.over, self.started = 0, False, False, []

    def send_all(self):
        buf = self.bufs[self.at]
        base = sum(len(q) for q in self.peers[:self.at])
        self.flying = [remote(buf.at[0], buf.at[1 + k], self.send.at[base + k], self.recv.at[base + k], device)
                       for k, device in enumerate(self.peers[self.at])]
        for copy in self.flying:
            copy.start()
        self.started += self.flying

    def begin(self, groups):
        buf = self.bufs[0]
        buf[0] = jnp.zeros(buf.shape[1:], F32)
        for index, r, j, row in small_pieces():
            v = groups[index][0][r:r + 1, j * STATE:(j + 1) * STATE]
            for other in groups[index][1:]:
                v = v + other[r:r + 1, j * STATE:(j + 1) * STATE]
            buf[0, row:row + 1] = v
        self.begun = True
        self.send_all()

    def advance(self):
        if self.over:
            return
        for copy in self.flying:
            copy.wait_recv()
        buf = self.bufs[self.at]
        if self.at < 3:
            v = buf[0]
            for k in range(1, buf.shape[0]):
                v = v + buf[k]
            self.at += 1
            self.bufs[self.at][0] = v
            self.send_all()
            return
        v = None
        for k in range(self.Z):
            piece = buf[lax.rem(self.z - k + self.Z, self.Z)]
            v = piece if v is None else v + piece
        self.out[...] = v
        self.over = True

    def finish(self):
        for copy in self.started:
            copy.wait_send()


def unpack_body(g1_ref, g2_ref, sm_ref, gin_ref, gout_ref, cw_ref, cb_ref, ng_ref, og_ref, skip_ref, rate_ref, step_ref):
    R = gin_ref.shape[1]
    U = R // UNIT
    tile = lambda ref, j: ref[j * U:(j + 1) * U].astype(F32).reshape(R, STATE)
    eye = jnp.where(iota((STATE, STATE), 0) == iota((STATE, STATE), 1), 1.0, 0.0).astype(BF16)
    turned = lambda ref, j: mm_nt(eye, ref[j * U:(j + 1) * U].reshape(R, STATE))
    for j in range(12):
        gin_ref[j * STATE:(j + 1) * STATE] = turned(g1_ref, j)
    for j in range(14):
        gin_ref[DIN + j * STATE:DIN + (j + 1) * STATE] = turned(g2_ref, j)
    gin_ref[DIN + XBC:] = turned(g2_ref, 14)[:HEADS]
    for half in range(2):
        for j in range(D // STATE):
            gout_ref[half * R:(half + 1) * R, j * STATE:(j + 1) * STATE] = tile(g1_ref, 12 + half * 6 + j)
    outs = {1: cb_ref, 2: ng_ref, 3: og_ref}
    low, high = iota((1, STATE), 1) < HEAD_DIM, iota((1, STATE), 1)
    lane = iota((1, STATE), 1)
    skip = jnp.zeros((1, STATE), F32)
    for index, r, j, row in small_pieces():
        v = sm_ref[row:row + 1]
        if index == 0:
            cw_ref[r:r + 1, j * STATE:(j + 1) * STATE] = v
        elif index in outs:
            outs[index][j * STATE:(j + 1) * STATE] = v[0]
        elif index == 4:
            left = jnp.sum(jnp.where(low, v, 0.0), axis=1, keepdims=True)
            right = jnp.sum(jnp.where(low, 0.0, v), axis=1, keepdims=True)
            skip = skip + jnp.where(lane == 2 * j, left, 0.0) + jnp.where(lane == 2 * j + 1, right, 0.0)
        else:
            (rate_ref, step_ref)[r][...] = v[0, :HEADS]
    skip_ref[...] = skip[0, :HEADS]


def unpack(g1, g2, sm, R):
    vmem = pl.BlockSpec(memory_space=pltpu.VMEM)
    sds = lambda *s: jax.ShapeDtypeStruct(s, F32)
    return pl.pallas_call(
        unpack_body,
        in_specs=[vmem] * 3,
        out_specs=[vmem] * 9,
        out_shape=[sds(PROJ, R), sds(2 * R, D), sds(CONV, XBC), sds(XBC), sds(D), sds(DIN), sds(HEADS), sds(HEADS), sds(HEADS)],
        compiler_params=pltpu.CompilerParams(vmem_limit_bytes=VMEM_LIMIT),
        name="unpack_gradients",
    )(g1, g2, sm)
VMEM = pl.BlockSpec(memory_space=pltpu.VMEM)
ANY = pl.BlockSpec(memory_space=pl.ANY)


class Refs:
    pass


def run(name, body, ins, outs, scratch, carried=(), collective_id=None):
    names = list(ins) + list(outs) + list(scratch)
    aliases = {list(ins).index(k): list(outs).index(k) for k in carried}

    def kernel(*refs):
        r = Refs()
        for k, ref in zip(names, refs):
            setattr(r, k, ref)
        body(r)

    params = dict(vmem_limit_bytes=VMEM_LIMIT)
    if collective_id is not None:
        params.update(collective_id=collective_id, has_side_effects=True)
    got = pl.pallas_call(
        kernel,
        in_specs=[s for s, _ in ins.values()],
        out_specs=[s for s, _ in outs.values()],
        out_shape=[s for _, s in outs.values()],
        scratch_shapes=list(scratch.values()),
        input_output_aliases=aliases,
        compiler_params=pltpu.CompilerParams(**params),
        name=name,
    )(*[a for _, a in ins.values()])
    return dict(zip(outs, got))


class Mover:
    def __init__(self, sems):
        self.sems, self.count, self.flying = sems, 0, []

    def start(self, src, dst, late=True):
        copy = pltpu.make_async_copy(src, dst, self.sems.at[self.count])
        self.count += 1
        copy.start()
        if late:
            self.flying.append(copy)
        return copy

    def finish(self):
        for copy in self.flying:
            copy.wait()


def exchange_scratch(nseq):
    V = pltpu.VMEM
    Z = nseq // PLANE
    quarter = (STATE, QUARTER)
    return dict(x_out=V((STATE, DIN), KIND), x_got=V((PLANE,) + quarter, KIND), x_tots=V((PLANE, 8, STATE), F32), x_pre=V(quarter, F32),
                x_zin=V((Z,) + quarter, HOP_KIND), x_ztots=V((Z, 8, STATE), F32), x_back=V((PLANE,) + quarter, KIND),
                x_ts=DMA((3,)), x_tr=DMA((3,)), x_s=DMA((2, 3)), x_r=DMA((2, 3)), x_zs=DMA((2, Z - 1)), x_zr=DMA((2, Z - 1)), x_zts=DMA((Z - 1,)),
                x_ztr=DMA((Z - 1,)), x_bs=DMA((2, 3)), x_br=DMA((2, 3)))


class Exchange:
    def __init__(self, nseq, upward, state, totals, r):
        self.upward, self.state, self.totals, self.r = upward, state, totals, r
        self.dp, self.seq, self.p, self.z = places()
        self.Z = nseq // PLANE
        self.base = self.z * PLANE
        self.peers = [lax.rem(self.p + d, PLANE) for d in range(PLANE)]
        self.line = [(self.dp, lax.rem(self.z + d, self.Z) * PLANE + self.p) for d in range(1, self.Z)]
        self.greeted = [(self.dp, self.base + q) for q in self.peers[1:]] + self.line
        self.steps = 7
        self.at = 0

    def columns(self, q):
        return pl.ds(pl.multiple_of(q * QUARTER, QUARTER), QUARTER)

    def rows(self, part):
        return pl.ds(part * (STATE // 2), STATE // 2)

    def first(self, part):
        r = self.r
        found = []
        for d in range(1, PLANE):
            to = (self.dp, self.base + self.peers[d])
            if part == 0:
                found.append(remote(self.totals, r.x_tots.at[d], r.x_ts.at[d - 1], r.x_tr.at[d - 1], to))
            found.append(remote(self.state.at[self.rows(part), self.columns(self.peers[d])], r.x_got.at[d, self.rows(part)], r.x_s.at[part, d - 1],
                                r.x_r.at[part, d - 1], to))
        return found

    def along(self, part, d):
        r = self.r
        to = (self.dp, lax.rem(self.z + (self.Z - d if self.upward else d), self.Z) * PLANE + self.p)
        copies = [remote(r.x_zin.at[0, self.rows(part)], r.x_zin.at[d, self.rows(part)], r.x_zs.at[part, d - 1], r.x_zr.at[part, d - 1], to)]
        if part == 0:
            copies.append(remote(r.x_ztots.at[0], r.x_ztots.at[d], r.x_zts.at[d - 1], r.x_ztr.at[d - 1], to))
        sends = self.z >= d if self.upward else self.z + d < self.Z
        receives = self.z + d < self.Z if self.upward else self.z >= d
        return copies, sends, receives

    def last(self, part):
        r = self.r
        return [remote(r.x_back.at[d, self.rows(part)], r.x_out.at[self.rows(part), self.columns(self.p)], r.x_bs.at[part, d - 1],
                       r.x_br.at[part, d - 1], (self.dp, self.base + lax.rem(self.p + PLANE - d, PLANE))) for d in range(1, PLANE)]

    def turn(self):
        order = range(PLANE - 1, -1, -1) if self.upward else range(PLANE)
        slots = [lax.rem(self.p - q + PLANE, PLANE) for q in order]
        return slots, spread_matrix(self.p * QUARTER, QUARTER)

    def begin(self):
        r = self.r
        for copy in self.first(0):
            copy.start()
        r.x_tots[0] = self.totals[...]
        r.x_got[0] = self.state[:, self.columns(self.p)].astype(KIND)

    def plane(self, part):
        r = self.r
        for copy in self.first(part):
            copy.wait_recv()
        slots, matrix = self.turn()
        total = jnp.zeros((STATE // 2, QUARTER), F32)
        for slot in slots:
            total = spread(jnp.exp2(r.x_tots[slot]), matrix)[0:1] * total + r.x_got[slot, self.rows(part)].astype(F32)
        r.x_zin[0, self.rows(part)] = total.astype(HOP_KIND)
        if part == 0:
            r.x_ztots[0] = r.x_tots[0] + r.x_tots[1] + r.x_tots[2] + r.x_tots[3]
        for d in range(1, self.Z):
            copies, sends, _ = self.along(part, d)

            @pl.when(sends)
            def _():
                for copy in copies:
                    copy.start()

    def give(self, part):
        r = self.r
        rows = self.rows(part)
        slots, matrix = self.turn()
        r.x_pre[rows] = jnp.zeros((STATE // 2, QUARTER), F32)
        for d in range(self.Z - 1, 0, -1):
            copies, _, receives = self.along(part, d)

            @pl.when(receives)
            def _():
                for copy in copies:
                    copy.wait_recv()
                r.x_pre[rows] = spread(jnp.exp2(r.x_ztots[d]), matrix)[0:1] * r.x_pre[rows] + r.x_zin[d, rows].astype(F32)
        total = r.x_pre[rows]
        for slot in slots:
            r.x_back[slot, rows] = total.astype(KIND)
            total = spread(jnp.exp2(r.x_tots[slot]), matrix)[0:1] * total + r.x_got[slot, rows].astype(F32)
        for copy in self.last(part):
            copy.start()
        r.x_out[rows, self.columns(self.p)] = r.x_back[0, rows]

    def end(self):
        for part in range(2):
            for copy in self.last(part):
                copy.wait_recv()
        for part in range(2):
            for copy in self.first(part) + self.last(part):
                copy.wait_send()
            for d in range(1, self.Z):
                copies, sends, _ = self.along(part, d)

                @pl.when(sends)
                def _():
                    for copy in copies:
                        copy.wait_send()

    def step(self, k):
        if k == 0:
            self.begin()
        elif k == 1:
            for copy in self.first(1):
                copy.start()
        elif k in (2, 3):
            self.plane(k - 2)
        elif k in (4, 5):
            self.give(k - 4)
        else:
            self.end()

    def tick(self):
        if self.at < self.steps:
            self.step(self.at)
            self.at += 1

    def finish(self):
        while self.at < self.steps:
            self.tick()


class NoExchange:
    def tick(self):
        pass

    finish = tick


def chunks(T):
    return [(c, slice(c * CHUNK, (c + 1) * CHUNK)) for c in range(T // CHUNK)]


SHARED1 = ("cin", "cout", "bc", "info", "sl", "cum", "chalo")


def k1_body(nseq, m, ahead, r):
    T = r.gate_v.shape[0]
    NC = T // CHUNK
    moves = Mover(r.sems)
    loads = [moves.start(r.tok.at[m], r.tok_v, late=False), moves.start(r.w, r.w_v, late=False)]
    trade = NoExchange()
    if ahead:
        trade = Exchange(nseq, False, r.x_state, r.x_totals, r)
        greet(trade.greeted)
    trade.tick()
    decay, bias, hp = head_params(r.params)
    decay2 = decay * LOG2E
    gain = param(r.params, "ng")
    r.cb[...] = param(r.params, "cb")
    first = lax.axis_index("seq") == 0
    r.an[0:HALO] = jnp.where(first, 0.0, norm_rows(r.halo[m], gain)[2].astype(F32)).astype(BF16)
    loads[0].wait()
    r.an[HALO:] = norm_rows(r.tok_v[...], gain)[2]
    arg = mm_nt(r.an[HALO:], r.ws[...]) + bias
    dt = jnp.maximum(arg, 0.0) + jnp.log1p(jnp.exp(-jnp.abs(arg)))
    r.info_v[0] = arg
    r.info_v[1] = dt
    r.dt2[...] = jnp.concatenate(split2(dt), axis=1)
    tri = triangle(False)
    ends = []
    for c, rows in chunks(T):
        lc = tri_sum(tri, dt[rows] * decay2)
        r.info_v[2, rows] = lc
        ends.append(lc[CHUNK - 1:CHUNK])
        r.tw2[rows] = jnp.concatenate(split2(jnp.exp2(lc[CHUNK - 1:CHUNK] - lc)), axis=1)
    before, after = jnp.zeros((1, STATE), F32), jnp.zeros((1, STATE), F32)
    for c in range(NC + 1):
        r.cum_v[0, c:c + 1] = before
        r.cum_v[1, NC - c:NC - c + 1] = after
        if c < NC:
            before, after = before + ends[c], after + ends[NC - 1 - c]
    r.totals[...] = jnp.broadcast_to(before, (8, STATE))
    trade.tick()
    moves.start(r.info_v, r.info.at[m])
    moves.start(r.cum_v, r.cum.at[m])
    loads[1].wait()

    def conv_tile(j, cols):
        wcols = pl.ds(pl.multiple_of(DIN + j * TILE, TILE), TILE)
        raw = mm_nt(r.an[...], r.w_v[wcols, :])
        r.cpad[...] = raw
        r.cin_v[:, cols] = raw[HALO:].astype(BF16)
        r.chalo_v[:, cols] = raw[:HALO]
        out = r.cb[:, cols]
        for k in range(CONV):
            out = out + r.cw[k:k + 1, cols] * r.cpad[HALO - CONV + 1 + k:HALO - CONV + 1 + k + T]
        r.cout_v[:, cols] = out
        for k, name in enumerate(("cin", "cout")):
            pltpu.make_async_copy(getattr(r, name + "_v").at[:, cols], getattr(r, name).at[m, :, cols], r.tsems.at[k, j]).start()
        return out * sigmoid(out)

    def x_tile(j):
        cols = pl.ds(pl.multiple_of(j * TILE, TILE), TILE)
        x = conv_tile(j, cols)
        matrix = spread_matrix(j * TILE, TILE)
        ux = x * mm(r.dt2[...], matrix)
        r.u[:, cols] = ux.astype(BF16)
        hi, lo = split2(ux * mm(r.tw2[...], matrix))
        for c, rows in chunks(T):
            r.ub[c, 0:CHUNK, cols] = hi[rows]
            r.ub[c, CHUNK:, cols] = lo[rows]
        skip_tile = spread(jnp.broadcast_to(hp[2:3], (8, STATE)), matrix)[0:1]
        r.ypart_v[:, cols] = x * skip_tile

    pl.loop(0, DIN // TILE // 2 + 1)(x_tile)
    trade.tick()
    pl.loop(DIN // TILE // 2 + 1, DIN // TILE)(x_tile)
    r.bc_v[...] = conv_tile(DIN // TILE, pl.ds(DIN, TILE))
    moves.start(r.chalo_v, r.chalo.at[m])
    moves.start(r.bc_v, r.bc.at[m])
    trade.tick()
    matrix = spread_matrix(0, DIN)
    state = jnp.zeros((STATE, DIN), F32)
    for c, rows in chunks(T):
        b16 = r.bc_v[rows, 0:STATE].astype(BF16)
        r.sl_v[c] = state
        keep = spread(jnp.exp2(jnp.broadcast_to(ends[c], (8, STATE))), matrix)[0:1]
        state = keep * state + mm_tn(jnp.concatenate([b16, b16], axis=0), r.ub[c])
    r.sl_v[NC] = state
    r.sdev[...] = state
    moves.start(r.sl_v, r.sl.at[m])

    @pl.loop(0, DIN // TILE)
    def _(j):
        cols = pl.ds(pl.multiple_of(j * TILE, TILE), TILE)
        r.gate_v[:, cols] = mm_nt(r.an[HALO:], r.w_v[cols, :])
        pltpu.make_async_copy(r.gate_v.at[:, cols], r.gate.at[:, cols], r.tsems.at[2, j]).start()
    trade.tick()

    causal = iota((CHUNK, CHUNK), 0) >= iota((CHUNK, CHUNK), 1)
    for c, rows in chunks(T):
        gram = jnp.where(causal, fine_nt(r.bc_v[rows, STATE:2 * STATE], r.bc_v[rows, 0:STATE]), 0.0)
        lc = r.info_v[2, rows]
        lct = lc.T
        for p in range(HEADS // 2):
            cols = slice(p * STATE, (p + 1) * STATE)
            mixes = []
            for h in (2 * p, 2 * p + 1):
                gap = lc[:, h:h + 1] - lct[h:h + 1, :]
                mixes.append((gram * jnp.exp2(jnp.minimum(gap, 0.0))).astype(BF16))
            r.ypart_v[rows, cols] = r.ypart_v[rows, cols] + mm(jnp.concatenate(mixes, axis=1), doubled(r.u[rows, cols]))
        moves.start(r.ypart_v.at[rows], r.ypart.at[rows])
        if c == NC // 2:
            trade.tick()
    trade.finish()
    if ahead:
        moves.start(r.x_out, r.starts.at[m - 1])
    moves.finish()
    for k, (src, dst) in enumerate(((r.cin_v, r.cin.at[m]), (r.cout_v, r.cout.at[m]), (r.gate_v, r.gate))):
        for j in range(src.shape[1] // TILE):
            cols = slice(j * TILE, (j + 1) * TILE)
            pltpu.make_async_copy(src.at[:, cols], dst.at[:, cols], r.tsems.at[k, j]).wait()


def k1(nseq, m, carried, tok, halo, w, ws, cw, params, sdev=None, totals=None):
    M, T, _ = tok.shape
    NC = T // CHUNK
    V = pltpu.VMEM
    sds = jax.ShapeDtypeStruct
    ahead = m > 0
    ins = dict(tok=(ANY, tok), w=(ANY, w), halo=(VMEM, halo), ws=(VMEM, ws), cw=(VMEM, cw), params=(VMEM, params))
    shapes = dict(cin=(T, XBC), cout=(T, XBC), bc=(T, 2 * STATE), info=(3, T, STATE), sl=(NC + 1, STATE, DIN), cum=(2, NC + 1, STATE),
                  chalo=(HALO, XBC))
    kinds = {k: BF16 if k == "cin" else F32 for k in SHARED1}
    outs = {k: (ANY, sds((M,) + shapes[k], kinds[k])) for k in SHARED1}
    outs.update(gate=(ANY, sds((T, DIN), F32)), ypart=(ANY, sds((T, DIN), F32)), sdev=(VMEM, sds((STATE, DIN), F32)),
                totals=(VMEM, sds((8, STATE), F32)))
    scratch = dict(cb=V((1, XBC), F32), tok_v=V((T, D), BF16), w_v=V(w.shape, BF16), cpad=V((HALO + T, TILE), F32), an=V((HALO + T, D), BF16), u=V((T, DIN), BF16),
                   ub=V((NC, 2 * CHUNK, DIN), BF16), dt2=V((T, 2 * STATE), BF16), tw2=V((T, 2 * STATE), BF16),
                   gate_v=V((T, DIN), F32), ypart_v=V((T, DIN), F32), sems=DMA((20 + NC,)), tsems=DMA((3, XBC // TILE)),
                   **{k + "_v": V(shapes[k], kinds[k]) for k in SHARED1})
    if ahead:
        ins.update({k: (ANY, carried[k]) for k in SHARED1}, x_state=(VMEM, sdev), x_totals=(VMEM, totals))
        outs.update(starts=(ANY, sds((M, STATE, DIN), KIND)))
        if m > 1:
            ins.update(starts=(ANY, carried["starts"]))
        scratch.update(exchange_scratch(nseq))
    keep = [k for k in SHARED1 + ("starts",) if k in ins]
    return run("forward_local", functools.partial(k1_body, nseq, m, ahead), ins, outs, scratch, keep, collective_id=1 + m if ahead else None)


SHARED2 = ("mixed", "dgate", "dy", "rows_dot", "gl")


def k2_body(nseq, M, m, kind, r):
    T = r.gate_v.shape[0]
    NC = T // CHUNK
    moves = Mover(r.sems)
    loads = {}
    for k, src in (("start", r.starts_in.at[m]), ("info", r.info.at[m]), ("cum", r.cum.at[m]), ("bc", r.bc.at[m]), ("sl", r.sl.at[m, 0:NC]),
                   ("ypart", r.ypart), ("gate", r.gate), ("tok", r.tok.at[m]), ("wo", r.wo), ("cot", r.cot.at[m])):
        loads[k] = moves.start(src, getattr(r, k + "_v"), late=False)
    upward = kind == "later"
    trade = Exchange(nseq, upward, r.x_state, r.x_totals, r)
    greet(trade.greeted)
    trade.tick()
    matrix = spread_matrix(0, DIN)
    gather = gather_matrix()
    loads["tok"].wait()
    r.norm_t[...] = norm_rows(r.tok_v[...], param(r.params, "ng"))[2].T
    og = param(r.params, "og")
    loads["cot"].wait()
    loads["wo"].wait()
    trade.tick()

    @pl.loop(0, DIN // TILE)
    def _(j):
        cols = pl.ds(pl.multiple_of(j * TILE, TILE), TILE)
        r.dbr[:, cols] = mm_nt(r.cot_v[...], r.wo_v[cols, :])

    for k in ("start", "info", "cum", "bc", "sl", "ypart", "gate"):
        loads[k].wait()
    trade.tick()
    for c, rows in chunks(T):
        keep = spread(jnp.exp2(jnp.broadcast_to(r.cum_v[0, c:c + 1], (8, STATE))), matrix)[0:1]
        state = halves(r.sl_v[c] + keep * r.start_v[...].astype(F32))
        c16 = r.bc_v[rows, STATE:2 * STATE].astype(BF16)
        lift = spread(jnp.exp2(r.info_v[2, rows]), matrix)
        yc = r.ypart_v[rows] + lift * mm(jnp.concatenate([c16, c16], axis=1), state)
        r.ypart_v[rows] = yc
        g = r.gate_v[rows]
        gated = yc * (g * sigmoid(g))
        scale = lax.rsqrt(jnp.mean(gated * gated, axis=-1, keepdims=True) + EPS)
        r.oscale[rows] = jnp.broadcast_to(scale, (CHUNK, STATE))
        r.branch[rows] = (gated * scale * og).astype(BF16)
        if c == 1:
            trade.tick()
    r.branch_t[...] = r.branch[...].T
    for j in range(D // TILE):
        cols = slice(j * TILE, (j + 1) * TILE)
        r.mixed_v[:, cols] = (r.tok_v[:, cols].astype(F32) + mm(r.branch[...], r.wo_v[:, cols])).astype(BF16)
    moves.start(r.mixed_v, r.mixed.at[m])
    trade.tick()
    r.ogr[...] = jnp.zeros_like(r.ogr)
    r.gdev[...] = jnp.zeros_like(r.gdev)
    for c, rows in reversed(chunks(T)):
        g = r.gate_v[rows]
        yc = r.ypart_v[rows]
        db = r.dbr[rows]
        scale = r.oscale[rows][:, 0:1]
        sig = sigmoid(g)
        act = g * sig
        gated = yc * act
        unit = gated * scale
        r.ogr[...] += jnp.sum(db * unit, axis=0, keepdims=True)
        e = db * og
        mean = jnp.mean(e * unit, axis=-1, keepdims=True)
        dgated = scale * (e - unit * mean)
        r.dgate_v[rows] = (dgated * yc * (sig * (1.0 + g * (1.0 - sig)))).astype(BF16)
        high, low = split2(dgated * act)
        dyf = high.astype(F32) + low.astype(F32)
        r.dy_v[rows] = dyf
        r.rows_dot_v[rows] = head_sums(dyf * yc, gather)
        lc = r.info_v[2, rows]
        lifted = halves(dyf * spread(jnp.exp2(lc), matrix))
        c16 = r.bc_v[rows, STATE:2 * STATE].astype(BF16)
        r.gl_v[c] = r.gdev[...]
        keep = spread(jnp.exp2(jnp.broadcast_to(lc[CHUNK - 1:CHUNK], (8, STATE))), matrix)[0:1]
        r.gdev[...] = keep * r.gdev[...] + mm_tn(jnp.concatenate([c16, c16], axis=0), lifted)
        moves.start(r.dy_v.at[rows], r.dy.at[m, rows])
        moves.start(r.gl_v.at[c], r.gl.at[m, c])
        if c == NC - 2:
            trade.tick()
    moves.start(r.dgate_v, r.dgate.at[m])
    moves.start(r.rows_dot_v, r.rows_dot.at[m])
    if m == M - 1:
        early_grads(r)
    trade.finish()
    if upward:
        moves.start(r.x_out, r.laters.at[m - 1])
    else:
        moves.start(r.x_out, r.starts.at[M - 1])
    moves.finish()


def early_grads(r):
    dp = r.g1.shape[0]
    rows = D // dp
    r.extra.finish()
    clear_tiles(r.g1, rows, 24)

    def summed(lefts, rights, cols):
        total = None
        for left, right in zip(lefts, rights):
            part = mm(left[...], right[:, cols])
            total = part if total is None else total + part
        return total.astype(BF16)

    @pl.loop(0, DIN // TILE)
    def _(j):
        part = summed(r.norm_ts + [r.norm_t], r.dgates + [r.dgate_v], pl.ds(pl.multiple_of(j * TILE, TILE), TILE))
        for d in range(dp):
            for k in range(TILE // STATE):
                put_tile(r.g1, d, j * (TILE // STATE) + k, part[d * rows:(d + 1) * rows, k * STATE:(k + 1) * STATE])

    @pl.loop(0, D // TILE)
    def _(j):
        part = summed(r.branch_ts + [r.branch_t], r.cots + [r.cot_v], pl.ds(pl.multiple_of(j * TILE, TILE), TILE))
        for d in range(dp):
            for half in range(2):
                low = (2 * d + half) * rows
                for k in range(TILE // STATE):
                    put_tile(r.g1, d, 12 + half * 6 + j * (TILE // STATE) + k, part[low:low + rows, k * STATE:(k + 1) * STATE])


def k2(ndp, nseq, m, one, before, tok, cot, params, wo, state, totals, count):
    M, T, _ = tok.shape
    NC = T // CHUNK
    V = pltpu.VMEM
    sds = jax.ShapeDtypeStruct
    kind = "earlier" if m == 0 else "later"
    ins = dict(tok=(ANY, tok), cot=(ANY, cot), wo=(ANY, wo), params=(VMEM, params), info=(ANY, one["info"]), cum=(ANY, one["cum"]),
               bc=(ANY, one["bc"]), sl=(ANY, one["sl"]), ypart=(ANY, one["ypart"]), gate=(ANY, one["gate"]),
               x_state=(VMEM, state), x_totals=(VMEM, totals))
    shapes = dict(mixed=((T, D), BF16), dgate=((T, DIN), BF16), dy=((T, DIN), F32), rows_dot=((T, STATE), F32), gl=((NC, STATE, DIN), F32))
    outs = {k: (ANY, sds((M,) + s, t)) for k, (s, t) in shapes.items()}
    outs.update(gdev=(VMEM, sds((STATE, DIN), F32)), ogr=(VMEM, sds((1, DIN), F32)))
    scratch = dict(tok_v=V((T, D), BF16), cot_v=V((T, D), BF16), wo_v=V(wo.shape, BF16), info_v=V((3, T, STATE), F32), cum_v=V((2, NC + 1, STATE), F32),
                   bc_v=V((T, 2 * STATE), F32), sl_v=V((NC, STATE, DIN), F32), ypart_v=V((T, DIN), F32), gate_v=V((T, DIN), F32),
                   start_v=V((STATE, DIN), KIND), dbr=V((T, DIN), F32), branch=V((T, DIN), BF16), oscale=V((T, STATE), F32),
                   sems=DMA((20 + 2 * NC,)), **{k + "_v": V(s, t) for k, (s, t) in shapes.items()})
    scratch.update(exchange_scratch(nseq))
    last = m == M - 1
    turned = dict(branch_t=sds((DIN, T), BF16), norm_t=sds((D, T), BF16))
    if last:
        scratch.update(branch_t=V((DIN, T), BF16))
        outs.update(norm_t=(VMEM, turned["norm_t"]))
        outs.update(g1=(VMEM, sds((ndp, count, UNIT, STATE), BF16)))
        for i, b in enumerate(before):
            for k in turned:
                ins[k + str(i)] = (VMEM, b[k])
            scratch["dgate_e%d" % i] = V((T, DIN), BF16)
            scratch["cot_e%d" % i] = V((T, D), BF16)
    else:
        outs.update({k: (VMEM, s) for k, s in turned.items()})
    keep = []
    if m == 0:
        ins.update(starts=(ANY, one["starts"]))
        outs.update(starts=(ANY, sds(one["starts"].shape, KIND)))
        keep += ["starts"]
    else:
        ins.update({k: (ANY, before[-1][k]) for k in SHARED2}, starts_in=(ANY, one["starts"]))
        outs.update(laters=(ANY, sds((M, STATE, DIN), KIND)))
        keep += list(SHARED2)
        if m > 1:
            ins.update(laters=(ANY, before[-1]["laters"]))
            keep += ["laters"]

    def body(r):
        if m == 0:
            r.starts_in = r.starts
        if last:
            named = lambda k: [getattr(r, k + str(i)) for i in range(len(before))]
            r.norm_ts, r.branch_ts, r.dgates, r.cots = named("norm_t"), named("branch_t"), named("dgate_e"), named("cot_e")
            extra = Mover(r.esems)
            copies = []
            for i in range(len(before)):
                copies += [extra.start(r.dgate.at[i], r.dgates[i]), extra.start(r.cot.at[i], r.cots[i])]
            r.extra = extra
        k2_body(nseq, M, m, kind, r)

    if last:
        scratch.update(esems=DMA((2 * M,)))
    return run("gate_and_out", body, ins, outs, scratch, keep, collective_id=1 + M + m)
TURNS = 4
EARLY_TURNS = ((0, 4, 9, 13, 18, 25, 32), (0, 8, 12, 17, 22, 29, 32))


def k3_body(ndp, nseq, micros, parts, hp_ref, cw_ref, chalo_ref, cum_ref, cin_ref, cout_ref, bc_ref, info_ref, sl_ref, sl_next_ref, start_ref, dy_ref, r_ref,
            gl_ref, later_ref, g1_ref, x_state, x_totals,
            dcin_ref, tail_ref, head_ref, dstep_ref, gcw_ref, gcb_ref, gskip_ref, ghead_ref, sum1_ref,
            dconv, w, xdu, ub, dyl, dgt, dt_x, tail_x, bg, later_v, landing, *rest):
    m, i = pl.program_id(0), pl.program_id(1)
    NC = pl.num_programs(1)
    c = NC - 1 - i
    step = m * NC + i
    steps = pl.num_programs(0) * NC
    traded = exchange_scratch(nseq)
    r = Refs()
    for name, ref in zip(traded, rest):
        setattr(r, name, ref)
    trade = Exchange(nseq, True, x_state, x_totals, r)
    reducer = Reducer(ndp, nseq, g1_ref, landing, rest[len(traded):], wait_only=6)
    M, own_turns = micros, TURNS * (micros - 1) * parts
    all_turns = TURNS * micros * parts
    trade_turns = [own_turns * t // 16 for t in (0, 2, 4, 6, 9, 11, 16)]
    table = [[min(t * all_turns // 32, all_turns) for t in row] for row in EARLY_TURNS]

    def comm(place):
        for turn in range(all_turns):
            if turn % TURNS != place:
                continue
            busy = turn in table[0] or turn in table[1]
            if not (busy or turn in trade_turns):
                continue

            @pl.when(step == turn // TURNS)
            def _():
                for n in range(trade.steps):
                    if trade_turns[n] == turn:
                        trade.step(n)
                reducer.at(turn, table)

    @pl.when(step == 0)
    def _():
        greet(reducer.partners() + trade.greeted)

    comm(0)

    @pl.when(jnp.logical_and(i == 0, m < M - 1))
    def _():
        later_v[...] = later_ref[0]

    @pl.when(jnp.logical_and(i == 0, m == M - 1))
    def _():
        later_v[...] = r.x_out[...]

    decay, _, hp = head_params(hp_ref)
    matrix = spread_matrix(0, DIN)
    gather = gather_matrix()
    skip = spread(jnp.broadcast_to(hp[2:3], (8, STATE)), matrix)[0:1]

    @pl.when(step == 0)
    def _():
        gcw_ref[...] = jnp.zeros_like(gcw_ref)
        gcb_ref[...] = jnp.zeros_like(gcb_ref)
        gskip_ref[...] = jnp.zeros_like(gskip_ref)
        ghead_ref[...] = jnp.zeros_like(ghead_ref)

    @pl.when(i == 0)
    def _():
        dconv[CHUNK:] = jnp.zeros((8, XBC), F32)

    @pl.when(i > 0)
    def _():
        dconv[CHUNK:] = dconv[0:8]

    tri_up = triangle(True)
    b32 = bc_ref[0, :, 0:STATE]
    c32 = bc_ref[0, :, STATE:2 * STATE]
    keeps_st = iota((CHUNK, CHUNK), 0) <= iota((CHUNK, CHUNK), 1)
    gram_t = jnp.where(keeps_st, fine_nt(c32, b32).T, 0.0)
    b, cc = b32.astype(BF16), c32.astype(BF16)
    lc = info_ref[0, 2]
    lct = lc.T
    dt = info_ref[0, 1]
    dt_x[...] = spread(dt, matrix)
    tail_x[...] = spread(jnp.exp2(lc[CHUNK - 1:CHUNK] - lc), matrix)
    dyl[...] = (dy_ref[0] * spread(jnp.exp2(lc), matrix)).astype(BF16)
    wide8 = lambda v: spread(jnp.exp2(jnp.broadcast_to(v, (8, STATE))), matrix)[0:1]
    gc = gl_ref[0, 0] + wide8(cum_ref[0, 1, pl.ds(c + 1, 1)]) * later_v[...].astype(F32)
    s_in = sl_ref[0, 0] + wide8(cum_ref[0, 0, pl.ds(c, 1)]) * start_ref[0].astype(F32)
    s_out = sl_next_ref[0, 0] + wide8(cum_ref[0, 0, pl.ds(c + 1, 1)]) * start_ref[0].astype(F32)
    gc2 = halves(gc)
    gcb16 = gc2[0:STATE]
    bnd = head_sums(jnp.broadcast_to(jnp.sum(gc * s_out, axis=0, keepdims=True), (8, DIN)), gather)[0:1]
    bg[...] = mm(jnp.concatenate([b, b], axis=1), gc2)
    dgt[...] = jnp.zeros((CHUNK, CHUNK), F32)
    for p in range(HEADS // 2):
        if p == 4:
            comm(1)
        if p == 8:
            comm(2)
        cols = slice(p * STATE, (p + 1) * STATE)
        v = cout_ref[0, :, cols]
        sig = sigmoid(v)
        x = v * sig
        dtx, tlx = dt_x[:, cols], tail_x[:, cols]
        ux = x * dtx
        u16 = ux.astype(BF16)
        ub[:, cols] = (ux * tlx).astype(BF16)
        dyf = dy_ref[0, :, cols]
        dy_high, dy_low = split2(dyf)
        dy2 = doubled(dy_high)
        decays, mixes = [], []
        for h in (2 * p, 2 * p + 1):
            gap = lct[h:h + 1, :] - lc[:, h:h + 1]
            e = jnp.exp2(jnp.minimum(gap, 0.0))
            decays.append(e)
            mixes.append((gram_t * e).astype(BF16))
        mix = jnp.concatenate(mixes, axis=1)
        du = mm(mix, dy2) + mm(mix, doubled(dy_low))
        dmix = mm_nt(u16, dy2)
        dgt[...] = dgt[...] + (dmix[:, :CHUNK] * decays[0] + dmix[:, CHUNK:] * decays[1])
        du_state = tlx * bg[:, cols]
        sk = skip[:, cols]
        dyx = dyf * x
        gskip_ref[:, cols] = gskip_ref[:, cols] + jnp.sum(dyx, axis=0, keepdims=True)
        w[:, cols] = dyx * sk + u16.astype(F32) * du + ux * du_state
        du = du + du_state
        xdu[:, cols] = x * du
        dx = dtx * du + sk * dyf
        dconv[0:CHUNK, cols] = dx * (sig * (1.0 + v * (1.0 - sig)))
    dg16 = jnp.where(keeps_st, dgt[...], 0.0).astype(BF16)
    db = mm(dg16, cc) + mm_nt(ub[...], gcb16)
    dc = mm_tn(dg16, b) + mm_nt(dyl[...], s_in.astype(BF16))
    v = cout_ref[0, :, DIN:XBC]
    sig = sigmoid(v)
    dconv[0:CHUNK, DIN:XBC] = jnp.concatenate([db, dc], axis=1) * (sig * (1.0 + v * (1.0 - sig)))
    dl = r_ref[0] - head_sums(w[...], gather)
    da = bnd + tri_sum(tri_up, dl)
    d_dt = head_sums(xdu[...], gather, 2) + da * decay
    dstep = d_dt * sigmoid(info_ref[0, 0])
    dstep_ref[0] = dstep.astype(BF16)
    ghead_ref[0:1] = ghead_ref[0:1] + decay * jnp.sum(da * dt, axis=0, keepdims=True)
    ghead_ref[1:2] = ghead_ref[1:2] + jnp.sum(dstep, axis=0, keepdims=True)

    @pl.loop(0, XBC // TILE)
    def _(j):
        cols = pl.ds(pl.multiple_of(j * TILE, TILE), TILE)
        gcb_ref[:, cols] = gcb_ref[:, cols] + jnp.sum(dconv[0:CHUNK, cols], axis=0, keepdims=True)
        own = cin_ref[0, :, cols].astype(F32)
        total = None
        for k in range(CONV):
            ahead = dconv[CONV - 1 - k:CONV - 1 - k + CHUNK, cols]
            gcw_ref[k:k + 1, cols] = gcw_ref[k:k + 1, cols] + jnp.sum(own * ahead, axis=0, keepdims=True)
            term = cw_ref[k:k + 1, cols] * ahead
            total = term if total is None else total + term
        dcin_ref[0, :, cols] = total.astype(BF16)

        @pl.when(i == 0)
        def _():
            tail_ref[0, :, cols] = total[CHUNK - HALO:]

    @pl.when(i == NC - 1)
    def _():
        head_ref[0] = dconv[0:8]
        for k in range(CONV - 1):
            for n in range(CONV - 1 - k):
                low = HALO - CONV + 1 + k + n
                gcw_ref[k:k + 1] = gcw_ref[k:k + 1] + chalo_ref[0, low:low + 1] * dconv[n:n + 1]

    comm(TURNS - 1)

    @pl.when(step == steps - 1)
    def _():
        reducer.at(all_turns, table)
        reducer.finish()

        def body(at, c):
            sum1_ref[pl.ds(at, c)] = landing[pl.ds(at, c)]
        strided(landing.shape[0], body)


def k3(ndp, nseq, hp, cw, chalo, cum, cin, cout, bc, info, sl, start, dy, r, gl, later, g1, x_state, x_totals):
    M, T, _ = cout.shape
    NC = T // CHUNK
    at = lambda m, i: NC - 1 - i
    const = lambda a: (pl.BlockSpec(a.shape, lambda m, i: (0,) * a.ndim), a)
    micro = lambda a: (pl.BlockSpec((1,) + a.shape[1:], lambda m, i: (m,) + (0,) * (a.ndim - 1)), a)
    chunk = lambda a: (pl.BlockSpec((1, CHUNK) + a.shape[2:], lambda m, i: (m, at(m, i), 0)), a)
    entry = lambda a, ahead: (pl.BlockSpec((1, 1) + a.shape[2:], lambda m, i: (m, at(m, i) + ahead, 0, 0)), a)
    inner = (pl.BlockSpec((1, 3, CHUNK, STATE), lambda m, i: (m, 0, at(m, i), 0)), info)
    sds = jax.ShapeDtypeStruct
    C = lambda width, dt: (pl.BlockSpec((1, CHUNK, width), lambda m, i: (m, at(m, i), 0)), sds((M, T, width), dt))
    S = lambda rows: (pl.BlockSpec((1, rows, XBC), lambda m, i: (m, 0, 0)), sds((M, rows, XBC), F32))
    W = lambda shape, dt: (pl.BlockSpec(shape, lambda m, i: (0,) * len(shape)), sds(shape, dt))
    V = pltpu.VMEM
    ins = [const(hp), const(cw), micro(chalo), micro(cum), chunk(cin), chunk(cout), chunk(bc), inner, entry(sl, 0), entry(sl, 1), micro(start),
           chunk(dy), chunk(r), entry(gl, 0), micro(later), const(g1), const(x_state), const(x_totals)]
    outs = [C(XBC, BF16), S(HALO), S(8), C(STATE, BF16), W((CONV, XBC), F32), W((1, XBC), F32), W((1, DIN), F32), W((2, STATE), F32),
            W(g1.shape[1:], BF16)]
    return pl.pallas_call(
        functools.partial(k3_body, ndp, nseq, M, NC),
        grid=(M, NC),
        in_specs=[b for b, _ in ins],
        out_specs=[b for b, _ in outs],
        out_shape=[o for _, o in outs],
        scratch_shapes=[V((CHUNK + 8, XBC), F32), V((CHUNK, DIN), F32), V((CHUNK, DIN), F32), V((CHUNK, DIN), BF16), V((CHUNK, DIN), BF16),
                        V((CHUNK, CHUNK), F32), V((CHUNK, DIN), F32), V((CHUNK, DIN), F32), V((CHUNK, DIN), F32), V((STATE, DIN), KIND), V(g1.shape[1:], BF16)] + list(exchange_scratch(nseq).values()) + reducer_scratch(ndp, nseq, g1.shape[1]),
        compiler_params=pltpu.CompilerParams(vmem_limit_bytes=VMEM_LIMIT, dimension_semantics=("arbitrary",) * 2, collective_id=10,
                                             has_side_effects=True),
        name="scan_backward",
    )(*[a for _, a in ins])


def k4_body(ndp, nseq, M, tok_ref, cot_hbm, params_ref, w_hbm, ws_ref, cw_ref, dgate_hbm, dcin_hbm, dstep_hbm, tail_ref, head_ref, sum1_in, *refs):
    norm_hbm, smalls, rest = refs[:M], refs[M:4 + 2 * M], refs[4 + 2 * M:]
    gtok_ref, sum1_ref, sum2_ref, small_out = rest[:4]
    g2, nxt, dc, norm_t, ngr, cot_ref, w_ref, dgate_ref, lsem, esend, erecv, hsem, hrsem = rest[4:17]
    rest = rest[7:]
    count = len(reducer_scratch(ndp, nseq, g2.shape[1]))
    reducer = Reducer(ndp, nseq, g2, sum2_ref, rest[10:10 + count])
    tiny = SmallReducer(ndp, nseq, small_out, rest[10 + count:])
    T = tok_ref.shape[1]
    dp, seq, _, _ = places()
    following, prev = lax.rem(seq + 1, nseq), lax.rem(seq + nseq - 1, nseq)
    loads = Mover(lsem)
    needed = []
    for m in range(M):
        needed += [loads.start(norm_hbm[m], norm_t.at[m], late=False),
                   loads.start(dcin_hbm.at[m, 0:T - HALO], dc.at[m, 0:T - HALO, 0:XBC], late=False),
                   loads.start(dstep_hbm.at[m], dc.at[m, :, XBC:], late=False)]
    greet(reducer.partners() + [(dp, following), (dp, prev)])
    halo = remote(head_ref, nxt, hsem, hrsem, (dp, prev))
    halo.start()
    halves_of_sum1 = reducer_like(reducer, sum1_in).halves(sum1_in, sum1_ref, (esend, erecv))
    for copy in halves_of_sum1:
        copy.start()
    for src, dst in ((w_hbm, w_ref), (dgate_hbm, dgate_ref), (cot_hbm, cot_ref)):
        loads.start(src, dst)
    rows = D // ndp
    gain = param(params_ref, "ng")
    clear_tiles(g2, rows, 15)
    for copy in needed:
        copy.wait()
    halo.wait()
    last = seq == nseq - 1
    row = iota((HALO, XBC), 0)
    for m in range(M):
        tail = tail_ref[m]
        for s in range(CONV - 1):
            extra = jnp.zeros((1, XBC), F32)
            for k in range(s + 1):
                extra = extra + cw_ref[k:k + 1] * nxt[m, s - k:s - k + 1]
            tail = tail + jnp.where(jnp.logical_and(row == HALO - CONV + 1 + s, jnp.logical_not(last)), extra, 0.0)
        dc[m, T - HALO:T, 0:XBC] = tail.astype(BF16)
    ngr[...] = jnp.zeros_like(ngr)
    dn = rest[-1]

    def backward(m, part):
        if part < D // TILE:
            cols = slice(part * TILE, (part + 1) * TILE)
            dn[:, cols] = (mm(dgate_ref[m], w_ref[0:DIN, cols]) + mm(dc[m, :, 0:XBC], w_ref[DIN:DIN + XBC, cols])
                           + mm(dc[m, :, XBC:], ws_ref[:, cols]))
        else:
            src, scale, _ = norm_rows(tok_ref[m], gain)
            unit = src * scale
            d_normed = dn[...]
            ngr[...] += jnp.sum(d_normed * unit, axis=0, keepdims=True)
            f = d_normed * gain
            mean = jnp.mean(f * unit, axis=-1, keepdims=True)
            gtok_ref[m] = (cot_ref[m].astype(F32) + scale * (f - unit * mean)).astype(BF16)

    half = (reducer.size * 2) // (rows // UNIT)
    weight_tiles(g2, rows, norm_t, dc, 0, half)
    for g in (0, 1):
        reducer.stage(0, g)
    weight_tiles(g2, rows, norm_t, dc, half, 15)
    for g in (2, 3):
        reducer.stage(0, g)
    parts = [(m, part) for m in range(M) for part in range(D // TILE + 1)]
    reducer_like(reducer, sum1_in).own_halves(sum1_in, sum1_ref)
    loads.finish()
    for k in range(1, 9):
        for stage, groups in ((k, (0, 1)), (k - 1, (2, 3))):
            if 1 <= stage <= 7:
                for g in groups:
                    reducer.stage(stage, g)
            if parts:
                backward(*parts[0])
                parts = parts[1:]
        if not parts and not tiny.begun:
            tiny.begin([[r[...] for r in group] for group in small_groups(smalls, ngr, M)])
        elif tiny.begun:
            tiny.advance()
    while not tiny.over:
        tiny.advance()
    tiny.finish()
    reducer.finish()
    for copy in halves_of_sum1:
        copy.wait()


def reducer_like(reducer, src):
    other = Refs()
    other.__class__ = Reducer
    other.__dict__.update(reducer.__dict__)
    other.size = src.shape[0] // GROUPS
    other.half = other.size // 2
    return other


def small_groups(smalls, ngr, M):
    gcw, gcb, gskip, ghead = smalls[:4]
    return [[gcw], [gcb], [ngr], list(smalls[4:4 + M]), [gskip], [ghead]]


def k4(ndp, nseq, tok, cot, params, w, ws, cw, dgate, dcin, dstep, tail, head, sum1, norm_ts, gcw, gcb, gskip, ghead, ogrs):
    M, T, _ = tok.shape
    V = pltpu.VMEM
    sds = jax.ShapeDtypeStruct
    vmem = pl.BlockSpec(memory_space=pltpu.VMEM)
    count = units(ndp, nseq, 15)
    args = (tok, cot, params, w, ws, cw, dgate, dcin, dstep, tail, head, sum1, *norm_ts, gcw, gcb, gskip, ghead, *ogrs)
    anywhere = (1, 3, 6, 7, 8) + tuple(range(12, 12 + M))
    return pl.pallas_call(
        functools.partial(k4_body, ndp, nseq, M),
        in_specs=[ANY if i in anywhere else vmem for i in range(len(args))],
        out_specs=[vmem] * 4,
        out_shape=[sds((M, T, D), BF16), sds(sum1.shape, BF16), sds((count, UNIT, STATE), BF16), sds((SMALL_ROWS, STATE), F32)],
        scratch_shapes=[V((ndp, count, UNIT, STATE), BF16), V(head.shape, F32), V((M, T, XBC + STATE), BF16), V((M, D, T), BF16), V((1, D), F32),
                        V(cot.shape, BF16), V(w.shape, BF16), V(dgate.shape, BF16), DMA((3 + 3 * M,)), DMA((GROUPS,)), DMA((GROUPS,)), DMA, DMA] + reducer_scratch(ndp, nseq, count) + small_scratch(ndp, nseq) + [V((T, D), F32)],
        compiler_params=pltpu.CompilerParams(collective_id=11, has_side_effects=True, vmem_limit_bytes=VMEM_LIMIT),
        name="projection_backward",
    )(*args)


def per_device(ndp, nseq, tokens, in_weight, out_weight, conv_weight, conv_bias, norm_gain, out_gain, skip_gain, rate_code, step_code, cotangent):
    micro, groups, T, _ = tokens.shape
    M = micro * groups
    tok = tokens.reshape(M, T, D)
    cot = cotangent.reshape(M, T, D)
    seq = lax.axis_index("seq")
    turned = in_weight.T
    pad = lambda v: jnp.pad(v.astype(F32), (0, STATE - HEADS))
    params = jnp.concatenate([norm_gain, out_gain, conv_bias, pad(rate_code), pad(step_code), pad(skip_gain)]).reshape(-1, STATE)
    if in_weight.shape[0] % STATE == 0:
        w, ws, wo, halo = open_kernel(ndp, nseq, turned, out_weight, tok)
    else:
        steps = jnp.pad(turned[DIN + XBC:], ((0, STATE - HEADS), (0, 0)))
        w, ws, wo = [lax.all_gather(v, "dp", axis=at, tiled=True) for v, at in ((turned[:DIN + XBC], 1), (steps, 1), (out_weight, 0))]
        halo = lax.ppermute(tok[:, T - HALO:], "seq", [(i, i + 1) for i in range(nseq - 1)])
    first, second = [], []
    for m in range(M):
        last = first[-1] if first else {}
        first.append(k1(nseq, m, last, tok, halo, w, ws, conv_weight, params, last.get("sdev"), last.get("totals")))
    shared = {k: first[-1][k] for k in SHARED1}
    starts = first[-1]["starts"]
    for m in range(M):
        one = dict(shared, gate=first[m]["gate"], ypart=first[m]["ypart"], starts=starts)
        traded = (first[-1]["sdev"], first[-1]["totals"]) if m == 0 else (second[-1]["gdev"], first[m - 1]["totals"])
        second.append(k2(ndp, nseq, m, one, second, tok, cot, params, wo, *traded, units(ndp, nseq, 24)))
        starts = second[0]["starts"]
    s = dict(shared, starts=starts, laters=second[-1]["laters"], g1=second[-1]["g1"], **{k: second[-1][k] for k in SHARED2})
    dcin, tail, head, dstep, gcw, gcb, gskip, ghead, sum1 = k3(
        ndp, nseq, params, conv_weight, s["chalo"], s["cum"], s["cin"], s["cout"], s["bc"], s["info"], s["sl"], s["starts"], s["dy"],
        s["rows_dot"], s["gl"], s["laters"], s["g1"], second[-1]["gdev"], first[-1]["totals"])
    mixed = s["mixed"]
    gtok, sum1, sum2, sm = k4(ndp, nseq, tok, cot, params, w, ws, conv_weight, s["dgate"], dcin, dstep, tail, head, sum1, [b["norm_t"] for b in second], gcw, gcb, gskip, ghead,
                        [b["ogr"] for b in second])
    g_in, g_out, *rest = unpack(sum1, sum2, sm, D // ndp)
    return (mixed.reshape(tokens.shape), gtok.reshape(tokens.shape), g_in.T, g_out, *rest)


def solution(mesh):
    rows, split = P("dp", None), P(None, "dp", "seq", None)
    return jax.shard_map(
        functools.partial(per_device, mesh.shape["dp"], mesh.shape["seq"]),
        mesh=mesh,
        in_specs=(split, rows, rows) + (P(),) * 7 + (split,),
        out_specs=(split, split, rows, rows) + (P(),) * 7,
        check_vma=False,
    )
```

```python
import functools

import jax
import jax.numpy as jnp
from jax import lax
from jax.experimental import pallas as pl
from jax.experimental.pallas import tpu as pltpu
from jax.sharding import PartitionSpec as P

D = 768
DIN = 1536
HEADS = 24
HEAD_DIM = 64
STATE = 128
CONV = 4
XBC = 1792
PROJ = 3352
EPS = 1e-05
LOG2E = 1.4426950408889634
CHUNK = 128
TILE = 256
HALO = 16
UNIT = 16
KIND = jnp.bfloat16
HOP_KIND = jnp.bfloat16
F32 = jnp.float32
BF16 = jnp.bfloat16
VMEM_LIMIT = 62 * 1024 * 1024


def mm(a, b):
    return lax.dot_general(a, b, (((1,), (0,)), ((), ())), preferred_element_type=F32)


def mm_nt(a, b):
    return lax.dot_general(a, b, (((1,), (1,)), ((), ())), preferred_element_type=F32)


def mm_tn(a, b):
    return lax.dot_general(a, b, (((0,), (0,)), ((), ())), preferred_element_type=F32)


def split2(v):
    hi = v.astype(BF16)
    return hi, (v - hi.astype(F32)).astype(BF16)


def split3(v):
    hi = v.astype(BF16)
    rest = v - hi.astype(F32)
    mid = rest.astype(BF16)
    return hi, mid, (rest - mid.astype(F32)).astype(BF16)


def iota(shape, dim):
    return lax.broadcasted_iota(jnp.int32, shape, dim)


def spread_matrix(start, width):
    head = iota((2 * STATE, width), 0) & (STATE - 1)
    column = (iota((2 * STATE, width), 1) + start) >> 6
    return jnp.where(head == column, 1.0, 0.0).astype(BF16)


def gather_matrix():
    return jnp.where((iota((DIN, STATE), 0) >> 6) == iota((DIN, STATE), 1), 1.0, 0.0).astype(BF16)


def spread(v, matrix):
    return mm(jnp.concatenate(split2(v), axis=1), matrix)


def head_sums(v, matrix, parts=3):
    pieces = split3(v) if parts == 3 else split2(v)
    total = mm(pieces[0], matrix)
    for piece in pieces[1:]:
        total = total + mm(piece, matrix)
    return total


def fine_nt(a, b):
    ah, al = split2(a)
    bh, bl = split2(b)
    return mm_nt(jnp.concatenate([ah, ah, al], axis=1), jnp.concatenate([bh, bl, bh], axis=1))


def halves(v):
    return jnp.concatenate(split2(v), axis=0)


def triangle(upper):
    row, column = iota((CHUNK, CHUNK), 0), iota((CHUNK, CHUNK), 1)
    keep = column >= row if upper else column <= row
    return jnp.where(keep, 1.0, 0.0).astype(BF16)


def tri_sum(tri, v):
    return mm(jnp.concatenate([tri] * 3, axis=1), jnp.concatenate(split3(v), axis=0))


PARAMS = {"ng": (0, D), "og": (6, DIN), "cb": (18, XBC), "head": (32, 3 * STATE)}


def param(ref, name):
    row, width = PARAMS[name]
    return jnp.concatenate([ref[row + i:row + i + 1] for i in range(width // STATE)], axis=1)


def head_params(params_ref):
    row = PARAMS["head"][0]
    hp = params_ref[row:row + 3]
    decay = -jnp.exp(-4.0 + 0.25 * hp[0:1])
    bias = -9.0 + 0.25 * hp[1:2]
    return decay, bias, hp


def sigmoid(v):
    return 0.5 * jnp.tanh(0.5 * v) + 0.5


def norm_rows(tok, gain):
    src = tok.astype(F32)
    scale = lax.rsqrt(jnp.mean(src * src, axis=-1, keepdims=True) + EPS)
    return src, scale, (src * scale * gain).astype(BF16)


def doubled(v):
    low = jnp.where(iota((1, STATE), 1) < HEAD_DIM, 1.0, 0.0)
    return jnp.concatenate([v * low.astype(BF16), v * (1.0 - low).astype(BF16)], axis=0)


def product_sum(left, right, cols):
    total = mm(left[0], right[0, :, cols])
    for m in range(1, left.shape[0]):
        total = total + mm(left[m], right[m, :, cols])
    return total


def put_tile(gtile_ref, d, tile, part):
    count = part.shape[0] // UNIT
    gtile_ref[d, pl.ds(tile * count, count)] = part.reshape(count, UNIT, STATE)


def clear_tiles(gtile_ref, rows, tiles):
    low, high = tiles * (rows // UNIT), gtile_ref.shape[1]
    if high > low:
        gtile_ref[:, low:] = jnp.zeros((gtile_ref.shape[0], high - low, UNIT, STATE), BF16)


def weight_tiles(gtile_ref, rows, left, right, first, end):
    def tiles(j, count):
        cols = pl.ds(pl.multiple_of(j * STATE, STATE), count * STATE)
        part = product_sum(left, right, cols).astype(BF16)
        for d in range(gtile_ref.shape[0]):
            for k in range(count):
                put_tile(gtile_ref, d, j + k, part[d * rows:(d + 1) * rows, k * STATE:(k + 1) * STATE])

    pairs = (end - first) // 2

    @pl.loop(0, pairs)
    def _(j):
        tiles(first + 2 * j, 2)

    if first + 2 * pairs < end:
        tiles(end - 1, 1)


MESH = pl.DeviceIdType.MESH
PLANE = 4
QUARTER = DIN // PLANE
DMA = pltpu.SemaphoreType.DMA


def places():
    seq = lax.axis_index("seq")
    return lax.axis_index("dp"), seq, lax.rem(seq, PLANE), lax.div(seq, PLANE)


def greet(devices):
    barrier = pltpu.get_barrier_semaphore()
    for device in devices:
        pl.semaphore_signal(barrier, inc=1, device_id=device, device_id_type=MESH)
    pl.semaphore_wait(barrier, len(devices))


def remote(src, dst, send, recv, device):
    return pltpu.make_async_remote_copy(
        src_ref=src, dst_ref=dst, send_sem=send, recv_sem=recv, device_id=device, device_id_type=MESH)


def open_body(ndp, nseq, win_ref, tok_ref, w_ref, wsall_ref, halo_ref, ws_ref, send, recv, hsend, hrecv):
    dp, seq, _, _ = places()
    nxt, prev = lax.rem(seq + 1, nseq), lax.rem(seq + nseq - 1, nseq)
    others = [lax.rem(dp + d, ndp) for d in range(1, ndp)]
    ws_ref[...] = jnp.zeros_like(ws_ref)
    ws_ref[0:HEADS] = win_ref[DIN + XBC:PROJ]
    greet([(o, seq) for o in others] + [(dp, nxt), (dp, prev)])
    T = tok_ref.shape[1]
    width = win_ref.shape[1]
    columns = pl.ds(pl.multiple_of(dp * width, width), width)
    moves = [(ws_ref, wsall_ref.at[:, columns]), (win_ref.at[0:DIN + XBC], w_ref.at[:, columns])]
    copies = [remote(tok_ref.at[:, T - HALO:T], halo_ref, hsend, hrecv, (dp, nxt))]
    for i, o in enumerate(others):
        for k, (src, dst) in enumerate(moves):
            copies.append(remote(src, dst, send.at[i, k], recv.at[i, k], (o, seq)))
    for copy in copies:
        copy.start()
    w_ref[:, columns] = win_ref[0:DIN + XBC]
    wsall_ref[:, columns] = ws_ref[...]
    for copy in copies:
        copy.wait()


def open_kernel(ndp, nseq, win, tok):
    vmem = pl.BlockSpec(memory_space=pltpu.VMEM)
    M = tok.shape[0]
    shape = lambda *s: jax.ShapeDtypeStruct(s, BF16)
    return pl.pallas_call(
        functools.partial(open_body, ndp, nseq),
        in_specs=[vmem, pl.BlockSpec(memory_space=pl.ANY)],
        out_specs=[vmem] * 3,
        out_shape=[shape(DIN + XBC, D), shape(STATE, D), shape(M, HALO, D)],
        scratch_shapes=[pltpu.VMEM((STATE, win.shape[1]), BF16), DMA((ndp - 1, 2)), DMA((ndp - 1, 2)), DMA, DMA],
        compiler_params=pltpu.CompilerParams(collective_id=1, has_side_effects=True, vmem_limit_bytes=VMEM_LIMIT),
        name="gather_weights",
    )(win, tok)


SMALL = (("cw", CONV, XBC), ("cb", 1, XBC), ("ng", 1, D), ("og", 1, DIN), ("skip", 1, DIN), ("head", 2, STATE))
SMALL_ROWS = 104


def small_pieces():
    row, found = 0, []
    for index, (_, rows, width) in enumerate(SMALL):
        for r in range(rows):
            for j in range(width // STATE):
                found.append((index, r, j, row))
                row += 1
    return found


def strided(count, body):
    step = max(s for s in range(1, 13) if count % s == 0)

    @pl.loop(0, count // step)
    def _(i):
        body(pl.multiple_of(i * step, step), step)


GROUPS = 4


def units(ndp, nseq, tiles):
    need, step = tiles * (D // ndp // UNIT), GROUPS * nseq
    return -(-need // step) * step


def reducer_scratch(ndp, nseq, count):
    Z = nseq // PLANE
    u = lambda n, *lead: tuple(lead) + (n, UNIT, STATE)
    V = pltpu.VMEM
    pairs = [DMA((GROUPS, ndp - 1))] * 2 + [DMA((GROUPS,))] * 4 + [DMA((GROUPS, Z - 1))] * 4 + [DMA((GROUPS,))] * 4
    return [V(u(count, ndp - 1), BF16), V(u(count // 2), F32), V(u(count // 2), BF16), V(u(count // 2), BF16),
            V(u(count // 4), F32), V(u(count // 4), BF16), V(u(count // 4), BF16), V(u(count // 4), BF16),
            V(u(count // 4 // Z, Z - 1), BF16)] + pairs


class Reducer:
    def __init__(self, ndp, nseq, src, out, scratch, wait_only=7):
        self.wait_only = wait_only
        self.ndp, self.Z = ndp, nseq // PLANE
        self.src, self.out = src, out
        (self.r0, self.w1, self.st1, self.r1, self.w2, self.st2, self.r2, self.st3, self.r3) = scratch[:9]
        self.sems = [(scratch[9 + 2 * k], scratch[10 + 2 * k]) for k in range(7)]
        self.dp, self.seq, self.p, self.z = places()
        x, y = lax.rem(self.p, 2), lax.div(self.p, 2)
        self.others = [lax.rem(self.dp + d, ndp) for d in range(1, ndp)]
        self.pz = [lax.rem(self.z + d, self.Z) * PLANE + self.p for d in range(1, self.Z)]
        sides = ((x, self.seq + 1 - 2 * x), (y, self.seq + 2 - 4 * y))
        self.sides = [sides if g % 2 == 0 else sides[::-1] for g in range(GROUPS)]
        self.size = src.shape[1] // GROUPS
        self.half, self.quarter = self.size // 2, self.size // 4
        self.piece = self.quarter // self.Z

    def partners(self):
        (_, px), (_, py) = self.sides[0]
        return [(o, self.seq) for o in self.others] + [(self.dp, q) for q in (px, py)] + [(self.dp, q) for q in self.pz]

    def copies(self, stage, g):
        sizes, at = self.size, g * self.size
        o1, o2, o3 = g * self.half, g * self.quarter, g * self.piece
        send, recv = self.sems[stage]
        (b1, peer1), (b2, peer2) = self.sides[g]
        half_at = at + b1 * self.half
        quarter_at = half_at + b2 * self.quarter
        piece_at = quarter_at + self.z * self.piece
        if stage == 0:
            return [remote(self.src.at[o, pl.ds(at, sizes)], self.r0.at[i, pl.ds(at, sizes)], send.at[g, i], recv.at[g, i], (o, self.seq))
                    for i, o in enumerate(self.others)]
        if stage == 1:
            span = pl.ds(o1, self.half)
            return [remote(self.st1.at[span], self.r1.at[span], send.at[g], recv.at[g], (self.dp, peer1))]
        if stage == 2:
            span = pl.ds(o2, self.quarter)
            return [remote(self.st2.at[span], self.r2.at[span], send.at[g], recv.at[g], (self.dp, peer2))]
        if stage == 3:
            return [remote(self.st3.at[pl.ds(o2 + lax.rem(self.z + d, self.Z) * self.piece, self.piece)], self.r3.at[d - 1, pl.ds(o3, self.piece)],
                           send.at[g, d - 1], recv.at[g, d - 1], (self.dp, self.pz[d - 1])) for d in range(1, self.Z)]
        if stage == 4:
            span = pl.ds(piece_at, self.piece)
            return [remote(self.out.at[span], self.out.at[span], send.at[g, d - 1], recv.at[g, d - 1], (self.dp, self.pz[d - 1]))
                    for d in range(1, self.Z)]
        span, peer = (pl.ds(quarter_at, self.quarter), peer2) if stage == 5 else (pl.ds(half_at, self.half), peer1)
        return [remote(self.out.at[span], self.out.at[span], send.at[g], recv.at[g], (self.dp, peer))]

    def stage(self, stage, g):
        if stage > 0:
            for copy in self.copies(stage - 1, g):
                copy.wait_recv()
        if stage == self.wait_only:
            return
        (b1, _), (b2, _) = self.sides[g]
        at, o1, o2, o3 = g * self.size, g * self.half, g * self.quarter, g * self.piece
        if stage == 1:
            def total(i, c):
                v = self.src[self.dp, pl.ds(at + i, c)].astype(F32)
                for k in range(self.ndp - 1):
                    v = v + self.r0[k, pl.ds(at + i, c)].astype(F32)
                return v

            def body(i, c):
                self.w1[pl.ds(o1 + i, c)] = total(b1 * self.half + i, c)
                self.st1[pl.ds(o1 + i, c)] = total((1 - b1) * self.half + i, c).astype(BF16)
            strided(self.half, body)
        elif stage == 2:
            def body(i, c):
                keep, give = pl.ds(o1 + b2 * self.quarter + i, c), pl.ds(o1 + (1 - b2) * self.quarter + i, c)
                self.w2[pl.ds(o2 + i, c)] = self.w1[keep] + self.r1[keep].astype(F32)
                self.st2[pl.ds(o2 + i, c)] = (self.w1[give] + self.r1[give].astype(F32)).astype(BF16)
            strided(self.quarter, body)
        elif stage == 3:
            def body(i, c):
                span = pl.ds(o2 + i, c)
                v = self.w2[span] + self.r2[span].astype(F32)
                self.w2[span] = v
                self.st3[span] = v.astype(BF16)
            strided(self.quarter, body)
        elif stage == 4:
            v = self.w2[pl.ds(o2 + self.z * self.piece, self.piece)]
            for d in range(self.Z - 1):
                v = v + self.r3[d, pl.ds(o3, self.piece)].astype(F32)
            self.out[pl.ds(at + b1 * self.half + b2 * self.quarter + self.z * self.piece, self.piece)] = v.astype(BF16)
        for copy in self.copies(stage, g):
            copy.start()

    def at(self, k, table):
        for stage in range(self.wait_only + 1):
            for row, groups in ((0, (0, 1)), (1, (2, 3))):
                if table[row][stage] == k:
                    for g in groups:
                        self.stage(stage, g)

    def halves(self, src, out, sems):
        found = []
        for g in range(GROUPS):
            (b1, peer), _ = self.sides[g]
            span = pl.ds(g * self.size + b1 * self.half, self.half)
            found.append(remote(src.at[span], out.at[span], sems[0].at[g], sems[1].at[g], (self.dp, peer)))
        return found

    def own_halves(self, src, out):
        for g in range(GROUPS):
            (b1, _), _ = self.sides[g]
            at = g * self.size + b1 * self.half

            def body(i, c):
                out[pl.ds(at + i, c)] = src[pl.ds(at + i, c)]
            strided(self.half, body)

    def finish(self):
        for stage in range(self.wait_only):
            for g in range(GROUPS):
                for copy in self.copies(stage, g):
                    copy.wait_send()


def small_scratch(ndp, nseq):
    Z = nseq // PLANE
    V = pltpu.VMEM
    shape = (SMALL_ROWS, STATE)
    count = ndp - 1 + 2 + Z - 1
    return [V((ndp,) + shape, F32), V((2,) + shape, F32), V((2,) + shape, F32), V((Z,) + shape, F32), DMA((count,)), DMA((count,))]


class SmallReducer:
    def __init__(self, ndp, nseq, out, scratch):
        self.out = out
        self.bufs, (self.send, self.recv) = scratch[:4], scratch[4:6]
        dp, seq, p, z = places()
        Z = nseq // PLANE
        x, y = lax.rem(p, 2), lax.div(p, 2)
        self.z, self.Z = z, Z
        self.peers = [[(lax.rem(dp + d, ndp), seq) for d in range(1, ndp)], [(dp, seq + 1 - 2 * x)], [(dp, seq + 2 - 4 * y)],
                      [(dp, lax.rem(z + d, Z) * PLANE + p) for d in range(1, Z)]]
        self.at, self.begun, self.over, self.started = 0, False, False, []

    def send_all(self):
        buf = self.bufs[self.at]
        base = sum(len(q) for q in self.peers[:self.at])
        self.flying = [remote(buf.at[0], buf.at[1 + k], self.send.at[base + k], self.recv.at[base + k], device)
                       for k, device in enumerate(self.peers[self.at])]
        for copy in self.flying:
            copy.start()
        self.started += self.flying

    def begin(self, groups):
        buf = self.bufs[0]
        buf[0] = jnp.zeros(buf.shape[1:], F32)
        for index, r, j, row in small_pieces():
            v = groups[index][0][r:r + 1, j * STATE:(j + 1) * STATE]
            for other in groups[index][1:]:
                v = v + other[r:r + 1, j * STATE:(j + 1) * STATE]
            buf[0, row:row + 1] = v
        self.begun = True
        self.send_all()

    def advance(self):
        if self.over:
            return
        for copy in self.flying:
            copy.wait_recv()
        buf = self.bufs[self.at]
        if self.at < 3:
            v = buf[0]
            for k in range(1, buf.shape[0]):
                v = v + buf[k]
            self.at += 1
            self.bufs[self.at][0] = v
            self.send_all()
            return
        v = None
        for k in range(self.Z):
            piece = buf[lax.rem(self.z - k + self.Z, self.Z)]
            v = piece if v is None else v + piece
        self.out[...] = v
        self.over = True

    def finish(self):
        for copy in self.started:
            copy.wait_send()


def unpack_body(g1_ref, g2_ref, sm_ref, gin_hbm, gout_hbm, cw_ref, cb_ref, ng_ref, og_ref, skip_ref, rate_ref, step_ref, gin_ref, gout_ref, sems):
    R = gin_ref.shape[1]
    moves = Mover(sems)
    U = R // UNIT
    tile = lambda ref, j: ref[j * U:(j + 1) * U].astype(F32).reshape(R, STATE)
    eye = jnp.where(iota((STATE, STATE), 0) == iota((STATE, STATE), 1), 1.0, 0.0).astype(BF16)
    turned = lambda ref, j: mm_nt(eye, ref[j * U:(j + 1) * U].reshape(R, STATE))
    for low, source, first, count in ((0, g1_ref, 0, 12), (DIN, g2_ref, 0, 14)):
        for j in range(count):
            rows = slice(low + j * STATE, low + (j + 1) * STATE)
            gin_ref[rows] = turned(source, first + j)
            moves.start(gin_ref.at[rows], gin_hbm.at[rows])
    gin_ref[DIN + XBC:] = turned(g2_ref, 14)[:HEADS]
    moves.start(gin_ref.at[DIN + XBC:PROJ], gin_hbm.at[DIN + XBC:PROJ])
    for half in range(2):
        rows = slice(half * R, (half + 1) * R)
        for j in range(D // STATE):
            gout_ref[rows, j * STATE:(j + 1) * STATE] = tile(g1_ref, 12 + half * 6 + j)
        moves.start(gout_ref.at[rows], gout_hbm.at[rows])
    outs = {1: cb_ref, 2: ng_ref, 3: og_ref}
    low, high = iota((1, STATE), 1) < HEAD_DIM, iota((1, STATE), 1)
    lane = iota((1, STATE), 1)
    skip = jnp.zeros((1, STATE), F32)
    for index, r, j, row in small_pieces():
        v = sm_ref[row:row + 1]
        if index == 0:
            cw_ref[r:r + 1, j * STATE:(j + 1) * STATE] = v
        elif index in outs:
            outs[index][j * STATE:(j + 1) * STATE] = v[0]
        elif index == 4:
            left = jnp.sum(jnp.where(low, v, 0.0), axis=1, keepdims=True)
            right = jnp.sum(jnp.where(low, 0.0, v), axis=1, keepdims=True)
            skip = skip + jnp.where(lane == 2 * j, left, 0.0) + jnp.where(lane == 2 * j + 1, right, 0.0)
        else:
            (rate_ref, step_ref)[r][...] = v[0, :HEADS]
    skip_ref[...] = skip[0, :HEADS]
    moves.finish()


def unpack(g1, g2, sm, R):
    vmem = pl.BlockSpec(memory_space=pltpu.VMEM)
    sds = lambda *s: jax.ShapeDtypeStruct(s, F32)
    return pl.pallas_call(
        unpack_body,
        in_specs=[vmem] * 3,
        out_specs=[pl.BlockSpec(memory_space=pl.ANY)] * 2 + [vmem] * 7,
        scratch_shapes=[pltpu.VMEM((PROJ, R), F32), pltpu.VMEM((2 * R, D), F32), DMA((32,))],
        out_shape=[sds(PROJ, R), sds(2 * R, D), sds(CONV, XBC), sds(XBC), sds(D), sds(DIN), sds(HEADS), sds(HEADS), sds(HEADS)],
        compiler_params=pltpu.CompilerParams(vmem_limit_bytes=VMEM_LIMIT),
        name="unpack_gradients",
    )(g1, g2, sm)
VMEM = pl.BlockSpec(memory_space=pltpu.VMEM)
ANY = pl.BlockSpec(memory_space=pl.ANY)


class Refs:
    pass


def run(name, body, ins, outs, scratch, carried=(), collective_id=None):
    names = list(ins) + list(outs) + list(scratch)
    aliases = {list(ins).index(k): list(outs).index(k) for k in carried}

    def kernel(*refs):
        r = Refs()
        for k, ref in zip(names, refs):
            setattr(r, k, ref)
        body(r)

    params = dict(vmem_limit_bytes=VMEM_LIMIT)
    if collective_id is not None:
        params.update(collective_id=collective_id, has_side_effects=True)
    got = pl.pallas_call(
        kernel,
        in_specs=[s for s, _ in ins.values()],
        out_specs=[s for s, _ in outs.values()],
        out_shape=[s for _, s in outs.values()],
        scratch_shapes=list(scratch.values()),
        input_output_aliases=aliases,
        compiler_params=pltpu.CompilerParams(**params),
        name=name,
    )(*[a for _, a in ins.values()])
    return dict(zip(outs, got))


class Mover:
    def __init__(self, sems):
        self.sems, self.count, self.flying = sems, 0, []

    def start(self, src, dst, late=True):
        copy = pltpu.make_async_copy(src, dst, self.sems.at[self.count])
        self.count += 1
        copy.start()
        if late:
            self.flying.append(copy)
        return copy

    def finish(self):
        for copy in self.flying:
            copy.wait()


def exchange_scratch(nseq):
    V = pltpu.VMEM
    Z = nseq // PLANE
    quarter = (STATE, QUARTER)
    return dict(x_out=V((STATE, DIN), KIND), x_got=V((PLANE,) + quarter, F32), x_tots=V((PLANE, 8, STATE), F32), x_pre=V(quarter, F32),
                x_zin=V((Z,) + quarter, HOP_KIND), x_ztots=V((Z, 8, STATE), F32), x_back=V((PLANE,) + quarter, KIND),
                x_ts=DMA((3,)), x_tr=DMA((3,)), x_s=DMA((2, 3)), x_r=DMA((2, 3)), x_zs=DMA((2, Z - 1)), x_zr=DMA((2, Z - 1)), x_zts=DMA((Z - 1,)),
                x_ztr=DMA((Z - 1,)), x_bs=DMA((2, 3)), x_br=DMA((2, 3)))


class Exchange:
    def __init__(self, nseq, upward, state, totals, r):
        self.upward, self.state, self.totals, self.r = upward, state, totals, r
        self.dp, self.seq, self.p, self.z = places()
        self.Z = nseq // PLANE
        self.base = self.z * PLANE
        self.peers = [lax.rem(self.p + d, PLANE) for d in range(PLANE)]
        self.line = [(self.dp, lax.rem(self.z + d, self.Z) * PLANE + self.p) for d in range(1, self.Z)]
        self.greeted = [(self.dp, self.base + q) for q in self.peers[1:]] + self.line
        self.steps = 7
        self.at = 0

    def columns(self, q):
        return pl.ds(pl.multiple_of(q * QUARTER, QUARTER), QUARTER)

    def rows(self, part):
        return pl.ds(part * (STATE // 2), STATE // 2)

    def first(self, part):
        r = self.r
        found = []
        for d in range(1, PLANE):
            to = (self.dp, self.base + self.peers[d])
            if part == 0:
                found.append(remote(self.totals, r.x_tots.at[d], r.x_ts.at[d - 1], r.x_tr.at[d - 1], to))
            found.append(remote(self.state.at[self.rows(part), self.columns(self.peers[d])], r.x_got.at[d, self.rows(part)], r.x_s.at[part, d - 1],
                                r.x_r.at[part, d - 1], to))
        return found

    def along(self, part, d):
        r = self.r
        to = (self.dp, lax.rem(self.z + (self.Z - d if self.upward else d), self.Z) * PLANE + self.p)
        copies = [remote(r.x_zin.at[0, self.rows(part)], r.x_zin.at[d, self.rows(part)], r.x_zs.at[part, d - 1], r.x_zr.at[part, d - 1], to)]
        if part == 0:
            copies.append(remote(r.x_ztots.at[0], r.x_ztots.at[d], r.x_zts.at[d - 1], r.x_ztr.at[d - 1], to))
        sends = self.z >= d if self.upward else self.z + d < self.Z
        receives = self.z + d < self.Z if self.upward else self.z >= d
        return copies, sends, receives

    def last(self, part):
        r = self.r
        return [remote(r.x_back.at[d, self.rows(part)], r.x_out.at[self.rows(part), self.columns(self.p)], r.x_bs.at[part, d - 1],
                       r.x_br.at[part, d - 1], (self.dp, self.base + lax.rem(self.p + PLANE - d, PLANE))) for d in range(1, PLANE)]

    def turn(self):
        order = range(PLANE - 1, -1, -1) if self.upward else range(PLANE)
        slots = [lax.rem(self.p - q + PLANE, PLANE) for q in order]
        return slots, spread_matrix(self.p * QUARTER, QUARTER)

    def begin(self):
        r = self.r
        for copy in self.first(0):
            copy.start()
        r.x_tots[0] = self.totals[...]
        r.x_got[0] = self.state[:, self.columns(self.p)]

    def plane(self, part):
        r = self.r
        for copy in self.first(part):
            copy.wait_recv()
        slots, matrix = self.turn()
        total = jnp.zeros((STATE // 2, QUARTER), F32)
        for slot in slots:
            total = spread(jnp.exp2(r.x_tots[slot]), matrix)[0:1] * total + r.x_got[slot, self.rows(part)].astype(F32)
        r.x_zin[0, self.rows(part)] = total.astype(HOP_KIND)
        if part == 0:
            r.x_ztots[0] = r.x_tots[0] + r.x_tots[1] + r.x_tots[2] + r.x_tots[3]
        for d in range(1, self.Z):
            copies, sends, _ = self.along(part, d)

            @pl.when(sends)
            def _():
                for copy in copies:
                    copy.start()

    def give(self, part):
        r = self.r
        rows = self.rows(part)
        slots, matrix = self.turn()
        r.x_pre[rows] = jnp.zeros((STATE // 2, QUARTER), F32)
        for d in range(self.Z - 1, 0, -1):
            copies, _, receives = self.along(part, d)

            @pl.when(receives)
            def _():
                for copy in copies:
                    copy.wait_recv()
                r.x_pre[rows] = spread(jnp.exp2(r.x_ztots[d]), matrix)[0:1] * r.x_pre[rows] + r.x_zin[d, rows].astype(F32)
        total = r.x_pre[rows]
        for slot in slots:
            r.x_back[slot, rows] = total.astype(KIND)
            total = spread(jnp.exp2(r.x_tots[slot]), matrix)[0:1] * total + r.x_got[slot, rows].astype(F32)
        for copy in self.last(part):
            copy.start()
        r.x_out[rows, self.columns(self.p)] = r.x_back[0, rows]

    def end(self):
        for part in range(2):
            for copy in self.last(part):
                copy.wait_recv()
        for part in range(2):
            for copy in self.first(part) + self.last(part):
                copy.wait_send()
            for d in range(1, self.Z):
                copies, sends, _ = self.along(part, d)

                @pl.when(sends)
                def _():
                    for copy in copies:
                        copy.wait_send()

    def step(self, k):
        if k == 0:
            self.begin()
        elif k == 1:
            for copy in self.first(1):
                copy.start()
        elif k in (2, 3):
            self.plane(k - 2)
        elif k in (4, 5):
            self.give(k - 4)
        else:
            self.end()

    def tick(self):
        if self.at < self.steps:
            self.step(self.at)
            self.at += 1

    def finish(self):
        while self.at < self.steps:
            self.tick()


class NoExchange:
    def tick(self):
        pass

    finish = tick


def chunks(T):
    return [(c, slice(c * CHUNK, (c + 1) * CHUNK)) for c in range(T // CHUNK)]


SHARED1 = ("cin", "cout", "bc", "info", "sl", "cum", "chalo")


def k1_body(ndp, nseq, m, ahead, r):
    T = r.gate_v.shape[0]
    NC = T // CHUNK
    moves = Mover(r.sems)
    loads = [moves.start(r.tok.at[m], r.tok_v, late=False), moves.start(r.w, r.w_v, late=False)]
    trade = NoExchange()
    if ahead:
        trade = Exchange(nseq, False, r.x_state, r.x_totals, r)
    weights = []
    if m == 1:
        dp, seq, _, _ = places()
        count = r.wout.shape[0]
        mine = pl.ds(pl.multiple_of(dp * count, count), count)
        others = [(lax.rem(dp + d, ndp), seq) for d in range(1, ndp)]
        greet(trade.greeted + others)
        weights = [remote(r.wout, r.wo_land.at[mine], r.w_send.at[i], r.w_recv.at[i], o) for i, o in enumerate(others)]
    elif ahead:
        greet(trade.greeted)
    trade.tick()
    for copy in weights:
        copy.start()
    decay, bias, hp = head_params(r.params)
    decay2 = decay * LOG2E
    gain = param(r.params, "ng")
    r.cb[...] = param(r.params, "cb")
    first = lax.axis_index("seq") == 0
    r.an[0:HALO] = jnp.where(first, 0.0, norm_rows(r.halo[m], gain)[2].astype(F32)).astype(BF16)
    loads[0].wait()
    r.an[HALO:] = norm_rows(r.tok_v[...], gain)[2]
    arg = mm_nt(r.an[HALO:], r.ws[...]) + bias
    dt = jnp.maximum(arg, 0.0) + jnp.log1p(jnp.exp(-jnp.abs(arg)))
    r.info_v[0] = arg
    r.info_v[1] = dt
    r.dt2[...] = jnp.concatenate(split2(dt), axis=1)
    tri = triangle(False)
    ends = []
    for c, rows in chunks(T):
        lc = tri_sum(tri, dt[rows] * decay2)
        r.info_v[2, rows] = lc
        ends.append(lc[CHUNK - 1:CHUNK])
        r.tw2[rows] = jnp.concatenate(split2(jnp.exp2(lc[CHUNK - 1:CHUNK] - lc)), axis=1)
    before, after = jnp.zeros((1, STATE), F32), jnp.zeros((1, STATE), F32)
    for c in range(NC + 1):
        r.cum_v[0, c:c + 1] = before
        r.cum_v[1, NC - c:NC - c + 1] = after
        if c < NC:
            before, after = before + ends[c], after + ends[NC - 1 - c]
    r.totals[...] = jnp.broadcast_to(before, (8, STATE))
    trade.tick()
    moves.start(r.info_v, r.info.at[m])
    moves.start(r.cum_v, r.cum.at[m])
    loads[1].wait()

    def conv_tile(j, cols):
        wcols = pl.ds(pl.multiple_of(DIN + j * TILE, TILE), TILE)
        raw = mm_nt(r.an[...], r.w_v[wcols, :])
        r.cpad[...] = raw
        r.cin_v[:, cols] = raw[HALO:].astype(BF16)
        r.chalo_v[:, cols] = raw[:HALO]
        out = r.cb[:, cols]
        for k in range(CONV):
            out = out + r.cw[k:k + 1, cols] * r.cpad[HALO - CONV + 1 + k:HALO - CONV + 1 + k + T]
        r.cout_v[:, cols] = out
        for k, name in enumerate(("cin", "cout")):
            pltpu.make_async_copy(getattr(r, name + "_v").at[:, cols], getattr(r, name).at[m, :, cols], r.tsems.at[k, j]).start()
        return out * sigmoid(out)

    def x_tile(j):
        cols = pl.ds(pl.multiple_of(j * TILE, TILE), TILE)
        x = conv_tile(j, cols)
        matrix = spread_matrix(j * TILE, TILE)
        ux = x * mm(r.dt2[...], matrix)
        r.u[:, cols] = ux.astype(BF16)
        hi, lo = split2(ux * mm(r.tw2[...], matrix))
        for c, rows in chunks(T):
            r.ub[c, 0:CHUNK, cols] = hi[rows]
            r.ub[c, CHUNK:, cols] = lo[rows]
        skip_tile = spread(jnp.broadcast_to(hp[2:3], (8, STATE)), matrix)[0:1]
        r.ypart_v[:, cols] = x * skip_tile

    pl.loop(0, DIN // TILE // 2 + 1)(x_tile)
    trade.tick()
    pl.loop(DIN // TILE // 2 + 1, DIN // TILE)(x_tile)
    if m == 1:
        r.wo_land[mine] = r.wout[...]
    r.bc_v[...] = conv_tile(DIN // TILE, pl.ds(DIN, TILE))
    moves.start(r.chalo_v, r.chalo.at[m])
    moves.start(r.bc_v, r.bc.at[m])
    trade.tick()
    if m == 1:
        for copy in weights:
            copy.wait_recv()
        moves.start(r.wo_land, r.wo)
    matrix = spread_matrix(0, DIN)
    state = jnp.zeros((STATE, DIN), F32)
    for c, rows in chunks(T):
        b16 = r.bc_v[rows, 0:STATE].astype(BF16)
        r.sl_v[c] = state
        keep = spread(jnp.exp2(jnp.broadcast_to(ends[c], (8, STATE))), matrix)[0:1]
        state = keep * state + mm_tn(jnp.concatenate([b16, b16], axis=0), r.ub[c])
    r.sl_v[NC] = state
    r.sdev[...] = state
    moves.start(r.sl_v, r.sl.at[m])

    @pl.loop(0, DIN // TILE)
    def _(j):
        cols = pl.ds(pl.multiple_of(j * TILE, TILE), TILE)
        r.gate_v[:, cols] = mm_nt(r.an[HALO:], r.w_v[cols, :])
        pltpu.make_async_copy(r.gate_v.at[:, cols], r.gate.at[:, cols], r.tsems.at[2, j]).start()
    trade.tick()

    causal = iota((CHUNK, CHUNK), 0) >= iota((CHUNK, CHUNK), 1)
    for c, rows in chunks(T):
        gram = jnp.where(causal, fine_nt(r.bc_v[rows, STATE:2 * STATE], r.bc_v[rows, 0:STATE]), 0.0)
        lc = r.info_v[2, rows]
        lct = lc.T
        for p in range(HEADS // 2):
            cols = slice(p * STATE, (p + 1) * STATE)
            mixes = []
            for h in (2 * p, 2 * p + 1):
                gap = lc[:, h:h + 1] - lct[h:h + 1, :]
                mixes.append((gram * jnp.exp2(jnp.minimum(gap, 0.0))).astype(BF16))
            r.ypart_v[rows, cols] = r.ypart_v[rows, cols] + mm(jnp.concatenate(mixes, axis=1), doubled(r.u[rows, cols]))
        moves.start(r.ypart_v.at[rows], r.ypart.at[rows])
        if c == NC // 2:
            trade.tick()
    trade.finish()
    if ahead:
        moves.start(r.x_out, r.starts.at[m - 1])
    moves.finish()
    for copy in weights:
        copy.wait_send()
    for k, (src, dst) in enumerate(((r.cin_v, r.cin.at[m]), (r.cout_v, r.cout.at[m]), (r.gate_v, r.gate))):
        for j in range(src.shape[1] // TILE):
            cols = slice(j * TILE, (j + 1) * TILE)
            pltpu.make_async_copy(src.at[:, cols], dst.at[:, cols], r.tsems.at[k, j]).wait()


def k1(ndp, nseq, m, carried, tok, halo, w, ws, wout, cw, params, sdev=None, totals=None):
    M, T, _ = tok.shape
    NC = T // CHUNK
    V = pltpu.VMEM
    sds = jax.ShapeDtypeStruct
    ahead = m > 0
    ins = dict(tok=(ANY, tok), w=(ANY, w), halo=(VMEM, halo), ws=(VMEM, ws), cw=(VMEM, cw), params=(VMEM, params))
    shapes = dict(cin=(T, XBC), cout=(T, XBC), bc=(T, 2 * STATE), info=(3, T, STATE), sl=(NC + 1, STATE, DIN), cum=(2, NC + 1, STATE),
                  chalo=(HALO, XBC))
    kinds = {k: BF16 if k == "cin" else F32 for k in SHARED1}
    outs = {k: (ANY, sds((M,) + shapes[k], kinds[k])) for k in SHARED1}
    outs.update(gate=(ANY, sds((T, DIN), F32)), ypart=(ANY, sds((T, DIN), F32)), sdev=(VMEM, sds((STATE, DIN), F32)),
                totals=(VMEM, sds((8, STATE), F32)))
    scratch = dict(cb=V((1, XBC), F32), tok_v=V((T, D), BF16), w_v=V(w.shape, BF16), cpad=V((HALO + T, TILE), F32), an=V((HALO + T, D), BF16), u=V((T, DIN), BF16),
                   ub=V((NC, 2 * CHUNK, DIN), BF16), dt2=V((T, 2 * STATE), BF16), tw2=V((T, 2 * STATE), BF16),
                   gate_v=V((T, DIN), F32), ypart_v=V((T, DIN), F32), sems=DMA((20 + NC,)), tsems=DMA((3, XBC // TILE)),
                   **{k + "_v": V(shapes[k], kinds[k]) for k in SHARED1})
    if ahead:
        ins.update({k: (ANY, carried[k]) for k in SHARED1}, x_state=(VMEM, sdev), x_totals=(VMEM, totals))
        outs.update(starts=(ANY, sds((M, STATE, DIN), KIND)))
        if m > 1:
            ins.update(starts=(ANY, carried["starts"]))
        scratch.update(exchange_scratch(nseq))
    if m == 1:
        ins.update(wout=(VMEM, wout))
        outs.update(wo=(ANY, sds((DIN, D), BF16)))
        scratch.update(wo_land=V((DIN, D), BF16), w_send=DMA((ndp - 1,)), w_recv=DMA((ndp - 1,)))
    keep = [k for k in SHARED1 + ("starts",) if k in ins]
    return run("forward_local", functools.partial(k1_body, ndp, nseq, m, ahead), ins, outs, scratch, keep, collective_id=1 + m if ahead else None)


SHARED2 = ("mixed", "dgate", "dy", "rows_dot", "gl")


def k2_body(nseq, M, m, kind, r):
    T = r.gate_v.shape[0]
    NC = T // CHUNK
    moves = Mover(r.sems)
    loads = {}
    for k, src in (("start", r.starts_in.at[m]), ("info", r.info.at[m]), ("cum", r.cum.at[m]), ("bc", r.bc.at[m]), ("sl", r.sl.at[m, 0:NC]),
                   ("ypart", r.ypart), ("gate", r.gate), ("tok", r.tok.at[m]), ("wo", r.wo), ("cot", r.cot.at[m])):
        loads[k] = moves.start(src, getattr(r, k + "_v"), late=False)
    upward = kind == "later"
    trade = Exchange(nseq, upward, r.x_state, r.x_totals, r)
    greet(trade.greeted)
    trade.tick()
    matrix = spread_matrix(0, DIN)
    gather = gather_matrix()
    loads["tok"].wait()
    r.norm_t[...] = norm_rows(r.tok_v[...], param(r.params, "ng"))[2].T
    og = param(r.params, "og")
    loads["cot"].wait()
    loads["wo"].wait()
    trade.tick()

    @pl.loop(0, DIN // TILE)
    def _(j):
        cols = pl.ds(pl.multiple_of(j * TILE, TILE), TILE)
        r.dbr[:, cols] = mm_nt(r.cot_v[...], r.wo_v[cols, :])

    for k in ("start", "info", "cum", "bc", "sl", "ypart", "gate"):
        loads[k].wait()
    trade.tick()
    for c, rows in chunks(T):
        keep = spread(jnp.exp2(jnp.broadcast_to(r.cum_v[0, c:c + 1], (8, STATE))), matrix)[0:1]
        state = halves(r.sl_v[c] + keep * r.start_v[...].astype(F32))
        c16 = r.bc_v[rows, STATE:2 * STATE].astype(BF16)
        lift = spread(jnp.exp2(r.info_v[2, rows]), matrix)
        yc = r.ypart_v[rows] + lift * mm(jnp.concatenate([c16, c16], axis=1), state)
        r.ypart_v[rows] = yc
        g = r.gate_v[rows]
        gated = yc * (g * sigmoid(g))
        scale = lax.rsqrt(jnp.mean(gated * gated, axis=-1, keepdims=True) + EPS)
        r.oscale[rows] = jnp.broadcast_to(scale, (CHUNK, STATE))
        r.branch[rows] = (gated * scale * og).astype(BF16)
        if c == 1:
            trade.tick()
    r.branch_t[...] = r.branch[...].T
    for j in range(D // TILE):
        cols = slice(j * TILE, (j + 1) * TILE)
        r.mixed_v[:, cols] = (r.tok_v[:, cols].astype(F32) + mm(r.branch[...], r.wo_v[:, cols])).astype(BF16)
    moves.start(r.mixed_v, r.mixed.at[m])
    trade.tick()
    r.ogr[...] = jnp.zeros_like(r.ogr)
    r.gdev[...] = jnp.zeros_like(r.gdev)
    for c, rows in reversed(chunks(T)):
        g = r.gate_v[rows]
        yc = r.ypart_v[rows]
        db = r.dbr[rows]
        scale = r.oscale[rows][:, 0:1]
        sig = sigmoid(g)
        act = g * sig
        gated = yc * act
        unit = gated * scale
        r.ogr[...] += jnp.sum(db * unit, axis=0, keepdims=True)
        e = db * og
        mean = jnp.mean(e * unit, axis=-1, keepdims=True)
        dgated = scale * (e - unit * mean)
        r.dgate_v[rows] = (dgated * yc * (sig * (1.0 + g * (1.0 - sig)))).astype(BF16)
        high, low = split2(dgated * act)
        dyf = high.astype(F32) + low.astype(F32)
        r.dy_v[rows] = dyf
        r.rows_dot_v[rows] = head_sums(dyf * yc, gather)
        lc = r.info_v[2, rows]
        lifted = halves(dyf * spread(jnp.exp2(lc), matrix))
        c16 = r.bc_v[rows, STATE:2 * STATE].astype(BF16)
        r.gl_v[c] = r.gdev[...]
        keep = spread(jnp.exp2(jnp.broadcast_to(lc[CHUNK - 1:CHUNK], (8, STATE))), matrix)[0:1]
        r.gdev[...] = keep * r.gdev[...] + mm_tn(jnp.concatenate([c16, c16], axis=0), lifted)
        moves.start(r.dy_v.at[rows], r.dy.at[m, rows])
        moves.start(r.gl_v.at[c], r.gl.at[m, c])
        if c == NC - 2:
            trade.tick()
    moves.start(r.dgate_v, r.dgate.at[m])
    moves.start(r.rows_dot_v, r.rows_dot.at[m])
    if m == M - 1:
        early_grads(r)
    trade.finish()
    if upward:
        moves.start(r.x_out, r.laters.at[m - 1])
    else:
        moves.start(r.x_out, r.starts.at[M - 1])
    moves.finish()


def early_grads(r):
    dp = r.g1.shape[0]
    rows = D // dp
    r.extra.finish()
    clear_tiles(r.g1, rows, 24)

    def summed(lefts, rights, cols):
        total = None
        for left, right in zip(lefts, rights):
            part = mm(left[...], right[:, cols])
            total = part if total is None else total + part
        return total.astype(BF16)

    @pl.loop(0, DIN // TILE)
    def _(j):
        part = summed(r.norm_ts + [r.norm_t], r.dgates + [r.dgate_v], pl.ds(pl.multiple_of(j * TILE, TILE), TILE))
        for d in range(dp):
            for k in range(TILE // STATE):
                put_tile(r.g1, d, j * (TILE // STATE) + k, part[d * rows:(d + 1) * rows, k * STATE:(k + 1) * STATE])

    @pl.loop(0, D // TILE)
    def _(j):
        part = summed(r.branch_ts + [r.branch_t], r.cots + [r.cot_v], pl.ds(pl.multiple_of(j * TILE, TILE), TILE))
        for d in range(dp):
            for half in range(2):
                low = (2 * d + half) * rows
                for k in range(TILE // STATE):
                    put_tile(r.g1, d, 12 + half * 6 + j * (TILE // STATE) + k, part[low:low + rows, k * STATE:(k + 1) * STATE])


def k2(ndp, nseq, m, one, before, tok, cot, params, wo, state, totals, count):
    M, T, _ = tok.shape
    NC = T // CHUNK
    V = pltpu.VMEM
    sds = jax.ShapeDtypeStruct
    kind = "earlier" if m == 0 else "later"
    ins = dict(tok=(ANY, tok), cot=(ANY, cot), wo=(ANY, wo), params=(VMEM, params), info=(ANY, one["info"]), cum=(ANY, one["cum"]),
               bc=(ANY, one["bc"]), sl=(ANY, one["sl"]), ypart=(ANY, one["ypart"]), gate=(ANY, one["gate"]),
               x_state=(VMEM, state), x_totals=(VMEM, totals))
    shapes = dict(mixed=((T, D), BF16), dgate=((T, DIN), BF16), dy=((T, DIN), F32), rows_dot=((T, STATE), F32), gl=((NC, STATE, DIN), F32))
    outs = {k: (ANY, sds((M,) + s, t)) for k, (s, t) in shapes.items()}
    outs.update(gdev=(VMEM, sds((STATE, DIN), F32)), ogr=(VMEM, sds((1, DIN), F32)))
    scratch = dict(tok_v=V((T, D), BF16), cot_v=V((T, D), BF16), wo_v=V(wo.shape, BF16), info_v=V((3, T, STATE), F32), cum_v=V((2, NC + 1, STATE), F32),
                   bc_v=V((T, 2 * STATE), F32), sl_v=V((NC, STATE, DIN), F32), ypart_v=V((T, DIN), F32), gate_v=V((T, DIN), F32),
                   start_v=V((STATE, DIN), KIND), dbr=V((T, DIN), F32), branch=V((T, DIN), BF16), oscale=V((T, STATE), F32),
                   sems=DMA((20 + 2 * NC,)), **{k + "_v": V(s, t) for k, (s, t) in shapes.items()})
    scratch.update(exchange_scratch(nseq))
    last = m == M - 1
    turned = dict(branch_t=sds((DIN, T), BF16), norm_t=sds((D, T), BF16))
    if last:
        scratch.update(branch_t=V((DIN, T), BF16))
        outs.update(norm_t=(VMEM, turned["norm_t"]))
        outs.update(g1=(VMEM, sds((ndp, count, UNIT, STATE), BF16)))
        for i, b in enumerate(before):
            for k in turned:
                ins[k + str(i)] = (VMEM, b[k])
            scratch["dgate_e%d" % i] = V((T, DIN), BF16)
            scratch["cot_e%d" % i] = V((T, D), BF16)
    else:
        outs.update({k: (VMEM, s) for k, s in turned.items()})
    keep = []
    if m == 0:
        ins.update(starts=(ANY, one["starts"]))
        outs.update(starts=(ANY, sds(one["starts"].shape, KIND)))
        keep += ["starts"]
    else:
        ins.update({k: (ANY, before[-1][k]) for k in SHARED2}, starts_in=(ANY, one["starts"]))
        outs.update(laters=(ANY, sds((M, STATE, DIN), KIND)))
        keep += list(SHARED2)
        if m > 1:
            ins.update(laters=(ANY, before[-1]["laters"]))
            keep += ["laters"]

    def body(r):
        if m == 0:
            r.starts_in = r.starts
        if last:
            named = lambda k: [getattr(r, k + str(i)) for i in range(len(before))]
            r.norm_ts, r.branch_ts, r.dgates, r.cots = named("norm_t"), named("branch_t"), named("dgate_e"), named("cot_e")
            extra = Mover(r.esems)
            copies = []
            for i in range(len(before)):
                copies += [extra.start(r.dgate.at[i], r.dgates[i]), extra.start(r.cot.at[i], r.cots[i])]
            r.extra = extra
        k2_body(nseq, M, m, kind, r)

    if last:
        scratch.update(esems=DMA((2 * M,)))
    return run("gate_and_out", body, ins, outs, scratch, keep, collective_id=1 + M + m)
TURNS = 4
EARLY_TURNS = ((0, 4, 9, 13, 18, 25, 32), (0, 8, 12, 17, 22, 29, 32))


def k3_body(ndp, nseq, micros, parts, hp_ref, cw_ref, chalo_ref, cum_ref, cin_ref, cout_ref, bc_ref, info_ref, sl_ref, sl_next_ref, start_ref, dy_ref, r_ref,
            gl_ref, later_ref, g1_ref, x_state, x_totals,
            dcin_ref, tail_ref, head_ref, dstep_ref, gcw_ref, gcb_ref, gskip_ref, ghead_ref, sum1_ref,
            dconv, w, xdu, ub, dyl, dgt, dt_x, tail_x, bg, later_v, landing, *rest):
    m, i = pl.program_id(0), pl.program_id(1)
    NC = pl.num_programs(1)
    c = NC - 1 - i
    step = m * NC + i
    steps = pl.num_programs(0) * NC
    traded = exchange_scratch(nseq)
    r = Refs()
    for name, ref in zip(traded, rest):
        setattr(r, name, ref)
    trade = Exchange(nseq, True, x_state, x_totals, r)
    reducer = Reducer(ndp, nseq, g1_ref, landing, rest[len(traded):], wait_only=6)
    M, own_turns = micros, TURNS * (micros - 1) * parts
    all_turns = TURNS * micros * parts
    trade_turns = [own_turns * t // 16 for t in (0, 2, 4, 6, 9, 11, 16)]
    table = [[min(t * all_turns // 32, all_turns) for t in row] for row in EARLY_TURNS]

    def comm(place):
        for turn in range(all_turns):
            if turn % TURNS != place:
                continue
            busy = turn in table[0] or turn in table[1]
            if not (busy or turn in trade_turns):
                continue

            @pl.when(step == turn // TURNS)
            def _():
                for n in range(trade.steps):
                    if trade_turns[n] == turn:
                        trade.step(n)
                reducer.at(turn, table)

    @pl.when(step == 0)
    def _():
        greet(reducer.partners() + trade.greeted)

    comm(0)

    @pl.when(jnp.logical_and(i == 0, m < M - 1))
    def _():
        later_v[...] = later_ref[0]

    @pl.when(jnp.logical_and(i == 0, m == M - 1))
    def _():
        later_v[...] = r.x_out[...]

    decay, _, hp = head_params(hp_ref)
    matrix = spread_matrix(0, DIN)
    gather = gather_matrix()
    skip = spread(jnp.broadcast_to(hp[2:3], (8, STATE)), matrix)[0:1]

    @pl.when(step == 0)
    def _():
        gcw_ref[...] = jnp.zeros_like(gcw_ref)
        gcb_ref[...] = jnp.zeros_like(gcb_ref)
        gskip_ref[...] = jnp.zeros_like(gskip_ref)
        ghead_ref[...] = jnp.zeros_like(ghead_ref)

    @pl.when(i == 0)
    def _():
        dconv[CHUNK:] = jnp.zeros((8, XBC), F32)

    @pl.when(i > 0)
    def _():
        dconv[CHUNK:] = dconv[0:8]

    tri_up = triangle(True)
    b32 = bc_ref[0, :, 0:STATE]
    c32 = bc_ref[0, :, STATE:2 * STATE]
    keeps_st = iota((CHUNK, CHUNK), 0) <= iota((CHUNK, CHUNK), 1)
    gram_t = jnp.where(keeps_st, fine_nt(c32, b32).T, 0.0)
    b, cc = b32.astype(BF16), c32.astype(BF16)
    lc = info_ref[0, 2]
    lct = lc.T
    dt = info_ref[0, 1]
    dt_x[...] = spread(dt, matrix)
    tail_x[...] = spread(jnp.exp2(lc[CHUNK - 1:CHUNK] - lc), matrix)
    dyl[...] = (dy_ref[0] * spread(jnp.exp2(lc), matrix)).astype(BF16)
    wide8 = lambda v: spread(jnp.exp2(jnp.broadcast_to(v, (8, STATE))), matrix)[0:1]
    gc = gl_ref[0, 0] + wide8(cum_ref[0, 1, pl.ds(c + 1, 1)]) * later_v[...].astype(F32)
    s_in = sl_ref[0, 0] + wide8(cum_ref[0, 0, pl.ds(c, 1)]) * start_ref[0].astype(F32)
    s_out = sl_next_ref[0, 0] + wide8(cum_ref[0, 0, pl.ds(c + 1, 1)]) * start_ref[0].astype(F32)
    gc2 = halves(gc)
    gcb16 = gc2[0:STATE]
    bnd = head_sums(jnp.broadcast_to(jnp.sum(gc * s_out, axis=0, keepdims=True), (8, DIN)), gather)[0:1]
    bg[...] = mm(jnp.concatenate([b, b], axis=1), gc2)
    dgt[...] = jnp.zeros((CHUNK, CHUNK), F32)
    for p in range(HEADS // 2):
        if p == 4:
            comm(1)
        if p == 8:
            comm(2)
        cols = slice(p * STATE, (p + 1) * STATE)
        v = cout_ref[0, :, cols]
        sig = sigmoid(v)
        x = v * sig
        dtx, tlx = dt_x[:, cols], tail_x[:, cols]
        ux = x * dtx
        u16 = ux.astype(BF16)
        ub[:, cols] = (ux * tlx).astype(BF16)
        dyf = dy_ref[0, :, cols]
        dy_high, dy_low = split2(dyf)
        dy2 = doubled(dy_high)
        decays, mixes = [], []
        for h in (2 * p, 2 * p + 1):
            gap = lct[h:h + 1, :] - lc[:, h:h + 1]
            e = jnp.exp2(jnp.minimum(gap, 0.0))
            decays.append(e)
            mixes.append((gram_t * e).astype(BF16))
        mix = jnp.concatenate(mixes, axis=1)
        du = mm(mix, dy2) + mm(mix, doubled(dy_low))
        dmix = mm_nt(u16, dy2)
        dgt[...] = dgt[...] + (dmix[:, :CHUNK] * decays[0] + dmix[:, CHUNK:] * decays[1])
        du_state = tlx * bg[:, cols]
        sk = skip[:, cols]
        dyx = dyf * x
        gskip_ref[:, cols] = gskip_ref[:, cols] + jnp.sum(dyx, axis=0, keepdims=True)
        w[:, cols] = dyx * sk + u16.astype(F32) * du + ux * du_state
        du = du + du_state
        xdu[:, cols] = x * du
        dx = dtx * du + sk * dyf
        dconv[0:CHUNK, cols] = dx * (sig * (1.0 + v * (1.0 - sig)))
    dg16 = jnp.where(keeps_st, dgt[...], 0.0).astype(BF16)
    db = mm(dg16, cc) + mm_nt(ub[...], gcb16)
    dc = mm_tn(dg16, b) + mm_nt(dyl[...], s_in.astype(BF16))
    v = cout_ref[0, :, DIN:XBC]
    sig = sigmoid(v)
    dconv[0:CHUNK, DIN:XBC] = jnp.concatenate([db, dc], axis=1) * (sig * (1.0 + v * (1.0 - sig)))
    dl = r_ref[0] - head_sums(w[...], gather)
    da = bnd + tri_sum(tri_up, dl)
    d_dt = head_sums(xdu[...], gather, 2) + da * decay
    dstep = d_dt * sigmoid(info_ref[0, 0])
    dstep_ref[0] = dstep.astype(BF16)
    ghead_ref[0:1] = ghead_ref[0:1] + decay * jnp.sum(da * dt, axis=0, keepdims=True)
    ghead_ref[1:2] = ghead_ref[1:2] + jnp.sum(dstep, axis=0, keepdims=True)

    @pl.loop(0, XBC // TILE)
    def _(j):
        cols = pl.ds(pl.multiple_of(j * TILE, TILE), TILE)
        gcb_ref[:, cols] = gcb_ref[:, cols] + jnp.sum(dconv[0:CHUNK, cols], axis=0, keepdims=True)
        own = cin_ref[0, :, cols].astype(F32)
        total = None
        for k in range(CONV):
            ahead = dconv[CONV - 1 - k:CONV - 1 - k + CHUNK, cols]
            gcw_ref[k:k + 1, cols] = gcw_ref[k:k + 1, cols] + jnp.sum(own * ahead, axis=0, keepdims=True)
            term = cw_ref[k:k + 1, cols] * ahead
            total = term if total is None else total + term
        dcin_ref[0, :, cols] = total.astype(BF16)

        @pl.when(i == 0)
        def _():
            tail_ref[0, :, cols] = total[CHUNK - HALO:]

    @pl.when(i == NC - 1)
    def _():
        head_ref[0] = dconv[0:8]
        for k in range(CONV - 1):
            for n in range(CONV - 1 - k):
                low = HALO - CONV + 1 + k + n
                gcw_ref[k:k + 1] = gcw_ref[k:k + 1] + chalo_ref[0, low:low + 1] * dconv[n:n + 1]

    comm(TURNS - 1)

    @pl.when(step == steps - 1)
    def _():
        reducer.at(all_turns, table)
        reducer.finish()

        def body(at, c):
            sum1_ref[pl.ds(at, c)] = landing[pl.ds(at, c)]
        strided(landing.shape[0], body)


def k3(ndp, nseq, hp, cw, chalo, cum, cin, cout, bc, info, sl, start, dy, r, gl, later, g1, x_state, x_totals):
    M, T, _ = cout.shape
    NC = T // CHUNK
    at = lambda m, i: NC - 1 - i
    const = lambda a: (pl.BlockSpec(a.shape, lambda m, i: (0,) * a.ndim), a)
    micro = lambda a: (pl.BlockSpec((1,) + a.shape[1:], lambda m, i: (m,) + (0,) * (a.ndim - 1)), a)
    chunk = lambda a: (pl.BlockSpec((1, CHUNK) + a.shape[2:], lambda m, i: (m, at(m, i), 0)), a)
    entry = lambda a, ahead: (pl.BlockSpec((1, 1) + a.shape[2:], lambda m, i: (m, at(m, i) + ahead, 0, 0)), a)
    inner = (pl.BlockSpec((1, 3, CHUNK, STATE), lambda m, i: (m, 0, at(m, i), 0)), info)
    sds = jax.ShapeDtypeStruct
    C = lambda width, dt: (pl.BlockSpec((1, CHUNK, width), lambda m, i: (m, at(m, i), 0)), sds((M, T, width), dt))
    S = lambda rows: (pl.BlockSpec((1, rows, XBC), lambda m, i: (m, 0, 0)), sds((M, rows, XBC), F32))
    W = lambda shape, dt: (pl.BlockSpec(shape, lambda m, i: (0,) * len(shape)), sds(shape, dt))
    V = pltpu.VMEM
    ins = [const(hp), const(cw), micro(chalo), micro(cum), chunk(cin), chunk(cout), chunk(bc), inner, entry(sl, 0), entry(sl, 1), micro(start),
           chunk(dy), chunk(r), entry(gl, 0), micro(later), const(g1), const(x_state), const(x_totals)]
    outs = [C(XBC, BF16), S(HALO), S(8), C(STATE, BF16), W((CONV, XBC), F32), W((1, XBC), F32), W((1, DIN), F32), W((2, STATE), F32),
            W(g1.shape[1:], BF16)]
    return pl.pallas_call(
        functools.partial(k3_body, ndp, nseq, M, NC),
        grid=(M, NC),
        in_specs=[b for b, _ in ins],
        out_specs=[b for b, _ in outs],
        out_shape=[o for _, o in outs],
        scratch_shapes=[V((CHUNK + 8, XBC), F32), V((CHUNK, DIN), F32), V((CHUNK, DIN), F32), V((CHUNK, DIN), BF16), V((CHUNK, DIN), BF16),
                        V((CHUNK, CHUNK), F32), V((CHUNK, DIN), F32), V((CHUNK, DIN), F32), V((CHUNK, DIN), F32), V((STATE, DIN), KIND), V(g1.shape[1:], BF16)] + list(exchange_scratch(nseq).values()) + reducer_scratch(ndp, nseq, g1.shape[1]),
        compiler_params=pltpu.CompilerParams(vmem_limit_bytes=VMEM_LIMIT, dimension_semantics=("arbitrary",) * 2, collective_id=10,
                                             has_side_effects=True),
        name="scan_backward",
    )(*[a for _, a in ins])


def k4_body(ndp, nseq, M, tok_ref, cot_hbm, params_ref, w_hbm, ws_ref, cw_ref, dgate_hbm, dcin_hbm, dstep_hbm, tail_ref, head_ref, sum1_in, *refs):
    norm_hbm, smalls, rest = refs[:M], refs[M:4 + 2 * M], refs[4 + 2 * M:]
    gtok_ref, sum1_ref, sum2_ref, small_out = rest[:4]
    g2, nxt, dc, norm_t, ngr, cot_ref, w_ref, dgate_ref, lsem, esend, erecv, hsem, hrsem = rest[4:17]
    rest = rest[7:]
    count = len(reducer_scratch(ndp, nseq, g2.shape[1]))
    reducer = Reducer(ndp, nseq, g2, sum2_ref, rest[10:10 + count])
    tiny = SmallReducer(ndp, nseq, small_out, rest[10 + count:])
    T = tok_ref.shape[1]
    dp, seq, _, _ = places()
    following, prev = lax.rem(seq + 1, nseq), lax.rem(seq + nseq - 1, nseq)
    loads = Mover(lsem)
    needed = []
    for m in range(M):
        needed += [loads.start(norm_hbm[m], norm_t.at[m], late=False),
                   loads.start(dcin_hbm.at[m, 0:T - HALO], dc.at[m, 0:T - HALO, 0:XBC], late=False),
                   loads.start(dstep_hbm.at[m], dc.at[m, :, XBC:], late=False)]
    greet(reducer.partners() + [(dp, following), (dp, prev)])
    halo = remote(head_ref, nxt, hsem, hrsem, (dp, prev))
    halo.start()
    halves_of_sum1 = reducer_like(reducer, sum1_in).halves(sum1_in, sum1_ref, (esend, erecv))
    for copy in halves_of_sum1:
        copy.start()
    for src, dst in ((w_hbm, w_ref), (dgate_hbm, dgate_ref), (cot_hbm, cot_ref)):
        loads.start(src, dst)
    rows = D // ndp
    gain = param(params_ref, "ng")
    clear_tiles(g2, rows, 15)
    for copy in needed:
        copy.wait()
    halo.wait()
    last = seq == nseq - 1
    row = iota((HALO, XBC), 0)
    for m in range(M):
        tail = tail_ref[m]
        for s in range(CONV - 1):
            extra = jnp.zeros((1, XBC), F32)
            for k in range(s + 1):
                extra = extra + cw_ref[k:k + 1] * nxt[m, s - k:s - k + 1]
            tail = tail + jnp.where(jnp.logical_and(row == HALO - CONV + 1 + s, jnp.logical_not(last)), extra, 0.0)
        dc[m, T - HALO:T, 0:XBC] = tail.astype(BF16)
    ngr[...] = jnp.zeros_like(ngr)
    dn = rest[-1]

    def backward(m, part):
        if part < D // TILE:
            cols = slice(part * TILE, (part + 1) * TILE)
            dn[:, cols] = (mm(dgate_ref[m], w_ref[0:DIN, cols]) + mm(dc[m, :, 0:XBC], w_ref[DIN:DIN + XBC, cols])
                           + mm(dc[m, :, XBC:], ws_ref[:, cols]))
        else:
            src, scale, _ = norm_rows(tok_ref[m], gain)
            unit = src * scale
            d_normed = dn[...]
            ngr[...] += jnp.sum(d_normed * unit, axis=0, keepdims=True)
            f = d_normed * gain
            mean = jnp.mean(f * unit, axis=-1, keepdims=True)
            gtok_ref[m] = (cot_ref[m].astype(F32) + scale * (f - unit * mean)).astype(BF16)

    half = (reducer.size * 2) // (rows // UNIT)
    weight_tiles(g2, rows, norm_t, dc, 0, half)
    for g in (0, 1):
        reducer.stage(0, g)
    weight_tiles(g2, rows, norm_t, dc, half, 15)
    for g in (2, 3):
        reducer.stage(0, g)
    parts = [(m, part) for m in range(M) for part in range(D // TILE + 1)]
    reducer_like(reducer, sum1_in).own_halves(sum1_in, sum1_ref)
    loads.finish()
    for k in range(1, 9):
        for stage, groups in ((k, (0, 1)), (k - 1, (2, 3))):
            if 1 <= stage <= 7:
                for g in groups:
                    reducer.stage(stage, g)
            if parts:
                backward(*parts[0])
                parts = parts[1:]
        if not parts and not tiny.begun:
            tiny.begin([[r[...] for r in group] for group in small_groups(smalls, ngr, M)])
        elif tiny.begun:
            tiny.advance()
    while not tiny.over:
        tiny.advance()
    tiny.finish()
    reducer.finish()
    for copy in halves_of_sum1:
        copy.wait()


def reducer_like(reducer, src):
    other = Refs()
    other.__class__ = Reducer
    other.__dict__.update(reducer.__dict__)
    other.size = src.shape[0] // GROUPS
    other.half = other.size // 2
    return other


def small_groups(smalls, ngr, M):
    gcw, gcb, gskip, ghead = smalls[:4]
    return [[gcw], [gcb], [ngr], list(smalls[4:4 + M]), [gskip], [ghead]]


def k4(ndp, nseq, tok, cot, params, w, ws, cw, dgate, dcin, dstep, tail, head, sum1, norm_ts, gcw, gcb, gskip, ghead, ogrs):
    M, T, _ = tok.shape
    V = pltpu.VMEM
    sds = jax.ShapeDtypeStruct
    vmem = pl.BlockSpec(memory_space=pltpu.VMEM)
    count = units(ndp, nseq, 15)
    args = (tok, cot, params, w, ws, cw, dgate, dcin, dstep, tail, head, sum1, *norm_ts, gcw, gcb, gskip, ghead, *ogrs)
    anywhere = (1, 3, 6, 7, 8) + tuple(range(12, 12 + M))
    return pl.pallas_call(
        functools.partial(k4_body, ndp, nseq, M),
        in_specs=[ANY if i in anywhere else vmem for i in range(len(args))],
        out_specs=[vmem] * 4,
        out_shape=[sds((M, T, D), BF16), sds(sum1.shape, BF16), sds((count, UNIT, STATE), BF16), sds((SMALL_ROWS, STATE), F32)],
        scratch_shapes=[V((ndp, count, UNIT, STATE), BF16), V(head.shape, F32), V((M, T, XBC + STATE), BF16), V((M, D, T), BF16), V((1, D), F32),
                        V(cot.shape, BF16), V(w.shape, BF16), V(dgate.shape, BF16), DMA((3 + 3 * M,)), DMA((GROUPS,)), DMA((GROUPS,)), DMA, DMA] + reducer_scratch(ndp, nseq, count) + small_scratch(ndp, nseq) + [V((T, D), F32)],
        compiler_params=pltpu.CompilerParams(collective_id=11, has_side_effects=True, vmem_limit_bytes=VMEM_LIMIT),
        name="projection_backward",
    )(*args)


def per_device(ndp, nseq, tokens, in_weight, out_weight, conv_weight, conv_bias, norm_gain, out_gain, skip_gain, rate_code, step_code, cotangent):
    micro, groups, T, _ = tokens.shape
    M = micro * groups
    tok = tokens.reshape(M, T, D)
    cot = cotangent.reshape(M, T, D)
    seq = lax.axis_index("seq")
    turned = in_weight.T
    pad = lambda v: jnp.pad(v.astype(F32), (0, STATE - HEADS))
    params = jnp.concatenate([norm_gain, out_gain, conv_bias, pad(rate_code), pad(step_code), pad(skip_gain)]).reshape(-1, STATE)
    if in_weight.shape[0] % STATE == 0:
        w, ws, halo = open_kernel(ndp, nseq, turned, tok)
    else:
        steps = jnp.pad(turned[DIN + XBC:], ((0, STATE - HEADS), (0, 0)))
        w, ws = [lax.all_gather(v, "dp", axis=1, tiled=True) for v in (turned[:DIN + XBC], steps)]
        halo = lax.ppermute(tok[:, T - HALO:], "seq", [(i, i + 1) for i in range(nseq - 1)])
    first, second = [], []
    for m in range(M):
        last = first[-1] if first else {}
        first.append(k1(ndp, nseq, m, last, tok, halo, w, ws, out_weight, conv_weight, params, last.get("sdev"), last.get("totals")))
    shared = {k: first[-1][k] for k in SHARED1}
    starts, wo = first[-1]["starts"], first[1]["wo"]
    for m in range(M):
        one = dict(shared, gate=first[m]["gate"], ypart=first[m]["ypart"], starts=starts)
        traded = (first[-1]["sdev"], first[-1]["totals"]) if m == 0 else (second[-1]["gdev"], first[m - 1]["totals"])
        second.append(k2(ndp, nseq, m, one, second, tok, cot, params, wo, *traded, units(ndp, nseq, 24)))
        starts = second[0]["starts"]
    s = dict(shared, starts=starts, laters=second[-1]["laters"], g1=second[-1]["g1"], **{k: second[-1][k] for k in SHARED2})
    dcin, tail, head, dstep, gcw, gcb, gskip, ghead, sum1 = k3(
        ndp, nseq, params, conv_weight, s["chalo"], s["cum"], s["cin"], s["cout"], s["bc"], s["info"], s["sl"], s["starts"], s["dy"],
        s["rows_dot"], s["gl"], s["laters"], s["g1"], second[-1]["gdev"], first[-1]["totals"])
    mixed = s["mixed"]
    gtok, sum1, sum2, sm = k4(ndp, nseq, tok, cot, params, w, ws, conv_weight, s["dgate"], dcin, dstep, tail, head, sum1, [b["norm_t"] for b in second], gcw, gcb, gskip, ghead,
                        [b["ogr"] for b in second])
    g_in, g_out, *rest = unpack(sum1, sum2, sm, D // ndp)
    return (mixed.reshape(tokens.shape), gtok.reshape(tokens.shape), g_in.T, g_out, *rest)


def solution(mesh):
    rows, split = P("dp", None), P(None, "dp", "seq", None)
    return jax.shard_map(
        functools.partial(per_device, mesh.shape["dp"], mesh.shape["seq"]),
        mesh=mesh,
        in_specs=(split, rows, rows) + (P(),) * 7 + (split,),
        out_specs=(split, split, rows, rows) + (P(),) * 7,
        check_vma=False,
    )
```

```python
import functools

import jax
import jax.numpy as jnp
from jax import lax
from jax.experimental import pallas as pl
from jax.experimental.pallas import tpu as pltpu
from jax.sharding import PartitionSpec as P

D = 768
DIN = 1536
HEADS = 24
HEAD_DIM = 64
STATE = 128
CONV = 4
XBC = 1792
PROJ = 3352
EPS = 1e-05
LOG2E = 1.4426950408889634
CHUNK = 128
TILE = 256
HALO = 16
UNIT = 16
KIND = jnp.float32
HOP_KIND = jnp.bfloat16
F32 = jnp.float32
BF16 = jnp.bfloat16
VMEM_LIMIT = 62 * 1024 * 1024


def mm(a, b):
    return lax.dot_general(a, b, (((1,), (0,)), ((), ())), preferred_element_type=F32)


def mm_nt(a, b):
    return lax.dot_general(a, b, (((1,), (1,)), ((), ())), preferred_element_type=F32)


def mm_tn(a, b):
    return lax.dot_general(a, b, (((0,), (0,)), ((), ())), preferred_element_type=F32)


def split2(v):
    hi = v.astype(BF16)
    return hi, (v - hi.astype(F32)).astype(BF16)


def split3(v):
    hi = v.astype(BF16)
    rest = v - hi.astype(F32)
    mid = rest.astype(BF16)
    return hi, mid, (rest - mid.astype(F32)).astype(BF16)


def iota(shape, dim):
    return lax.broadcasted_iota(jnp.int32, shape, dim)


def spread_matrix(start, width):
    head = iota((2 * STATE, width), 0) & (STATE - 1)
    column = (iota((2 * STATE, width), 1) + start) >> 6
    return jnp.where(head == column, 1.0, 0.0).astype(BF16)


def gather_matrix():
    return jnp.where((iota((DIN, STATE), 0) >> 6) == iota((DIN, STATE), 1), 1.0, 0.0).astype(BF16)


def spread(v, matrix):
    return mm(jnp.concatenate(split2(v), axis=1), matrix)


def head_sums(v, matrix, parts=3):
    pieces = split3(v) if parts == 3 else split2(v)
    total = mm(pieces[0], matrix)
    for piece in pieces[1:]:
        total = total + mm(piece, matrix)
    return total


def fine_nt(a, b):
    ah, al = split2(a)
    bh, bl = split2(b)
    return mm_nt(jnp.concatenate([ah, ah, al], axis=1), jnp.concatenate([bh, bl, bh], axis=1))


def halves(v):
    return jnp.concatenate(split2(v), axis=0)


def triangle(upper):
    row, column = iota((CHUNK, CHUNK), 0), iota((CHUNK, CHUNK), 1)
    keep = column >= row if upper else column <= row
    return jnp.where(keep, 1.0, 0.0).astype(BF16)


def tri_sum(tri, v):
    return mm(jnp.concatenate([tri] * 3, axis=1), jnp.concatenate(split3(v), axis=0))


PARAMS = {"ng": (0, D), "og": (6, DIN), "cb": (18, XBC), "head": (32, 3 * STATE)}


def param(ref, name):
    row, width = PARAMS[name]
    return jnp.concatenate([ref[row + i:row + i + 1] for i in range(width // STATE)], axis=1)


def head_params(params_ref):
    row = PARAMS["head"][0]
    hp = params_ref[row:row + 3]
    decay = -jnp.exp(-4.0 + 0.25 * hp[0:1])
    bias = -9.0 + 0.25 * hp[1:2]
    return decay, bias, hp


def sigmoid(v):
    return 0.5 * jnp.tanh(0.5 * v) + 0.5


def norm_rows(tok, gain):
    src = tok.astype(F32)
    scale = lax.rsqrt(jnp.mean(src * src, axis=-1, keepdims=True) + EPS)
    return src, scale, (src * scale * gain).astype(BF16)


def doubled(v):
    low = jnp.where(iota((1, STATE), 1) < HEAD_DIM, 1.0, 0.0)
    return jnp.concatenate([v * low.astype(BF16), v * (1.0 - low).astype(BF16)], axis=0)


def product_sum(left, right, cols):
    total = mm(left[0], right[0, :, cols])
    for m in range(1, left.shape[0]):
        total = total + mm(left[m], right[m, :, cols])
    return total


def put_tile(gtile_ref, d, tile, part):
    count = part.shape[0] // UNIT
    gtile_ref[d, pl.ds(tile * count, count)] = part.reshape(count, UNIT, STATE)


def clear_tiles(gtile_ref, rows, tiles):
    low, high = tiles * (rows // UNIT), gtile_ref.shape[1]
    if high > low:
        gtile_ref[:, low:] = jnp.zeros((gtile_ref.shape[0], high - low, UNIT, STATE), BF16)


def weight_tiles(gtile_ref, rows, left, right, first, end):
    def tiles(j, count):
        cols = pl.ds(pl.multiple_of(j * STATE, STATE), count * STATE)
        part = product_sum(left, right, cols).astype(BF16)
        for d in range(gtile_ref.shape[0]):
            for k in range(count):
                put_tile(gtile_ref, d, j + k, part[d * rows:(d + 1) * rows, k * STATE:(k + 1) * STATE])

    pairs = (end - first) // 2

    @pl.loop(0, pairs)
    def _(j):
        tiles(first + 2 * j, 2)

    if first + 2 * pairs < end:
        tiles(end - 1, 1)


MESH = pl.DeviceIdType.MESH
PLANE = 4
QUARTER = DIN // PLANE
DMA = pltpu.SemaphoreType.DMA


def places():
    seq = lax.axis_index("seq")
    return lax.axis_index("dp"), seq, lax.rem(seq, PLANE), lax.div(seq, PLANE)


def greet(devices):
    barrier = pltpu.get_barrier_semaphore()
    for device in devices:
        pl.semaphore_signal(barrier, inc=1, device_id=device, device_id_type=MESH)
    pl.semaphore_wait(barrier, len(devices))


def remote(src, dst, send, recv, device):
    return pltpu.make_async_remote_copy(
        src_ref=src, dst_ref=dst, send_sem=send, recv_sem=recv, device_id=device, device_id_type=MESH)


def open_body(ndp, nseq, win_ref, tok_ref, w_ref, wsall_ref, halo_ref, ws_ref, send, recv, hsend, hrecv):
    dp, seq, _, _ = places()
    nxt, prev = lax.rem(seq + 1, nseq), lax.rem(seq + nseq - 1, nseq)
    others = [lax.rem(dp + d, ndp) for d in range(1, ndp)]
    ws_ref[...] = jnp.zeros_like(ws_ref)
    ws_ref[0:HEADS] = win_ref[DIN + XBC:PROJ]
    greet([(o, seq) for o in others] + [(dp, nxt), (dp, prev)])
    T = tok_ref.shape[1]
    width = win_ref.shape[1]
    columns = pl.ds(pl.multiple_of(dp * width, width), width)
    moves = [(ws_ref, wsall_ref.at[:, columns]), (win_ref.at[0:DIN + XBC], w_ref.at[:, columns])]
    copies = [remote(tok_ref.at[:, T - HALO:T], halo_ref, hsend, hrecv, (dp, nxt))]
    for i, o in enumerate(others):
        for k, (src, dst) in enumerate(moves):
            copies.append(remote(src, dst, send.at[i, k], recv.at[i, k], (o, seq)))
    for copy in copies:
        copy.start()
    w_ref[:, columns] = win_ref[0:DIN + XBC]
    wsall_ref[:, columns] = ws_ref[...]
    for copy in copies:
        copy.wait()


def open_kernel(ndp, nseq, win, tok):
    vmem = pl.BlockSpec(memory_space=pltpu.VMEM)
    M = tok.shape[0]
    shape = lambda *s: jax.ShapeDtypeStruct(s, BF16)
    return pl.pallas_call(
        functools.partial(open_body, ndp, nseq),
        in_specs=[vmem, pl.BlockSpec(memory_space=pl.ANY)],
        out_specs=[vmem] * 3,
        out_shape=[shape(DIN + XBC, D), shape(STATE, D), shape(M, HALO, D)],
        scratch_shapes=[pltpu.VMEM((STATE, win.shape[1]), BF16), DMA((ndp - 1, 2)), DMA((ndp - 1, 2)), DMA, DMA],
        compiler_params=pltpu.CompilerParams(collective_id=1, has_side_effects=True, vmem_limit_bytes=VMEM_LIMIT),
        name="gather_weights",
    )(win, tok)


SMALL = (("cw", CONV, XBC), ("cb", 1, XBC), ("ng", 1, D), ("og", 1, DIN), ("skip", 1, DIN), ("head", 2, STATE))
SMALL_ROWS = 104


def small_pieces():
    row, found = 0, []
    for index, (_, rows, width) in enumerate(SMALL):
        for r in range(rows):
            for j in range(width // STATE):
                found.append((index, r, j, row))
                row += 1
    return found


def strided(count, body):
    step = max(s for s in range(1, 13) if count % s == 0)

    @pl.loop(0, count // step)
    def _(i):
        body(pl.multiple_of(i * step, step), step)


GROUPS = 4


def units(ndp, nseq, tiles):
    need, step = tiles * (D // ndp // UNIT), GROUPS * nseq
    return -(-need // step) * step


def reducer_scratch(ndp, nseq, count):
    Z = nseq // PLANE
    u = lambda n, *lead: tuple(lead) + (n, UNIT, STATE)
    V = pltpu.VMEM
    pairs = [DMA((GROUPS, ndp - 1))] * 2 + [DMA((GROUPS,))] * 4 + [DMA((GROUPS, Z - 1))] * 4 + [DMA((GROUPS,))] * 4
    return [V(u(count, ndp - 1), BF16), V(u(count // 2), F32), V(u(count // 2), BF16), V(u(count // 2), BF16),
            V(u(count // 4), F32), V(u(count // 4), BF16), V(u(count // 4), BF16), V(u(count // 4), BF16),
            V(u(count // 4 // Z, Z - 1), BF16)] + pairs


class Reducer:
    def __init__(self, ndp, nseq, src, out, scratch, wait_only=7):
        self.wait_only = wait_only
        self.ndp, self.Z = ndp, nseq // PLANE
        self.src, self.out = src, out
        (self.r0, self.w1, self.st1, self.r1, self.w2, self.st2, self.r2, self.st3, self.r3) = scratch[:9]
        self.sems = [(scratch[9 + 2 * k], scratch[10 + 2 * k]) for k in range(7)]
        self.dp, self.seq, self.p, self.z = places()
        x, y = lax.rem(self.p, 2), lax.div(self.p, 2)
        self.others = [lax.rem(self.dp + d, ndp) for d in range(1, ndp)]
        self.pz = [lax.rem(self.z + d, self.Z) * PLANE + self.p for d in range(1, self.Z)]
        sides = ((x, self.seq + 1 - 2 * x), (y, self.seq + 2 - 4 * y))
        self.sides = [sides if g % 2 == 0 else sides[::-1] for g in range(GROUPS)]
        self.size = src.shape[1] // GROUPS
        self.half, self.quarter = self.size // 2, self.size // 4
        self.piece = self.quarter // self.Z

    def partners(self):
        (_, px), (_, py) = self.sides[0]
        return [(o, self.seq) for o in self.others] + [(self.dp, q) for q in (px, py)] + [(self.dp, q) for q in self.pz]

    def copies(self, stage, g):
        sizes, at = self.size, g * self.size
        o1, o2, o3 = g * self.half, g * self.quarter, g * self.piece
        send, recv = self.sems[stage]
        (b1, peer1), (b2, peer2) = self.sides[g]
        half_at = at + b1 * self.half
        quarter_at = half_at + b2 * self.quarter
        piece_at = quarter_at + self.z * self.piece
        if stage == 0:
            return [remote(self.src.at[o, pl.ds(at, sizes)], self.r0.at[i, pl.ds(at, sizes)], send.at[g, i], recv.at[g, i], (o, self.seq))
                    for i, o in enumerate(self.others)]
        if stage == 1:
            span = pl.ds(o1, self.half)
            return [remote(self.st1.at[span], self.r1.at[span], send.at[g], recv.at[g], (self.dp, peer1))]
        if stage == 2:
            span = pl.ds(o2, self.quarter)
            return [remote(self.st2.at[span], self.r2.at[span], send.at[g], recv.at[g], (self.dp, peer2))]
        if stage == 3:
            return [remote(self.st3.at[pl.ds(o2 + lax.rem(self.z + d, self.Z) * self.piece, self.piece)], self.r3.at[d - 1, pl.ds(o3, self.piece)],
                           send.at[g, d - 1], recv.at[g, d - 1], (self.dp, self.pz[d - 1])) for d in range(1, self.Z)]
        if stage == 4:
            span = pl.ds(piece_at, self.piece)
            return [remote(self.out.at[span], self.out.at[span], send.at[g, d - 1], recv.at[g, d - 1], (self.dp, self.pz[d - 1]))
                    for d in range(1, self.Z)]
        span, peer = (pl.ds(quarter_at, self.quarter), peer2) if stage == 5 else (pl.ds(half_at, self.half), peer1)
        return [remote(self.out.at[span], self.out.at[span], send.at[g], recv.at[g], (self.dp, peer))]

    def stage(self, stage, g):
        if stage > 0:
            for copy in self.copies(stage - 1, g):
                copy.wait_recv()
        if stage == self.wait_only:
            return
        (b1, _), (b2, _) = self.sides[g]
        at, o1, o2, o3 = g * self.size, g * self.half, g * self.quarter, g * self.piece
        if stage == 1:
            def total(i, c):
                v = self.src[self.dp, pl.ds(at + i, c)].astype(F32)
                for k in range(self.ndp - 1):
                    v = v + self.r0[k, pl.ds(at + i, c)].astype(F32)
                return v

            def body(i, c):
                self.w1[pl.ds(o1 + i, c)] = total(b1 * self.half + i, c)
                self.st1[pl.ds(o1 + i, c)] = total((1 - b1) * self.half + i, c).astype(BF16)
            strided(self.half, body)
        elif stage == 2:
            def body(i, c):
                keep, give = pl.ds(o1 + b2 * self.quarter + i, c), pl.ds(o1 + (1 - b2) * self.quarter + i, c)
                self.w2[pl.ds(o2 + i, c)] = self.w1[keep] + self.r1[keep].astype(F32)
                self.st2[pl.ds(o2 + i, c)] = (self.w1[give] + self.r1[give].astype(F32)).astype(BF16)
            strided(self.quarter, body)
        elif stage == 3:
            def body(i, c):
                span = pl.ds(o2 + i, c)
                v = self.w2[span] + self.r2[span].astype(F32)
                self.w2[span] = v
                self.st3[span] = v.astype(BF16)
            strided(self.quarter, body)
        elif stage == 4:
            v = self.w2[pl.ds(o2 + self.z * self.piece, self.piece)]
            for d in range(self.Z - 1):
                v = v + self.r3[d, pl.ds(o3, self.piece)].astype(F32)
            self.out[pl.ds(at + b1 * self.half + b2 * self.quarter + self.z * self.piece, self.piece)] = v.astype(BF16)
        for copy in self.copies(stage, g):
            copy.start()

    def at(self, k, table):
        for stage in range(self.wait_only + 1):
            for row, groups in ((0, (0, 1)), (1, (2, 3))):
                if table[row][stage] == k:
                    for g in groups:
                        self.stage(stage, g)

    def halves(self, src, out, sems):
        found = []
        for g in range(GROUPS):
            (b1, peer), _ = self.sides[g]
            span = pl.ds(g * self.size + b1 * self.half, self.half)
            found.append(remote(src.at[span], out.at[span], sems[0].at[g], sems[1].at[g], (self.dp, peer)))
        return found

    def own_halves(self, src, out):
        for g in range(GROUPS):
            (b1, _), _ = self.sides[g]
            at = g * self.size + b1 * self.half

            def body(i, c):
                out[pl.ds(at + i, c)] = src[pl.ds(at + i, c)]
            strided(self.half, body)

    def finish(self):
        for stage in range(self.wait_only):
            for g in range(GROUPS):
                for copy in self.copies(stage, g):
                    copy.wait_send()


def small_scratch(ndp, nseq):
    Z = nseq // PLANE
    V = pltpu.VMEM
    shape = (SMALL_ROWS, STATE)
    count = ndp - 1 + 2 + Z - 1
    return [V((ndp,) + shape, F32), V((2,) + shape, F32), V((2,) + shape, F32), V((Z,) + shape, F32), DMA((count,)), DMA((count,))]


class SmallReducer:
    def __init__(self, ndp, nseq, out, scratch):
        self.out = out
        self.bufs, (self.send, self.recv) = scratch[:4], scratch[4:6]
        dp, seq, p, z = places()
        Z = nseq // PLANE
        x, y = lax.rem(p, 2), lax.div(p, 2)
        self.z, self.Z = z, Z
        self.peers = [[(lax.rem(dp + d, ndp), seq) for d in range(1, ndp)], [(dp, seq + 1 - 2 * x)], [(dp, seq + 2 - 4 * y)],
                      [(dp, lax.rem(z + d, Z) * PLANE + p) for d in range(1, Z)]]
        self.at, self.begun, self.over, self.started = 0, False, False, []

    def send_all(self):
        buf = self.bufs[self.at]
        base = sum(len(q) for q in self.peers[:self.at])
        self.flying = [remote(buf.at[0], buf.at[1 + k], self.send.at[base + k], self.recv.at[base + k], device)
                       for k, device in enumerate(self.peers[self.at])]
        for copy in self.flying:
            copy.start()
        self.started += self.flying

    def begin(self, groups):
        buf = self.bufs[0]
        buf[0] = jnp.zeros(buf.shape[1:], F32)
        for index, r, j, row in small_pieces():
            v = groups[index][0][r:r + 1, j * STATE:(j + 1) * STATE]
            for other in groups[index][1:]:
                v = v + other[r:r + 1, j * STATE:(j + 1) * STATE]
            buf[0, row:row + 1] = v
        self.begun = True
        self.send_all()

    def advance(self):
        if self.over:
            return
        for copy in self.flying:
            copy.wait_recv()
        buf = self.bufs[self.at]
        if self.at < 3:
            v = buf[0]
            for k in range(1, buf.shape[0]):
                v = v + buf[k]
            self.at += 1
            self.bufs[self.at][0] = v
            self.send_all()
            return
        v = None
        for k in range(self.Z):
            piece = buf[lax.rem(self.z - k + self.Z, self.Z)]
            v = piece if v is None else v + piece
        self.out[...] = v
        self.over = True

    def finish(self):
        for copy in self.started:
            copy.wait_send()


def unpack_body(g1_ref, g2_ref, sm_ref, gin_hbm, gout_hbm, cw_ref, cb_ref, ng_ref, og_ref, skip_ref, rate_ref, step_ref, gin_ref, gout_ref, sems):
    R = gin_ref.shape[1]
    moves = Mover(sems)
    U = R // UNIT
    tile = lambda ref, j: ref[j * U:(j + 1) * U].astype(F32).reshape(R, STATE)
    eye = jnp.where(iota((STATE, STATE), 0) == iota((STATE, STATE), 1), 1.0, 0.0).astype(BF16)
    turned = lambda ref, j: mm_nt(eye, ref[j * U:(j + 1) * U].reshape(R, STATE))
    for low, source, first, count in ((0, g1_ref, 0, 12), (DIN, g2_ref, 0, 14)):
        for j in range(count):
            rows = slice(low + j * STATE, low + (j + 1) * STATE)
            gin_ref[rows] = turned(source, first + j)
            moves.start(gin_ref.at[rows], gin_hbm.at[rows])
    gin_ref[DIN + XBC:] = turned(g2_ref, 14)[:HEADS]
    moves.start(gin_ref.at[DIN + XBC:PROJ], gin_hbm.at[DIN + XBC:PROJ])
    for half in range(2):
        rows = slice(half * R, (half + 1) * R)
        for j in range(D // STATE):
            gout_ref[rows, j * STATE:(j + 1) * STATE] = tile(g1_ref, 12 + half * 6 + j)
        moves.start(gout_ref.at[rows], gout_hbm.at[rows])
    outs = {1: cb_ref, 2: ng_ref, 3: og_ref}
    low, high = iota((1, STATE), 1) < HEAD_DIM, iota((1, STATE), 1)
    lane = iota((1, STATE), 1)
    skip = jnp.zeros((1, STATE), F32)
    for index, r, j, row in small_pieces():
        v = sm_ref[row:row + 1]
        if index == 0:
            cw_ref[r:r + 1, j * STATE:(j + 1) * STATE] = v
        elif index in outs:
            outs[index][j * STATE:(j + 1) * STATE] = v[0]
        elif index == 4:
            left = jnp.sum(jnp.where(low, v, 0.0), axis=1, keepdims=True)
            right = jnp.sum(jnp.where(low, 0.0, v), axis=1, keepdims=True)
            skip = skip + jnp.where(lane == 2 * j, left, 0.0) + jnp.where(lane == 2 * j + 1, right, 0.0)
        else:
            (rate_ref, step_ref)[r][...] = v[0, :HEADS]
    skip_ref[...] = skip[0, :HEADS]
    moves.finish()


def unpack(g1, g2, sm, R):
    vmem = pl.BlockSpec(memory_space=pltpu.VMEM)
    sds = lambda *s: jax.ShapeDtypeStruct(s, F32)
    return pl.pallas_call(
        unpack_body,
        in_specs=[vmem] * 3,
        out_specs=[pl.BlockSpec(memory_space=pl.ANY)] * 2 + [vmem] * 7,
        scratch_shapes=[pltpu.VMEM((PROJ, R), F32), pltpu.VMEM((2 * R, D), F32), DMA((32,))],
        out_shape=[sds(PROJ, R), sds(2 * R, D), sds(CONV, XBC), sds(XBC), sds(D), sds(DIN), sds(HEADS), sds(HEADS), sds(HEADS)],
        compiler_params=pltpu.CompilerParams(vmem_limit_bytes=VMEM_LIMIT),
        name="unpack_gradients",
    )(g1, g2, sm)
VMEM = pl.BlockSpec(memory_space=pltpu.VMEM)
ANY = pl.BlockSpec(memory_space=pl.ANY)


class Refs:
    pass


def run(name, body, ins, outs, scratch, carried=(), collective_id=None):
    names = list(ins) + list(outs) + list(scratch)
    aliases = {list(ins).index(k): list(outs).index(k) for k in carried}

    def kernel(*refs):
        r = Refs()
        for k, ref in zip(names, refs):
            setattr(r, k, ref)
        body(r)

    params = dict(vmem_limit_bytes=VMEM_LIMIT)
    if collective_id is not None:
        params.update(collective_id=collective_id, has_side_effects=True)
    got = pl.pallas_call(
        kernel,
        in_specs=[s for s, _ in ins.values()],
        out_specs=[s for s, _ in outs.values()],
        out_shape=[s for _, s in outs.values()],
        scratch_shapes=list(scratch.values()),
        input_output_aliases=aliases,
        compiler_params=pltpu.CompilerParams(**params),
        name=name,
    )(*[a for _, a in ins.values()])
    return dict(zip(outs, got))


class Mover:
    def __init__(self, sems):
        self.sems, self.count, self.flying = sems, 0, []

    def start(self, src, dst, late=True):
        copy = pltpu.make_async_copy(src, dst, self.sems.at[self.count])
        self.count += 1
        copy.start()
        if late:
            self.flying.append(copy)
        return copy

    def finish(self):
        for copy in self.flying:
            copy.wait()


def exchange_scratch(nseq):
    V = pltpu.VMEM
    Z = nseq // PLANE
    quarter = (STATE, QUARTER)
    return dict(x_out=V((STATE, DIN), KIND), x_got=V((PLANE,) + quarter, F32), x_tots=V((PLANE, 8, STATE), F32), x_pre=V(quarter, F32),
                x_zin=V((Z,) + quarter, HOP_KIND), x_ztots=V((Z, 8, STATE), F32), x_back=V((PLANE,) + quarter, KIND),
                x_ts=DMA((3,)), x_tr=DMA((3,)), x_s=DMA((2, 3)), x_r=DMA((2, 3)), x_zs=DMA((2, Z - 1)), x_zr=DMA((2, Z - 1)), x_zts=DMA((Z - 1,)),
                x_ztr=DMA((Z - 1,)), x_bs=DMA((2, 3)), x_br=DMA((2, 3)))


class Exchange:
    def __init__(self, nseq, upward, state, totals, r):
        self.upward, self.state, self.totals, self.r = upward, state, totals, r
        self.dp, self.seq, self.p, self.z = places()
        self.Z = nseq // PLANE
        self.base = self.z * PLANE
        self.peers = [lax.rem(self.p + d, PLANE) for d in range(PLANE)]
        self.line = [(self.dp, lax.rem(self.z + d, self.Z) * PLANE + self.p) for d in range(1, self.Z)]
        self.greeted = [(self.dp, self.base + q) for q in self.peers[1:]] + self.line
        self.steps = 7
        self.at = 0

    def columns(self, q):
        return pl.ds(pl.multiple_of(q * QUARTER, QUARTER), QUARTER)

    def rows(self, part):
        return pl.ds(part * (STATE // 2), STATE // 2)

    def first(self, part):
        r = self.r
        found = []
        for d in range(1, PLANE):
            to = (self.dp, self.base + self.peers[d])
            if part == 0:
                found.append(remote(self.totals, r.x_tots.at[d], r.x_ts.at[d - 1], r.x_tr.at[d - 1], to))
            found.append(remote(self.state.at[self.rows(part), self.columns(self.peers[d])], r.x_got.at[d, self.rows(part)], r.x_s.at[part, d - 1],
                                r.x_r.at[part, d - 1], to))
        return found

    def along(self, part, d):
        r = self.r
        to = (self.dp, lax.rem(self.z + (self.Z - d if self.upward else d), self.Z) * PLANE + self.p)
        copies = [remote(r.x_zin.at[0, self.rows(part)], r.x_zin.at[d, self.rows(part)], r.x_zs.at[part, d - 1], r.x_zr.at[part, d - 1], to)]
        if part == 0:
            copies.append(remote(r.x_ztots.at[0], r.x_ztots.at[d], r.x_zts.at[d - 1], r.x_ztr.at[d - 1], to))
        sends = self.z >= d if self.upward else self.z + d < self.Z
        receives = self.z + d < self.Z if self.upward else self.z >= d
        return copies, sends, receives

    def last(self, part):
        r = self.r
        return [remote(r.x_back.at[d, self.rows(part)], r.x_out.at[self.rows(part), self.columns(self.p)], r.x_bs.at[part, d - 1],
                       r.x_br.at[part, d - 1], (self.dp, self.base + lax.rem(self.p + PLANE - d, PLANE))) for d in range(1, PLANE)]

    def turn(self):
        order = range(PLANE - 1, -1, -1) if self.upward else range(PLANE)
        slots = [lax.rem(self.p - q + PLANE, PLANE) for q in order]
        return slots, spread_matrix(self.p * QUARTER, QUARTER)

    def begin(self):
        r = self.r
        for copy in self.first(0):
            copy.start()
        r.x_tots[0] = self.totals[...]
        r.x_got[0] = self.state[:, self.columns(self.p)]

    def plane(self, part):
        r = self.r
        for copy in self.first(part):
            copy.wait_recv()
        slots, matrix = self.turn()
        total = jnp.zeros((STATE // 2, QUARTER), F32)
        for slot in slots:
            total = spread(jnp.exp2(r.x_tots[slot]), matrix)[0:1] * total + r.x_got[slot, self.rows(part)].astype(F32)
        r.x_zin[0, self.rows(part)] = total.astype(HOP_KIND)
        if part == 0:
            r.x_ztots[0] = r.x_tots[0] + r.x_tots[1] + r.x_tots[2] + r.x_tots[3]
        for d in range(1, self.Z):
            copies, sends, _ = self.along(part, d)

            @pl.when(sends)
            def _():
                for copy in copies:
                    copy.start()

    def give(self, part):
        r = self.r
        rows = self.rows(part)
        slots, matrix = self.turn()
        r.x_pre[rows] = jnp.zeros((STATE // 2, QUARTER), F32)
        for d in range(self.Z - 1, 0, -1):
            copies, _, receives = self.along(part, d)

            @pl.when(receives)
            def _():
                for copy in copies:
                    copy.wait_recv()
                r.x_pre[rows] = spread(jnp.exp2(r.x_ztots[d]), matrix)[0:1] * r.x_pre[rows] + r.x_zin[d, rows].astype(F32)
        total = r.x_pre[rows]
        for slot in slots:
            r.x_back[slot, rows] = total.astype(KIND)
            total = spread(jnp.exp2(r.x_tots[slot]), matrix)[0:1] * total + r.x_got[slot, rows].astype(F32)
        for copy in self.last(part):
            copy.start()
        r.x_out[rows, self.columns(self.p)] = r.x_back[0, rows]

    def end(self):
        for part in range(2):
            for copy in self.last(part):
                copy.wait_recv()
        for part in range(2):
            for copy in self.first(part) + self.last(part):
                copy.wait_send()
            for d in range(1, self.Z):
                copies, sends, _ = self.along(part, d)

                @pl.when(sends)
                def _():
                    for copy in copies:
                        copy.wait_send()

    def step(self, k):
        if k == 0:
            self.begin()
        elif k == 1:
            for copy in self.first(1):
                copy.start()
        elif k in (2, 3):
            self.plane(k - 2)
        elif k in (4, 5):
            self.give(k - 4)
        else:
            self.end()

    def tick(self):
        if self.at < self.steps:
            self.step(self.at)
            self.at += 1

    def finish(self):
        while self.at < self.steps:
            self.tick()


class NoExchange:
    def tick(self):
        pass

    finish = tick


def chunks(T):
    return [(c, slice(c * CHUNK, (c + 1) * CHUNK)) for c in range(T // CHUNK)]


SHARED1 = ("cin", "cout", "bc", "info", "sl", "cum", "chalo")


def k1_body(ndp, nseq, m, ahead, r):
    T = r.gate_v.shape[0]
    NC = T // CHUNK
    moves = Mover(r.sems)
    loads = [moves.start(r.tok.at[m], r.tok_v, late=False), moves.start(r.w, r.w_v, late=False)]
    trade = NoExchange()
    if ahead:
        trade = Exchange(nseq, False, r.x_state, r.x_totals, r)
    weights = []
    if m == 1:
        dp, seq, _, _ = places()
        count = r.wout.shape[0]
        mine = pl.ds(pl.multiple_of(dp * count, count), count)
        others = [(lax.rem(dp + d, ndp), seq) for d in range(1, ndp)]
        greet(trade.greeted + others)
        weights = [remote(r.wout, r.wo_land.at[mine], r.w_send.at[i], r.w_recv.at[i], o) for i, o in enumerate(others)]
    elif ahead:
        greet(trade.greeted)
    trade.tick()
    for copy in weights:
        copy.start()
    decay, bias, hp = head_params(r.params)
    decay2 = decay * LOG2E
    gain = param(r.params, "ng")
    r.cb[...] = param(r.params, "cb")
    first = lax.axis_index("seq") == 0
    r.an[0:HALO] = jnp.where(first, 0.0, norm_rows(r.halo[m], gain)[2].astype(F32)).astype(BF16)
    loads[0].wait()
    r.an[HALO:] = norm_rows(r.tok_v[...], gain)[2]
    arg = mm_nt(r.an[HALO:], r.ws[...]) + bias
    dt = jnp.maximum(arg, 0.0) + jnp.log1p(jnp.exp(-jnp.abs(arg)))
    r.info_v[0] = arg
    r.info_v[1] = dt
    r.dt2[...] = jnp.concatenate(split2(dt), axis=1)
    tri = triangle(False)
    ends = []
    for c, rows in chunks(T):
        lc = tri_sum(tri, dt[rows] * decay2)
        r.info_v[2, rows] = lc
        ends.append(lc[CHUNK - 1:CHUNK])
        r.tw2[rows] = jnp.concatenate(split2(jnp.exp2(lc[CHUNK - 1:CHUNK] - lc)), axis=1)
    before, after = jnp.zeros((1, STATE), F32), jnp.zeros((1, STATE), F32)
    for c in range(NC + 1):
        r.cum_v[0, c:c + 1] = before
        r.cum_v[1, NC - c:NC - c + 1] = after
        if c < NC:
            before, after = before + ends[c], after + ends[NC - 1 - c]
    r.totals[...] = jnp.broadcast_to(before, (8, STATE))
    trade.tick()
    moves.start(r.info_v, r.info.at[m])
    moves.start(r.cum_v, r.cum.at[m])
    loads[1].wait()

    def conv_tile(j, cols):
        wcols = pl.ds(pl.multiple_of(DIN + j * TILE, TILE), TILE)
        raw = mm_nt(r.an[...], r.w_v[wcols, :])
        r.cpad[...] = raw
        r.cin_v[:, cols] = raw[HALO:].astype(BF16)
        r.chalo_v[:, cols] = raw[:HALO]
        out = r.cb[:, cols]
        for k in range(CONV):
            out = out + r.cw[k:k + 1, cols] * r.cpad[HALO - CONV + 1 + k:HALO - CONV + 1 + k + T]
        r.cout_v[:, cols] = out
        for k, name in enumerate(("cin", "cout")):
            pltpu.make_async_copy(getattr(r, name + "_v").at[:, cols], getattr(r, name).at[m, :, cols], r.tsems.at[k, j]).start()
        return out * sigmoid(out)

    def x_tile(j):
        cols = pl.ds(pl.multiple_of(j * TILE, TILE), TILE)
        x = conv_tile(j, cols)
        matrix = spread_matrix(j * TILE, TILE)
        ux = x * mm(r.dt2[...], matrix)
        r.u[:, cols] = ux.astype(BF16)
        hi, lo = split2(ux * mm(r.tw2[...], matrix))
        for c, rows in chunks(T):
            r.ub[c, 0:CHUNK, cols] = hi[rows]
            r.ub[c, CHUNK:, cols] = lo[rows]
        skip_tile = spread(jnp.broadcast_to(hp[2:3], (8, STATE)), matrix)[0:1]
        r.ypart_v[:, cols] = x * skip_tile

    pl.loop(0, DIN // TILE // 2 + 1)(x_tile)
    trade.tick()
    pl.loop(DIN // TILE // 2 + 1, DIN // TILE)(x_tile)
    if m == 1:
        r.wo_land[mine] = r.wout[...]
    r.bc_v[...] = conv_tile(DIN // TILE, pl.ds(DIN, TILE))
    moves.start(r.chalo_v, r.chalo.at[m])
    moves.start(r.bc_v, r.bc.at[m])
    trade.tick()
    if m == 1:
        for copy in weights:
            copy.wait_recv()
        moves.start(r.wo_land, r.wo)
    matrix = spread_matrix(0, DIN)
    state = jnp.zeros((STATE, DIN), F32)
    for c, rows in chunks(T):
        b16 = r.bc_v[rows, 0:STATE].astype(BF16)
        r.sl_v[c] = state
        keep = spread(jnp.exp2(jnp.broadcast_to(ends[c], (8, STATE))), matrix)[0:1]
        state = keep * state + mm_tn(jnp.concatenate([b16, b16], axis=0), r.ub[c])
    r.sl_v[NC] = state
    r.sdev[...] = state
    moves.start(r.sl_v, r.sl.at[m])

    @pl.loop(0, DIN // TILE)
    def _(j):
        cols = pl.ds(pl.multiple_of(j * TILE, TILE), TILE)
        r.gate_v[:, cols] = mm_nt(r.an[HALO:], r.w_v[cols, :])
        pltpu.make_async_copy(r.gate_v.at[:, cols], r.gate.at[:, cols], r.tsems.at[2, j]).start()
    trade.tick()

    causal = iota((CHUNK, CHUNK), 0) >= iota((CHUNK, CHUNK), 1)
    for c, rows in chunks(T):
        gram = jnp.where(causal, fine_nt(r.bc_v[rows, STATE:2 * STATE], r.bc_v[rows, 0:STATE]), 0.0)
        lc = r.info_v[2, rows]
        lct = lc.T
        for p in range(HEADS // 2):
            cols = slice(p * STATE, (p + 1) * STATE)
            mixes = []
            for h in (2 * p, 2 * p + 1):
                gap = lc[:, h:h + 1] - lct[h:h + 1, :]
                mixes.append((gram * jnp.exp2(jnp.minimum(gap, 0.0))).astype(BF16))
            r.ypart_v[rows, cols] = r.ypart_v[rows, cols] + mm(jnp.concatenate(mixes, axis=1), doubled(r.u[rows, cols]))
        moves.start(r.ypart_v.at[rows], r.ypart.at[rows])
        if c == NC // 2:
            trade.tick()
    trade.finish()
    if ahead:
        moves.start(r.x_out, r.starts.at[m - 1])
    moves.finish()
    for copy in weights:
        copy.wait_send()
    for k, (src, dst) in enumerate(((r.cin_v, r.cin.at[m]), (r.cout_v, r.cout.at[m]), (r.gate_v, r.gate))):
        for j in range(src.shape[1] // TILE):
            cols = slice(j * TILE, (j + 1) * TILE)
            pltpu.make_async_copy(src.at[:, cols], dst.at[:, cols], r.tsems.at[k, j]).wait()


def k1(ndp, nseq, m, carried, tok, halo, w, ws, wout, cw, params, sdev=None, totals=None):
    M, T, _ = tok.shape
    NC = T // CHUNK
    V = pltpu.VMEM
    sds = jax.ShapeDtypeStruct
    ahead = m > 0
    ins = dict(tok=(ANY, tok), w=(ANY, w), halo=(VMEM, halo), ws=(VMEM, ws), cw=(VMEM, cw), params=(VMEM, params))
    shapes = dict(cin=(T, XBC), cout=(T, XBC), bc=(T, 2 * STATE), info=(3, T, STATE), sl=(NC + 1, STATE, DIN), cum=(2, NC + 1, STATE),
                  chalo=(HALO, XBC))
    kinds = {k: BF16 if k == "cin" else F32 for k in SHARED1}
    outs = {k: (ANY, sds((M,) + shapes[k], kinds[k])) for k in SHARED1}
    outs.update(gate=(ANY, sds((T, DIN), F32)), ypart=(ANY, sds((T, DIN), F32)), sdev=(VMEM, sds((STATE, DIN), F32)),
                totals=(VMEM, sds((8, STATE), F32)))
    scratch = dict(cb=V((1, XBC), F32), tok_v=V((T, D), BF16), w_v=V(w.shape, BF16), cpad=V((HALO + T, TILE), F32), an=V((HALO + T, D), BF16), u=V((T, DIN), BF16),
                   ub=V((NC, 2 * CHUNK, DIN), BF16), dt2=V((T, 2 * STATE), BF16), tw2=V((T, 2 * STATE), BF16),
                   gate_v=V((T, DIN), F32), ypart_v=V((T, DIN), F32), sems=DMA((20 + NC,)), tsems=DMA((3, XBC // TILE)),
                   **{k + "_v": V(shapes[k], kinds[k]) for k in SHARED1})
    if ahead:
        ins.update({k: (ANY, carried[k]) for k in SHARED1}, x_state=(VMEM, sdev), x_totals=(VMEM, totals))
        outs.update(starts=(ANY, sds((M, STATE, DIN), KIND)))
        if m > 1:
            ins.update(starts=(ANY, carried["starts"]))
        scratch.update(exchange_scratch(nseq))
    if m == 1:
        ins.update(wout=(VMEM, wout))
        outs.update(wo=(ANY, sds((DIN, D), BF16)))
        scratch.update(wo_land=V((DIN, D), BF16), w_send=DMA((ndp - 1,)), w_recv=DMA((ndp - 1,)))
    keep = [k for k in SHARED1 + ("starts",) if k in ins]
    return run("forward_local", functools.partial(k1_body, ndp, nseq, m, ahead), ins, outs, scratch, keep, collective_id=1 + m if ahead else None)


SHARED2 = ("mixed", "dgate", "dy", "rows_dot", "gl")


def k2_body(nseq, M, m, kind, r):
    T = r.gate_v.shape[0]
    NC = T // CHUNK
    moves = Mover(r.sems)
    loads = {}
    for k, src in (("start", r.starts_in.at[m]), ("info", r.info.at[m]), ("cum", r.cum.at[m]), ("bc", r.bc.at[m]), ("sl", r.sl.at[m, 0:NC]),
                   ("ypart", r.ypart), ("gate", r.gate), ("tok", r.tok.at[m]), ("wo", r.wo), ("cot", r.cot.at[m])):
        loads[k] = moves.start(src, getattr(r, k + "_v"), late=False)
    upward = kind == "later"
    trade = Exchange(nseq, upward, r.x_state, r.x_totals, r)
    greet(trade.greeted)
    trade.tick()
    matrix = spread_matrix(0, DIN)
    gather = gather_matrix()
    loads["tok"].wait()
    r.norm_t[...] = norm_rows(r.tok_v[...], param(r.params, "ng"))[2].T
    og = param(r.params, "og")
    loads["cot"].wait()
    loads["wo"].wait()
    trade.tick()

    @pl.loop(0, DIN // TILE)
    def _(j):
        cols = pl.ds(pl.multiple_of(j * TILE, TILE), TILE)
        r.dbr[:, cols] = mm_nt(r.cot_v[...], r.wo_v[cols, :])

    for k in ("start", "info", "cum", "bc", "sl", "ypart", "gate"):
        loads[k].wait()
    trade.tick()
    for c, rows in chunks(T):
        keep = spread(jnp.exp2(jnp.broadcast_to(r.cum_v[0, c:c + 1], (8, STATE))), matrix)[0:1]
        state = halves(r.sl_v[c] + keep * r.start_v[...].astype(F32))
        c16 = r.bc_v[rows, STATE:2 * STATE].astype(BF16)
        lift = spread(jnp.exp2(r.info_v[2, rows]), matrix)
        yc = r.ypart_v[rows] + lift * mm(jnp.concatenate([c16, c16], axis=1), state)
        r.ypart_v[rows] = yc
        g = r.gate_v[rows]
        gated = yc * (g * sigmoid(g))
        scale = lax.rsqrt(jnp.mean(gated * gated, axis=-1, keepdims=True) + EPS)
        r.oscale[rows] = jnp.broadcast_to(scale, (CHUNK, STATE))
        r.branch[rows] = (gated * scale * og).astype(BF16)
        if c == 1:
            trade.tick()
    r.branch_t[...] = r.branch[...].T
    for j in range(D // TILE):
        cols = slice(j * TILE, (j + 1) * TILE)
        r.mixed_v[:, cols] = (r.tok_v[:, cols].astype(F32) + mm(r.branch[...], r.wo_v[:, cols])).astype(BF16)
    moves.start(r.mixed_v, r.mixed.at[m])
    trade.tick()
    r.ogr[...] = jnp.zeros_like(r.ogr)
    r.gdev[...] = jnp.zeros_like(r.gdev)
    for c, rows in reversed(chunks(T)):
        g = r.gate_v[rows]
        yc = r.ypart_v[rows]
        db = r.dbr[rows]
        scale = r.oscale[rows][:, 0:1]
        sig = sigmoid(g)
        act = g * sig
        gated = yc * act
        unit = gated * scale
        r.ogr[...] += jnp.sum(db * unit, axis=0, keepdims=True)
        e = db * og
        mean = jnp.mean(e * unit, axis=-1, keepdims=True)
        dgated = scale * (e - unit * mean)
        r.dgate_v[rows] = (dgated * yc * (sig * (1.0 + g * (1.0 - sig)))).astype(BF16)
        high, low = split2(dgated * act)
        dyf = high.astype(F32) + low.astype(F32)
        r.dy_v[rows] = dyf
        r.rows_dot_v[rows] = head_sums(dyf * yc, gather)
        lc = r.info_v[2, rows]
        lifted = halves(dyf * spread(jnp.exp2(lc), matrix))
        c16 = r.bc_v[rows, STATE:2 * STATE].astype(BF16)
        r.gl_v[c] = r.gdev[...]
        keep = spread(jnp.exp2(jnp.broadcast_to(lc[CHUNK - 1:CHUNK], (8, STATE))), matrix)[0:1]
        r.gdev[...] = keep * r.gdev[...] + mm_tn(jnp.concatenate([c16, c16], axis=0), lifted)
        moves.start(r.dy_v.at[rows], r.dy.at[m, rows])
        moves.start(r.gl_v.at[c], r.gl.at[m, c])
        if c == NC - 2:
            trade.tick()
    moves.start(r.dgate_v, r.dgate.at[m])
    moves.start(r.rows_dot_v, r.rows_dot.at[m])
    if m == M - 1:
        early_grads(r)
    trade.finish()
    if upward:
        moves.start(r.x_out, r.laters.at[m - 1])
    else:
        moves.start(r.x_out, r.starts.at[M - 1])
    moves.finish()


def early_grads(r):
    dp = r.g1.shape[0]
    rows = D // dp
    r.extra.finish()
    clear_tiles(r.g1, rows, 24)

    def summed(lefts, rights, cols):
        total = None
        for left, right in zip(lefts, rights):
            part = mm(left[...], right[:, cols])
            total = part if total is None else total + part
        return total.astype(BF16)

    @pl.loop(0, DIN // TILE)
    def _(j):
        part = summed(r.norm_ts + [r.norm_t], r.dgates + [r.dgate_v], pl.ds(pl.multiple_of(j * TILE, TILE), TILE))
        for d in range(dp):
            for k in range(TILE // STATE):
                put_tile(r.g1, d, j * (TILE // STATE) + k, part[d * rows:(d + 1) * rows, k * STATE:(k + 1) * STATE])

    @pl.loop(0, D // TILE)
    def _(j):
        part = summed(r.branch_ts + [r.branch_t], r.cots + [r.cot_v], pl.ds(pl.multiple_of(j * TILE, TILE), TILE))
        for d in range(dp):
            for half in range(2):
                low = (2 * d + half) * rows
                for k in range(TILE // STATE):
                    put_tile(r.g1, d, 12 + half * 6 + j * (TILE // STATE) + k, part[low:low + rows, k * STATE:(k + 1) * STATE])


def k2(ndp, nseq, m, one, before, tok, cot, params, wo, state, totals, count):
    M, T, _ = tok.shape
    NC = T // CHUNK
    V = pltpu.VMEM
    sds = jax.ShapeDtypeStruct
    kind = "earlier" if m == 0 else "later"
    ins = dict(tok=(ANY, tok), cot=(ANY, cot), wo=(ANY, wo), params=(VMEM, params), info=(ANY, one["info"]), cum=(ANY, one["cum"]),
               bc=(ANY, one["bc"]), sl=(ANY, one["sl"]), ypart=(ANY, one["ypart"]), gate=(ANY, one["gate"]),
               x_state=(VMEM, state), x_totals=(VMEM, totals))
    shapes = dict(mixed=((T, D), BF16), dgate=((T, DIN), BF16), dy=((T, DIN), F32), rows_dot=((T, STATE), F32), gl=((NC, STATE, DIN), F32))
    outs = {k: (ANY, sds((M,) + s, t)) for k, (s, t) in shapes.items()}
    outs.update(gdev=(VMEM, sds((STATE, DIN), F32)), ogr=(VMEM, sds((1, DIN), F32)))
    scratch = dict(tok_v=V((T, D), BF16), cot_v=V((T, D), BF16), wo_v=V(wo.shape, BF16), info_v=V((3, T, STATE), F32), cum_v=V((2, NC + 1, STATE), F32),
                   bc_v=V((T, 2 * STATE), F32), sl_v=V((NC, STATE, DIN), F32), ypart_v=V((T, DIN), F32), gate_v=V((T, DIN), F32),
                   start_v=V((STATE, DIN), KIND), dbr=V((T, DIN), F32), branch=V((T, DIN), BF16), oscale=V((T, STATE), F32),
                   sems=DMA((20 + 2 * NC,)), **{k + "_v": V(s, t) for k, (s, t) in shapes.items()})
    scratch.update(exchange_scratch(nseq))
    last = m == M - 1
    turned = dict(branch_t=sds((DIN, T), BF16), norm_t=sds((D, T), BF16))
    if last:
        scratch.update(branch_t=V((DIN, T), BF16))
        outs.update(norm_t=(VMEM, turned["norm_t"]))
        outs.update(g1=(VMEM, sds((ndp, count, UNIT, STATE), BF16)))
        for i, b in enumerate(before):
            for k in turned:
                ins[k + str(i)] = (VMEM, b[k])
            scratch["dgate_e%d" % i] = V((T, DIN), BF16)
            scratch["cot_e%d" % i] = V((T, D), BF16)
    else:
        outs.update({k: (VMEM, s) for k, s in turned.items()})
    keep = []
    if m == 0:
        ins.update(starts=(ANY, one["starts"]))
        outs.update(starts=(ANY, sds(one["starts"].shape, KIND)))
        keep += ["starts"]
    else:
        ins.update({k: (ANY, before[-1][k]) for k in SHARED2}, starts_in=(ANY, one["starts"]))
        outs.update(laters=(ANY, sds((M, STATE, DIN), KIND)))
        keep += list(SHARED2)
        if m > 1:
            ins.update(laters=(ANY, before[-1]["laters"]))
            keep += ["laters"]

    def body(r):
        if m == 0:
            r.starts_in = r.starts
        if last:
            named = lambda k: [getattr(r, k + str(i)) for i in range(len(before))]
            r.norm_ts, r.branch_ts, r.dgates, r.cots = named("norm_t"), named("branch_t"), named("dgate_e"), named("cot_e")
            extra = Mover(r.esems)
            copies = []
            for i in range(len(before)):
                copies += [extra.start(r.dgate.at[i], r.dgates[i]), extra.start(r.cot.at[i], r.cots[i])]
            r.extra = extra
        k2_body(nseq, M, m, kind, r)

    if last:
        scratch.update(esems=DMA((2 * M,)))
    return run("gate_and_out", body, ins, outs, scratch, keep, collective_id=1 + M + m)
TURNS = 4
EARLY_TURNS = ((0, 4, 9, 13, 18, 25, 32), (0, 8, 12, 17, 22, 29, 32))


def k3_body(ndp, nseq, micros, parts, hp_ref, cw_ref, chalo_ref, cum_ref, cin_ref, cout_ref, bc_ref, info_ref, sl_ref, sl_next_ref, start_ref, dy_ref, r_ref,
            gl_ref, later_ref, g1_ref, x_state, x_totals,
            dcin_ref, tail_ref, head_ref, dstep_ref, gcw_ref, gcb_ref, gskip_ref, ghead_ref, sum1_ref,
            dconv, w, xdu, ub, dyl, dgt, dt_x, tail_x, bg, later_v, landing, *rest):
    m, i = pl.program_id(0), pl.program_id(1)
    NC = pl.num_programs(1)
    c = NC - 1 - i
    step = m * NC + i
    steps = pl.num_programs(0) * NC
    traded = exchange_scratch(nseq)
    r = Refs()
    for name, ref in zip(traded, rest):
        setattr(r, name, ref)
    trade = Exchange(nseq, True, x_state, x_totals, r)
    reducer = Reducer(ndp, nseq, g1_ref, landing, rest[len(traded):], wait_only=6)
    M, own_turns = micros, TURNS * (micros - 1) * parts
    all_turns = TURNS * micros * parts
    trade_turns = [own_turns * t // 16 for t in (0, 2, 4, 6, 9, 11, 16)]
    table = [[min(t * all_turns // 32, all_turns) for t in row] for row in EARLY_TURNS]

    def comm(place):
        for turn in range(all_turns):
            if turn % TURNS != place:
                continue
            busy = turn in table[0] or turn in table[1]
            if not (busy or turn in trade_turns):
                continue

            @pl.when(step == turn // TURNS)
            def _():
                for n in range(trade.steps):
                    if trade_turns[n] == turn:
                        trade.step(n)
                reducer.at(turn, table)

    @pl.when(step == 0)
    def _():
        greet(reducer.partners() + trade.greeted)

    comm(0)

    @pl.when(jnp.logical_and(i == 0, m < M - 1))
    def _():
        later_v[...] = later_ref[0]

    @pl.when(jnp.logical_and(i == 0, m == M - 1))
    def _():
        later_v[...] = r.x_out[...]

    decay, _, hp = head_params(hp_ref)
    matrix = spread_matrix(0, DIN)
    gather = gather_matrix()
    skip = spread(jnp.broadcast_to(hp[2:3], (8, STATE)), matrix)[0:1]

    @pl.when(step == 0)
    def _():
        gcw_ref[...] = jnp.zeros_like(gcw_ref)
        gcb_ref[...] = jnp.zeros_like(gcb_ref)
        gskip_ref[...] = jnp.zeros_like(gskip_ref)
        ghead_ref[...] = jnp.zeros_like(ghead_ref)

    @pl.when(i == 0)
    def _():
        dconv[CHUNK:] = jnp.zeros((8, XBC), F32)

    @pl.when(i > 0)
    def _():
        dconv[CHUNK:] = dconv[0:8]

    tri_up = triangle(True)
    b32 = bc_ref[0, :, 0:STATE]
    c32 = bc_ref[0, :, STATE:2 * STATE]
    keeps_st = iota((CHUNK, CHUNK), 0) <= iota((CHUNK, CHUNK), 1)
    gram_t = jnp.where(keeps_st, fine_nt(c32, b32).T, 0.0)
    b, cc = b32.astype(BF16), c32.astype(BF16)
    lc = info_ref[0, 2]
    lct = lc.T
    dt = info_ref[0, 1]
    dt_x[...] = spread(dt, matrix)
    tail_x[...] = spread(jnp.exp2(lc[CHUNK - 1:CHUNK] - lc), matrix)
    dyl[...] = (dy_ref[0] * spread(jnp.exp2(lc), matrix)).astype(BF16)
    wide8 = lambda v: spread(jnp.exp2(jnp.broadcast_to(v, (8, STATE))), matrix)[0:1]
    gc = gl_ref[0, 0] + wide8(cum_ref[0, 1, pl.ds(c + 1, 1)]) * later_v[...].astype(F32)
    s_in = sl_ref[0, 0] + wide8(cum_ref[0, 0, pl.ds(c, 1)]) * start_ref[0].astype(F32)
    s_out = sl_next_ref[0, 0] + wide8(cum_ref[0, 0, pl.ds(c + 1, 1)]) * start_ref[0].astype(F32)
    gc2 = halves(gc)
    gcb16 = gc2[0:STATE]
    bnd = head_sums(jnp.broadcast_to(jnp.sum(gc * s_out, axis=0, keepdims=True), (8, DIN)), gather)[0:1]
    bg[...] = mm(jnp.concatenate([b, b], axis=1), gc2)
    dgt[...] = jnp.zeros((CHUNK, CHUNK), F32)
    for p in range(HEADS // 2):
        if p == 4:
            comm(1)
        if p == 8:
            comm(2)
        cols = slice(p * STATE, (p + 1) * STATE)
        v = cout_ref[0, :, cols]
        sig = sigmoid(v)
        x = v * sig
        dtx, tlx = dt_x[:, cols], tail_x[:, cols]
        ux = x * dtx
        u16 = ux.astype(BF16)
        ub[:, cols] = (ux * tlx).astype(BF16)
        dyf = dy_ref[0, :, cols]
        dy_high, dy_low = split2(dyf)
        dy2 = doubled(dy_high)
        decays, mixes = [], []
        for h in (2 * p, 2 * p + 1):
            gap = lct[h:h + 1, :] - lc[:, h:h + 1]
            e = jnp.exp2(jnp.minimum(gap, 0.0))
            decays.append(e)
            mixes.append((gram_t * e).astype(BF16))
        mix = jnp.concatenate(mixes, axis=1)
        du = mm(mix, dy2) + mm(mix, doubled(dy_low))
        dmix = mm_nt(u16, dy2)
        dgt[...] = dgt[...] + (dmix[:, :CHUNK] * decays[0] + dmix[:, CHUNK:] * decays[1])
        du_state = tlx * bg[:, cols]
        sk = skip[:, cols]
        dyx = dyf * x
        gskip_ref[:, cols] = gskip_ref[:, cols] + jnp.sum(dyx, axis=0, keepdims=True)
        w[:, cols] = dyx * sk + u16.astype(F32) * du + ux * du_state
        du = du + du_state
        xdu[:, cols] = x * du
        dx = dtx * du + sk * dyf
        dconv[0:CHUNK, cols] = dx * (sig * (1.0 + v * (1.0 - sig)))
    dg16 = jnp.where(keeps_st, dgt[...], 0.0).astype(BF16)
    db = mm(dg16, cc) + mm_nt(ub[...], gcb16)
    dc = mm_tn(dg16, b) + mm_nt(dyl[...], s_in.astype(BF16))
    v = cout_ref[0, :, DIN:XBC]
    sig = sigmoid(v)
    dconv[0:CHUNK, DIN:XBC] = jnp.concatenate([db, dc], axis=1) * (sig * (1.0 + v * (1.0 - sig)))
    dl = r_ref[0] - head_sums(w[...], gather)
    da = bnd + tri_sum(tri_up, dl)
    d_dt = head_sums(xdu[...], gather, 2) + da * decay
    dstep = d_dt * sigmoid(info_ref[0, 0])
    dstep_ref[0] = dstep.astype(BF16)
    ghead_ref[0:1] = ghead_ref[0:1] + decay * jnp.sum(da * dt, axis=0, keepdims=True)
    ghead_ref[1:2] = ghead_ref[1:2] + jnp.sum(dstep, axis=0, keepdims=True)

    @pl.loop(0, XBC // TILE)
    def _(j):
        cols = pl.ds(pl.multiple_of(j * TILE, TILE), TILE)
        gcb_ref[:, cols] = gcb_ref[:, cols] + jnp.sum(dconv[0:CHUNK, cols], axis=0, keepdims=True)
        own = cin_ref[0, :, cols].astype(F32)
        total = None
        for k in range(CONV):
            ahead = dconv[CONV - 1 - k:CONV - 1 - k + CHUNK, cols]
            gcw_ref[k:k + 1, cols] = gcw_ref[k:k + 1, cols] + jnp.sum(own * ahead, axis=0, keepdims=True)
            term = cw_ref[k:k + 1, cols] * ahead
            total = term if total is None else total + term
        dcin_ref[0, :, cols] = total.astype(BF16)

        @pl.when(i == 0)
        def _():
            tail_ref[0, :, cols] = total[CHUNK - HALO:]

    @pl.when(i == NC - 1)
    def _():
        head_ref[0] = dconv[0:8]
        for k in range(CONV - 1):
            for n in range(CONV - 1 - k):
                low = HALO - CONV + 1 + k + n
                gcw_ref[k:k + 1] = gcw_ref[k:k + 1] + chalo_ref[0, low:low + 1] * dconv[n:n + 1]

    comm(TURNS - 1)

    @pl.when(step == steps - 1)
    def _():
        reducer.at(all_turns, table)
        reducer.finish()

        def body(at, c):
            sum1_ref[pl.ds(at, c)] = landing[pl.ds(at, c)]
        strided(landing.shape[0], body)


def k3(ndp, nseq, hp, cw, chalo, cum, cin, cout, bc, info, sl, start, dy, r, gl, later, g1, x_state, x_totals):
    M, T, _ = cout.shape
    NC = T // CHUNK
    at = lambda m, i: NC - 1 - i
    const = lambda a: (pl.BlockSpec(a.shape, lambda m, i: (0,) * a.ndim), a)
    micro = lambda a: (pl.BlockSpec((1,) + a.shape[1:], lambda m, i: (m,) + (0,) * (a.ndim - 1)), a)
    chunk = lambda a: (pl.BlockSpec((1, CHUNK) + a.shape[2:], lambda m, i: (m, at(m, i), 0)), a)
    entry = lambda a, ahead: (pl.BlockSpec((1, 1) + a.shape[2:], lambda m, i: (m, at(m, i) + ahead, 0, 0)), a)
    inner = (pl.BlockSpec((1, 3, CHUNK, STATE), lambda m, i: (m, 0, at(m, i), 0)), info)
    sds = jax.ShapeDtypeStruct
    C = lambda width, dt: (pl.BlockSpec((1, CHUNK, width), lambda m, i: (m, at(m, i), 0)), sds((M, T, width), dt))
    S = lambda rows: (pl.BlockSpec((1, rows, XBC), lambda m, i: (m, 0, 0)), sds((M, rows, XBC), F32))
    W = lambda shape, dt: (pl.BlockSpec(shape, lambda m, i: (0,) * len(shape)), sds(shape, dt))
    V = pltpu.VMEM
    ins = [const(hp), const(cw), micro(chalo), micro(cum), chunk(cin), chunk(cout), chunk(bc), inner, entry(sl, 0), entry(sl, 1), micro(start),
           chunk(dy), chunk(r), entry(gl, 0), micro(later), const(g1), const(x_state), const(x_totals)]
    outs = [C(XBC, BF16), S(HALO), S(8), C(STATE, BF16), W((CONV, XBC), F32), W((1, XBC), F32), W((1, DIN), F32), W((2, STATE), F32),
            W(g1.shape[1:], BF16)]
    return pl.pallas_call(
        functools.partial(k3_body, ndp, nseq, M, NC),
        grid=(M, NC),
        in_specs=[b for b, _ in ins],
        out_specs=[b for b, _ in outs],
        out_shape=[o for _, o in outs],
        scratch_shapes=[V((CHUNK + 8, XBC), F32), V((CHUNK, DIN), F32), V((CHUNK, DIN), F32), V((CHUNK, DIN), BF16), V((CHUNK, DIN), BF16),
                        V((CHUNK, CHUNK), F32), V((CHUNK, DIN), F32), V((CHUNK, DIN), F32), V((CHUNK, DIN), F32), V((STATE, DIN), KIND), V(g1.shape[1:], BF16)] + list(exchange_scratch(nseq).values()) + reducer_scratch(ndp, nseq, g1.shape[1]),
        compiler_params=pltpu.CompilerParams(vmem_limit_bytes=VMEM_LIMIT, dimension_semantics=("arbitrary",) * 2, collective_id=10,
                                             has_side_effects=True),
        name="scan_backward",
    )(*[a for _, a in ins])


def k4_body(ndp, nseq, M, tok_ref, cot_hbm, params_ref, w_hbm, ws_ref, cw_ref, dgate_hbm, dcin_hbm, dstep_hbm, tail_ref, head_ref, sum1_in, *refs):
    norm_hbm, smalls, rest = refs[:M], refs[M:4 + 2 * M], refs[4 + 2 * M:]
    gtok_ref, sum1_ref, sum2_ref, small_out = rest[:4]
    g2, nxt, dc, norm_t, ngr, cot_ref, w_ref, dgate_ref, lsem, esend, erecv, hsem, hrsem = rest[4:17]
    rest = rest[7:]
    count = len(reducer_scratch(ndp, nseq, g2.shape[1]))
    reducer = Reducer(ndp, nseq, g2, sum2_ref, rest[10:10 + count])
    tiny = SmallReducer(ndp, nseq, small_out, rest[10 + count:])
    T = tok_ref.shape[1]
    dp, seq, _, _ = places()
    following, prev = lax.rem(seq + 1, nseq), lax.rem(seq + nseq - 1, nseq)
    loads = Mover(lsem)
    needed = []
    for m in range(M):
        needed += [loads.start(norm_hbm[m], norm_t.at[m], late=False),
                   loads.start(dcin_hbm.at[m, 0:T - HALO], dc.at[m, 0:T - HALO, 0:XBC], late=False),
                   loads.start(dstep_hbm.at[m], dc.at[m, :, XBC:], late=False)]
    greet(reducer.partners() + [(dp, following), (dp, prev)])
    halo = remote(head_ref, nxt, hsem, hrsem, (dp, prev))
    halo.start()
    halves_of_sum1 = reducer_like(reducer, sum1_in).halves(sum1_in, sum1_ref, (esend, erecv))
    for copy in halves_of_sum1:
        copy.start()
    for src, dst in ((w_hbm, w_ref), (dgate_hbm, dgate_ref), (cot_hbm, cot_ref)):
        loads.start(src, dst)
    rows = D // ndp
    gain = param(params_ref, "ng")
    clear_tiles(g2, rows, 15)
    for copy in needed:
        copy.wait()
    halo.wait()
    last = seq == nseq - 1
    row = iota((HALO, XBC), 0)
    for m in range(M):
        tail = tail_ref[m]
        for s in range(CONV - 1):
            extra = jnp.zeros((1, XBC), F32)
            for k in range(s + 1):
                extra = extra + cw_ref[k:k + 1] * nxt[m, s - k:s - k + 1]
            tail = tail + jnp.where(jnp.logical_and(row == HALO - CONV + 1 + s, jnp.logical_not(last)), extra, 0.0)
        dc[m, T - HALO:T, 0:XBC] = tail.astype(BF16)
    ngr[...] = jnp.zeros_like(ngr)
    dn = rest[-1]

    def backward(m, part):
        if part < D // TILE:
            cols = slice(part * TILE, (part + 1) * TILE)
            dn[:, cols] = (mm(dgate_ref[m], w_ref[0:DIN, cols]) + mm(dc[m, :, 0:XBC], w_ref[DIN:DIN + XBC, cols])
                           + mm(dc[m, :, XBC:], ws_ref[:, cols]))
        else:
            src, scale, _ = norm_rows(tok_ref[m], gain)
            unit = src * scale
            d_normed = dn[...]
            ngr[...] += jnp.sum(d_normed * unit, axis=0, keepdims=True)
            f = d_normed * gain
            mean = jnp.mean(f * unit, axis=-1, keepdims=True)
            gtok_ref[m] = (cot_ref[m].astype(F32) + scale * (f - unit * mean)).astype(BF16)

    half = (reducer.size * 2) // (rows // UNIT)
    weight_tiles(g2, rows, norm_t, dc, 0, half)
    for g in (0, 1):
        reducer.stage(0, g)
    weight_tiles(g2, rows, norm_t, dc, half, 15)
    for g in (2, 3):
        reducer.stage(0, g)
    parts = [(m, part) for m in range(M) for part in range(D // TILE + 1)]
    reducer_like(reducer, sum1_in).own_halves(sum1_in, sum1_ref)
    loads.finish()
    for k in range(1, 9):
        for stage, groups in ((k, (0, 1)), (k - 1, (2, 3))):
            if 1 <= stage <= 7:
                for g in groups:
                    reducer.stage(stage, g)
            if parts:
                backward(*parts[0])
                parts = parts[1:]
        if not parts and not tiny.begun:
            tiny.begin([[r[...] for r in group] for group in small_groups(smalls, ngr, M)])
        elif tiny.begun:
            tiny.advance()
    while not tiny.over:
        tiny.advance()
    tiny.finish()
    reducer.finish()
    for copy in halves_of_sum1:
        copy.wait()


def reducer_like(reducer, src):
    other = Refs()
    other.__class__ = Reducer
    other.__dict__.update(reducer.__dict__)
    other.size = src.shape[0] // GROUPS
    other.half = other.size // 2
    return other


def small_groups(smalls, ngr, M):
    gcw, gcb, gskip, ghead = smalls[:4]
    return [[gcw], [gcb], [ngr], list(smalls[4:4 + M]), [gskip], [ghead]]


def k4(ndp, nseq, tok, cot, params, w, ws, cw, dgate, dcin, dstep, tail, head, sum1, norm_ts, gcw, gcb, gskip, ghead, ogrs):
    M, T, _ = tok.shape
    V = pltpu.VMEM
    sds = jax.ShapeDtypeStruct
    vmem = pl.BlockSpec(memory_space=pltpu.VMEM)
    count = units(ndp, nseq, 15)
    args = (tok, cot, params, w, ws, cw, dgate, dcin, dstep, tail, head, sum1, *norm_ts, gcw, gcb, gskip, ghead, *ogrs)
    anywhere = (1, 3, 6, 7, 8) + tuple(range(12, 12 + M))
    return pl.pallas_call(
        functools.partial(k4_body, ndp, nseq, M),
        in_specs=[ANY if i in anywhere else vmem for i in range(len(args))],
        out_specs=[vmem] * 4,
        out_shape=[sds((M, T, D), BF16), sds(sum1.shape, BF16), sds((count, UNIT, STATE), BF16), sds((SMALL_ROWS, STATE), F32)],
        scratch_shapes=[V((ndp, count, UNIT, STATE), BF16), V(head.shape, F32), V((M, T, XBC + STATE), BF16), V((M, D, T), BF16), V((1, D), F32),
                        V(cot.shape, BF16), V(w.shape, BF16), V(dgate.shape, BF16), DMA((3 + 3 * M,)), DMA((GROUPS,)), DMA((GROUPS,)), DMA, DMA] + reducer_scratch(ndp, nseq, count) + small_scratch(ndp, nseq) + [V((T, D), F32)],
        compiler_params=pltpu.CompilerParams(collective_id=11, has_side_effects=True, vmem_limit_bytes=VMEM_LIMIT),
        name="projection_backward",
    )(*args)


def per_device(ndp, nseq, tokens, in_weight, out_weight, conv_weight, conv_bias, norm_gain, out_gain, skip_gain, rate_code, step_code, cotangent):
    micro, groups, T, _ = tokens.shape
    M = micro * groups
    tok = tokens.reshape(M, T, D)
    cot = cotangent.reshape(M, T, D)
    seq = lax.axis_index("seq")
    turned = in_weight.T
    pad = lambda v: jnp.pad(v.astype(F32), (0, STATE - HEADS))
    params = jnp.concatenate([norm_gain, out_gain, conv_bias, pad(rate_code), pad(step_code), pad(skip_gain)]).reshape(-1, STATE)
    if in_weight.shape[0] % STATE == 0:
        w, ws, halo = open_kernel(ndp, nseq, turned, tok)
    else:
        steps = jnp.pad(turned[DIN + XBC:], ((0, STATE - HEADS), (0, 0)))
        w, ws = [lax.all_gather(v, "dp", axis=1, tiled=True) for v in (turned[:DIN + XBC], steps)]
        halo = lax.ppermute(tok[:, T - HALO:], "seq", [(i, i + 1) for i in range(nseq - 1)])
    first, second = [], []
    for m in range(M):
        last = first[-1] if first else {}
        first.append(k1(ndp, nseq, m, last, tok, halo, w, ws, out_weight, conv_weight, params, last.get("sdev"), last.get("totals")))
    shared = {k: first[-1][k] for k in SHARED1}
    starts, wo = first[-1]["starts"], first[1]["wo"]
    for m in range(M):
        one = dict(shared, gate=first[m]["gate"], ypart=first[m]["ypart"], starts=starts)
        traded = (first[-1]["sdev"], first[-1]["totals"]) if m == 0 else (second[-1]["gdev"], first[m - 1]["totals"])
        second.append(k2(ndp, nseq, m, one, second, tok, cot, params, wo, *traded, units(ndp, nseq, 24)))
        starts = second[0]["starts"]
    s = dict(shared, starts=starts, laters=second[-1]["laters"], g1=second[-1]["g1"], **{k: second[-1][k] for k in SHARED2})
    dcin, tail, head, dstep, gcw, gcb, gskip, ghead, sum1 = k3(
        ndp, nseq, params, conv_weight, s["chalo"], s["cum"], s["cin"], s["cout"], s["bc"], s["info"], s["sl"], s["starts"], s["dy"],
        s["rows_dot"], s["gl"], s["laters"], s["g1"], second[-1]["gdev"], first[-1]["totals"])
    mixed = s["mixed"]
    gtok, sum1, sum2, sm = k4(ndp, nseq, tok, cot, params, w, ws, conv_weight, s["dgate"], dcin, dstep, tail, head, sum1, [b["norm_t"] for b in second], gcw, gcb, gskip, ghead,
                        [b["ogr"] for b in second])
    g_in, g_out, *rest = unpack(sum1, sum2, sm, D // ndp)
    return (mixed.reshape(tokens.shape), gtok.reshape(tokens.shape), g_in.T, g_out, *rest)


def solution(mesh):
    rows, split = P("dp", None), P(None, "dp", "seq", None)
    return jax.shard_map(
        functools.partial(per_device, mesh.shape["dp"], mesh.shape["seq"]),
        mesh=mesh,
        in_specs=(split, rows, rows) + (P(),) * 7 + (split,),
        out_specs=(split, split, rows, rows) + (P(),) * 7,
        check_vma=False,
    )
```
